32 devices in a mesh: dp: 4 (over z), heads: 2 (over y), rows: 4 (over x, core).
Axes of the slice: x: 2, y: 2, z: 4, core: 2. Of those that a mesh axis runs over, the one named last changes fastest.
Arguments:
- tokens: bfloat16 [16384, 2048], P(('dp', 'rows')), may hold values from -6 to 6
- segment_lengths: int32 [4, 8], P('dp'), may hold values from 1 to 3072, as said below
- pre_norm_gain: float32 [2048], replicated, may hold values from 0.5 to 1.5
- pre_norm_bias: float32 [2048], replicated, may hold values from -1 to 1
- query_weight: bfloat16 [2048, 2048], P(None, 'heads'), may hold values from -0.1875 to 0.1875
- query_bias: float32 [2048], P('heads'), may hold values from -3 to 3
- key_value_weight: bfloat16 [2048, 256], replicated, may hold values from -0.1875 to 0.1875
- value_bias: float32 [128], replicated, may hold values from -0.3 to 0.3
- output_weight: bfloat16 [2048, 2048], P('heads'), may hold values from -1 to 1
- output_bias: float32 [2048], replicated, may hold values from -2 to 2
- mlp_norm_gain: float32 [2048], replicated, may hold values from 0.5 to 1.5
- mlp_norm_bias: float32 [2048], replicated, may hold values from -1 to 1
- expand_weight: bfloat16 [2048, 8192], P(None, ('heads', 'rows')), may hold values from -0.125 to 0.125
- expand_bias: float32 [8192], P(('heads', 'rows')), may hold values from -3 to 3
- contract_weight: bfloat16 [8192, 2048], P(('heads', 'rows')), may hold values from -0.25 to 0.25
- contract_bias: float32 [2048], replicated, may hold values from -2 to 2
- cotangent: bfloat16 [16384, 2048], P(('dp', 'rows')), may hold values from -6 to 6
Outputs:
- layer_output: bfloat16 [16384, 2048], P(('dp', 'rows'))
- input_grad: bfloat16 [16384, 2048], P(('dp', 'rows'))
- pre_norm_gain_grad: float32 [2048], replicated
- pre_norm_bias_grad: float32 [2048], replicated
- query_weight_grad: float32 [2048, 2048], P(None, 'heads')
- query_bias_grad: float32 [2048], P('heads')
- key_value_weight_grad: float32 [2048, 256], replicated
- value_bias_grad: float32 [128], replicated
- output_weight_grad: float32 [2048, 2048], P('heads')
- output_bias_grad: float32 [2048], replicated
- mlp_norm_gain_grad: float32 [2048], replicated
- mlp_norm_bias_grad: float32 [2048], replicated
- expand_weight_grad: float32 [2048, 8192], P(None, ('heads', 'rows'))
- expand_bias_grad: float32 [8192], P(('heads', 'rows'))
- contract_weight_grad: float32 [8192, 2048], P(('heads', 'rows'))
- contract_bias_grad: float32 [2048], replicated
The draws below stay inside these ranges and needn't reach their ends.
Inputs may be any that keep to these rules, and one draw needn't show every extreme that they name: `segment_lengths`: each window's 8 segment lengths sum to at most 4096; the rest of the window is padding. Every window has a segment of exactly 3072 positions.
All inputs are finite; a program needn't handle non-finite values.
Results may differ from the reference program's by a relative error of at most 0.015.
Values may be sent and summed in bfloat16 or wider, within the bound.
No kernel may reach another device: no remote copies, remote signals or barrier semaphores. Data moves between devices by JAX's collectives and lax.ppermute only.
A program may use at most 448 MiB of HBM per device.

```python
import math
import jax
import jax.numpy as jnp
from jax import lax

D = 2048
HEADS = 16
HEAD_DIM = 128
FF = 8192
WINDOW = 4096
SEGS = 8
WINDOWS = 4
TOKENS = 16384


def draw_segment_lengths(key, part):
    key_big, key_small = jax.random.split(key, 2)
    small_most = WINDOW // 64
    small_lengths = jax.random.randint(key_small, (WINDOWS, SEGS), 1, small_most + 1)
    big_place = jax.random.randint(key_big, (WINDOWS, 1), 0, SEGS)
    slots = jnp.arange(SEGS)[None, :]
    chosen = slots == big_place
    single = slots == (big_place + 1) % SEGS
    small_lengths = jnp.where(single, 1, small_lengths)
    return jnp.where(chosen, 3 * WINDOW // 4, small_lengths).astype(jnp.int32)


def levels(stream_key, extent, cuts, least, largest):
    level = 1.0
    for position, blocks in cuts:
        draws = jax.random.uniform(jax.random.fold_in(jax.random.fold_in(stream_key, 6), position), (blocks,), jnp.float32, least / len(cuts), largest / len(cuts))
        level = level * jnp.repeat(jnp.exp(draws), extent[position] // blocks).reshape((-1,) + (1,) * (len(extent) - 1 - position))
    return level


def gaussian(key, extent, spread, bound, shards=(), held_as=jnp.bfloat16):
    values = jax.random.normal(key, extent, jnp.float32) * spread
    if len(shards) > 0:
        values = levels(key, extent, shards, -0.22, 0.18) * values
    return jnp.clip(values, min=-bound, max=bound).astype(held_as)


def setup_inputs(seed: int = 0) -> dict:
    streams_of = jax.random.split(jax.random.key(seed), 18)
    return {
        "tokens": gaussian(streams_of[0], (TOKENS, D), 1.0, 6.0, ((0, 16),)),
        "segment_lengths": draw_segment_lengths(jax.random.fold_in(streams_of[17], 71), 0),
        "pre_norm_gain": jnp.clip(1.0 + 0.1 * jax.random.normal(streams_of[2], (D,), jnp.float32), 0.5, 1.5),
        "pre_norm_bias": gaussian(streams_of[3], (D,), 0.2, 1.0, (), jnp.float32),
        "query_weight": gaussian(streams_of[4], (D, HEADS * HEAD_DIM), (D // 2) ** -0.5, 0.1875, ((1, 2),)),
        "query_bias": gaussian(streams_of[5], (HEADS * HEAD_DIM,), 0.5, 3.0, ((0, 2),), jnp.float32),
        "key_value_weight": gaussian(streams_of[6], (D, 2 * HEAD_DIM), (D // 2) ** -0.5, 0.1875),
        "value_bias": gaussian(streams_of[7], (HEAD_DIM,), 0.05, 0.3, (), jnp.float32),
        "output_weight": gaussian(streams_of[8], (HEADS * HEAD_DIM, D), (HEADS * HEAD_DIM // 64) ** -0.5, 1.0, ((0, 2),)),
        "output_bias": gaussian(streams_of[9], (D,), 0.3, 2.0, (), jnp.float32),
        "mlp_norm_gain": jnp.clip(1.0 + 0.1 * jax.random.normal(streams_of[10], (D,), jnp.float32), 0.5, 1.5),
        "mlp_norm_bias": gaussian(streams_of[11], (D,), 0.2, 1.0, (), jnp.float32),
        "expand_weight": gaussian(streams_of[12], (D, FF), D ** -0.5, 0.125, ((1, 8),)),
        "expand_bias": gaussian(streams_of[13], (FF,), 0.5, 3.0, ((0, 8),), jnp.float32),
        "contract_weight": gaussian(streams_of[14], (FF, D), (FF // 16) ** -0.5, 0.25, ((0, 8),)),
        "contract_bias": gaussian(streams_of[15], (D,), 0.3, 2.0, (), jnp.float32),
        "cotangent": gaussian(streams_of[16], (TOKENS, D), 1.0, 6.0, ((0, 16),)),
    }


NORM_EPSILON = 1e-05
MASKED_SCORE = -1000000000.0
HIGHEST = lax.Precision.HIGHEST

@jax.custom_vjp
def low(v):
    return lax.optimization_barrier(v.astype(jnp.bfloat16)).astype(jnp.float32)

@jax.custom_vjp
def low_back(v):
    return v

def low_keep(v):
    return (low(v), None)

def low_pass(kept, grad):
    return (grad,)

def back_keep(v):
    return (v, None)

def back_low(kept, grad):
    return (low(grad),)
low.defvjp(low_keep, low_pass)
low_back.defvjp(back_keep, back_low)

def layer_norm(values, gain_vector, bias_vector):
    row_mean = lax.optimization_barrier(jnp.mean(values, -1, keepdims=True))
    centred = values - row_mean
    row_var = lax.optimization_barrier(jnp.mean(centred * centred, -1, keepdims=True))
    return centred * lax.rsqrt(row_var + NORM_EPSILON) * gain_vector + bias_vector

def segment_ids(lengths, positions):
    segment_ends = jnp.cumsum(lengths.astype(jnp.int32)).astype(jnp.int32)
    places = jnp.arange(positions, dtype=jnp.int32)
    return lax.optimization_barrier(jnp.sum((places[:, None] >= segment_ends[None, :]).astype(jnp.int32), 1)).astype(jnp.int32)

def product(left, right):
    return jnp.dot(left, right, precision=HIGHEST)

def window_forward(weights, inputs):
    window_x, lengths = inputs
    norm_one_gain, norm_one_bias, query_weight, query_bias, key_value_weight, value_bias, output_weight, output_bias, norm_two_gain, norm_two_bias, expand_weight, expand_bias, contract_weight, contract_bias = weights
    normed_first = low(layer_norm(window_x, norm_one_gain, norm_one_bias))
    query = low_back(low(product(normed_first, query_weight) + query_bias))
    kv_bias = jnp.concatenate([jnp.zeros((HEAD_DIM,), jnp.float32), value_bias])
    key_value = low_back(low(product(normed_first, key_value_weight) + kv_bias))
    key_rows = key_value[:, :HEAD_DIM]
    value_rows = key_value[:, HEAD_DIM:]
    segment = segment_ids(lengths, WINDOW)
    places = jnp.arange(WINDOW, dtype=jnp.int32)
    block_rows = min(512, WINDOW)
    block_count = WINDOW // block_rows
    score_scale = 1.0 / math.sqrt(HEAD_DIM)

    def attend(args):
        query_block, query_pos, query_seg = args
        raw_scores = low_back(jnp.einsum('qhd,kd->hqk', query_block, key_rows, precision=HIGHEST))
        allowed = (query_seg[:, None] == segment[None, :]) & (places[None, :] <= query_pos[:, None])
        scores = jnp.where(allowed[None], raw_scores * score_scale, MASKED_SCORE)
        attn_weights = low(jax.nn.softmax(scores, axis=-1))
        attn_out = jnp.einsum('hqk,kd->qhd', attn_weights, value_rows, precision=HIGHEST)
        return low_back(low(attn_out)).reshape(block_rows, HEADS * HEAD_DIM)
    blocks = lax.map(jax.checkpoint(attend), (query.reshape(block_count, block_rows, HEADS, HEAD_DIM), places.reshape(block_count, block_rows), segment.reshape(block_count, block_rows)))
    attended = blocks.reshape(WINDOW, HEADS * HEAD_DIM)
    middle = window_x + low_back(product(attended, output_weight)) + output_bias
    normed_second = low(layer_norm(middle, norm_two_gain, norm_two_bias))
    before_act = low_back(product(normed_second, expand_weight)) + expand_bias
    hidden = low(jax.nn.gelu(before_act, approximate=True))
    return middle + product(hidden, contract_weight) + contract_bias

def reference(tokens, segment_lengths, pre_norm_gain, pre_norm_bias, query_weight, query_bias, key_value_weight, value_bias, output_weight, output_bias, mlp_norm_gain, mlp_norm_bias, expand_weight, expand_bias, contract_weight, contract_bias, cotangent):
    weights = tuple((w.astype(jnp.float32) for w in (pre_norm_gain, pre_norm_bias, query_weight, query_bias, key_value_weight, value_bias, output_weight, output_bias, mlp_norm_gain, mlp_norm_bias, expand_weight, expand_bias, contract_weight, contract_bias)))
    window_step = jax.checkpoint(window_forward)

    def whole(inputs_x, *params):
        return lax.map(lambda pair: window_step(params, pair), (inputs_x, segment_lengths))
    inputs_x = tokens.astype(jnp.float32).reshape(WINDOWS, WINDOW, D)
    result, back_fn = jax.vjp(whole, inputs_x, *weights)
    grads = back_fn(cotangent.astype(jnp.float32).reshape(WINDOWS, WINDOW, D))
    layer_output = result.reshape(TOKENS, D).astype(jnp.bfloat16)
    input_grad = grads[0].reshape(TOKENS, D).astype(jnp.bfloat16)
    return (layer_output, input_grad, grads[1], grads[2], grads[3], grads[4], grads[5], grads[6], grads[7], grads[8], grads[9], grads[10], grads[11], grads[12], grads[13], grads[14])
```

```python
import functools
import math

import jax
import jax.numpy as jnp
from jax import lax
from jax.experimental import pallas as pl
from jax.experimental.pallas import tpu as pltpu
from jax.sharding import PartitionSpec as P

NORM_EPSILON = 1e-05
FAR = -1e30
LOG2E = 1.4426950408889634
GELU_A = math.sqrt(2.0 / math.pi)
GELU_B = 0.044715
F32 = jnp.float32
BF16 = jnp.bfloat16
MIB = 1024 * 1024
FORWARD_BLOCK = (512, 1024)
BACKWARD_BLOCK = (256, 1024)


def dot(left, right):
    return jnp.dot(left, right, preferred_element_type=F32)


def dot_tn(left, right):
    return lax.dot_general(left, right, (((0,), (0,)), ((), ())), preferred_element_type=F32)


def dot_nt(left, right):
    return lax.dot_general(left, right, (((1,), (1,)), ((), ())), preferred_element_type=F32)


def call(kernel, grid, ins, outs, scratch=(), prefetch=0, vmem=48, flops=0, moved=0, alias=None):
    arrays = [a for a, _, _ in ins[prefetch:]]
    specs = [
        pl.BlockSpec(b, m, pipeline_mode=pl.Buffered(1)) if b == a.shape else pl.BlockSpec(b, m) for a, b, m in ins[prefetch:]
    ]
    scalars = [a for a, _, _ in ins[:prefetch]]
    return pl.pallas_call(
        kernel,
        grid_spec=pltpu.PrefetchScalarGridSpec(
            num_scalar_prefetch=prefetch,
            grid=grid,
            in_specs=specs,
            out_specs=[pl.BlockSpec(b, m) for _, _, b, m in outs],
            scratch_shapes=list(scratch),
        ),
        out_shape=[jax.ShapeDtypeStruct(s, d) for s, d, _, _ in outs],
        compiler_params=pltpu.CompilerParams(vmem_limit_bytes=vmem * MIB),
        cost_estimate=pl.CostEstimate(flops=int(flops), bytes_accessed=int(moved), transcendentals=0),
        input_output_aliases=alias or {},
    )(*scalars, *arrays)


def whole(array):
    zeros = (0,) * array.ndim
    return (array, array.shape, lambda *_: zeros)


def rows_of(array, block):
    return (array, (block, array.shape[1]), lambda i, *_: (i, 0))


def normed(values, gain, bias):
    mean = jnp.mean(values, -1, keepdims=True)
    centred = values - mean
    var = jnp.mean(centred * centred, -1, keepdims=True)
    return centred * lax.rsqrt(var + NORM_EPSILON) * gain + bias


def norm_back(values, grad, gain):
    mean = jnp.mean(values, -1, keepdims=True)
    centred = values - mean
    var = jnp.mean(centred * centred, -1, keepdims=True)
    inverse = lax.rsqrt(var + NORM_EPSILON)
    xhat = centred * inverse
    g = grad * gain
    g_mean = jnp.mean(g, -1, keepdims=True)
    gx_mean = jnp.mean(g * xhat, -1, keepdims=True)
    return xhat, (g - g_mean - xhat * gx_mean) * inverse


def norm_kv_kernel(t_ref, g_ref, b_ref, w_ref, wb_ref, n_ref, kv_ref):
    low = normed(t_ref[...].astype(F32), g_ref[...], b_ref[...]).astype(BF16)
    n_ref[...] = low
    kv_ref[...] = (dot(low, w_ref[...]) + wb_ref[...]).astype(BF16)


def project_kernel(core, n_ref, wa_ref, ba_ref, wb_ref, bb_ref, a_ref, b_ref):
    low = n_ref[...]
    b_ref[...] = (dot(low, wb_ref[...]) + bb_ref[...]).astype(BF16)
    a_ref[...] = (dot(low, wa_ref[...]) + ba_ref[...]).astype(BF16)


def attn_forward_kernel(heads, half, bk, scale2, info, qa_ref, qb_ref, kv_ref, vt_ref, st_ref, oa_ref, ob_ref, lse_ref, m_ref, l_ref, acc_ref):
    i = pl.program_id(0)
    first, low, high, clear_from, clear_to = (info[n, i] for n in range(5))
    bq, dim = qa_ref.shape[0], kv_ref.shape[1] // 2
    in_a = i < half
    start = st_ref[...]
    place = first + lax.broadcasted_iota(jnp.int32, (1, bq), 1)
    queries = jnp.where(in_a, qa_ref[...], qb_ref[...])
    m_ref[...] = jnp.full_like(m_ref, FAR)
    l_ref[...] = jnp.zeros_like(l_ref)
    acc_ref[...] = jnp.zeros_like(acc_ref)

    def step(block, masked):
        begin = pl.multiple_of(block * bk, bk)
        keys = kv_ref[pl.ds(begin, bk), :dim]
        values = vt_ref[:, pl.ds(begin, bk)]
        if masked:
            key_place = begin + lax.broadcasted_iota(jnp.int32, (bk, 1), 0)
            allowed = (key_place >= start) & (key_place <= place)
        for h in range(heads):
            s = dot_nt(keys, queries[:, h * dim : (h + 1) * dim])
            if masked:
                s = jnp.where(allowed, s, FAR)
            old = m_ref[h : h + 1, :]
            new = jnp.maximum(old, jnp.max(s, 0, keepdims=True) * scale2)
            p = jnp.exp2(s * scale2 - new)
            fix = jnp.exp2(old - new)
            l_ref[h : h + 1, :] = l_ref[h : h + 1, :] * fix + jnp.sum(p, 0, keepdims=True)
            m_ref[h : h + 1, :] = new
            acc_ref[h] = acc_ref[h] * fix + dot(values, p.astype(BF16))

    def body(block, carry):
        clear = (block >= clear_from) & (block < clear_to)

        @pl.when(clear)
        def _():
            step(block, False)

        @pl.when(jnp.logical_not(clear))
        def _():
            step(block, True)

        return carry

    lax.fori_loop(low, high, body, 0)
    outs = []
    for h in range(heads):
        total = l_ref[h : h + 1, :]
        outs.append((acc_ref[h] / total).T.astype(BF16))
    lse_ref[...] = m_ref[...] + jnp.log2(l_ref[...])

    @pl.when(in_a)
    def _():
        for h in range(heads):
            oa_ref[:, h * dim : (h + 1) * dim] = outs[h]

    @pl.when(jnp.logical_not(in_a))
    def _():
        for h in range(heads):
            ob_ref[:, h * dim : (h + 1) * dim] = outs[h]


def attn_backward_kernel(
    heads, half, bk, scale, scale2, info, qa_ref, qb_ref, ga_ref, gb_ref, oa_ref, ob_ref, kv_ref, kt_ref, st_ref, lse_ref, dqa_ref, dqb_ref, dkv_ref, dq_ref
):
    i = pl.program_id(0)
    first, low, high, clear_from, clear_to = (info[n, i] for n in range(5))
    bq, dim = qa_ref.shape[0], kv_ref.shape[1] // 2
    in_a = i < half

    @pl.when(i == 0)
    def _():
        dkv_ref[...] = jnp.zeros_like(dkv_ref)

    start = st_ref[...]
    place = first + lax.broadcasted_iota(jnp.int32, (1, bq), 1)
    queries = jnp.where(in_a, qa_ref[...], qb_ref[...])
    grads = jnp.where(in_a, ga_ref[...], gb_ref[...])
    outs = jnp.where(in_a, oa_ref[...], ob_ref[...])
    inner, lse = [], []
    for h in range(heads):
        cut = slice(h * dim, (h + 1) * dim)
        product = grads[:, cut].astype(F32) * outs[:, cut].astype(F32)
        inner.append(jnp.sum(product.T, 0, keepdims=True))
        lse.append(lse_ref[h : h + 1, :])
    dq_ref[...] = jnp.zeros_like(dq_ref)

    def step(block, masked):
        begin = pl.multiple_of(block * bk, bk)
        keys = kv_ref[pl.ds(begin, bk), :dim]
        values = kv_ref[pl.ds(begin, bk), dim:]
        keys_t = kt_ref[:, pl.ds(begin, bk)]
        if masked:
            key_place = begin + lax.broadcasted_iota(jnp.int32, (bk, 1), 0)
            allowed = (key_place >= start) & (key_place <= place)
        dk = None
        for h in range(heads):
            cut = slice(h * dim, (h + 1) * dim)
            s = dot_nt(keys, queries[:, cut])
            dp = dot_nt(values, grads[:, cut])
            p = jnp.exp2(s * scale2 - lse[h])
            if masked:
                p = jnp.where(allowed, p, 0.0)
            ds = (p * (dp - inner[h])).astype(BF16)
            dv_part = dot(p.astype(BF16), grads[:, cut])
            dk_part = dot(ds, queries[:, cut])
            dk, dv = (dk_part, dv_part) if dk is None else (dk + dk_part, dv + dv_part)
            dq_ref[h] += dot(keys_t, ds)
        dkv_ref[pl.ds(begin, bk), :dim] += dk * scale
        dkv_ref[pl.ds(begin, bk), dim:] += dv

    def body(block, carry):
        clear = (block >= clear_from) & (block < clear_to)

        @pl.when(clear)
        def _():
            step(block, False)

        @pl.when(jnp.logical_not(clear))
        def _():
            step(block, True)

        return carry

    lax.fori_loop(low, high, body, 0)

    def leave(ref):
        for h in range(heads):
            ref[:, h * dim : (h + 1) * dim] = (dq_ref[h] * scale).T.astype(BF16)

    @pl.when(in_a)
    def _():
        leave(dqa_ref)

    @pl.when(jnp.logical_not(in_a))
    def _():
        leave(dqb_ref)


def balanced(acts, weights, product, by_rows, scratch):
    act_ref, weight_ref, sums = scratch[0], scratch[1], scratch[2:]
    sides = len(sums)
    calls = len(acts) // sides
    cols = acts[0].shape[1] // 2
    for n in range(sides):

        @pl.when(pl.program_id(0) == 0)
        def _():
            keep, send = weights[2 * n], weights[2 * n + 1]
            if by_rows:
                size = keep.shape[0]
                weight_ref[n, :size, :] = keep[...]
                weight_ref[n, size:, :] = send[...]
            else:
                size = keep.shape[1]
                weight_ref[n, :, :size] = keep[...]
                weight_ref[n, :, size:] = send[...]

        for k in range(calls):
            act = acts[k * sides + n]
            act_ref[n, :, k * cols : (k + 1) * cols] = act[:, :cols]
            act_ref[n, :, (calls + k) * cols : (calls + k + 1) * cols] = act[:, cols:]
        sums[n][...] = product(act_ref[n], weight_ref[n])
    return functools.reduce(lambda u, v: u + v, [r[...] for r in sums])


def output_kernel(count, sides, *refs):
    acts, weights = refs[:count], refs[count : count + 2 * sides]
    t_ref, ob_ref, g_ref, b_ref, mid_ref, n_ref, *scratch = refs[count + 2 * sides :]
    near = balanced(acts, weights, dot, True, scratch)
    middle = t_ref[...].astype(F32) + near + ob_ref[...]
    mid_ref[...] = middle
    n_ref[...] = normed(middle, g_ref[...], b_ref[...]).astype(BF16)


def feed_tile(x, c, w, v, bias):
    before = dot(x, w) + bias
    grad = dot_nt(c, v)
    square = before * before
    t = jnp.tanh(before * (GELU_A + (GELU_A * GELU_B) * square))
    half = 0.5 + 0.5 * t
    slope = half + before * (half * (1.0 - t)) * (GELU_A + (3.0 * GELU_A * GELU_B) * square)
    return (before * half).astype(BF16), grad * slope


def stack(scratch, first, second):
    rows = first.shape[0]
    scratch[:rows, :] = first[...]
    scratch[rows:, :] = second[...]


def add_to(ref, value, fresh):
    @pl.when(fresh)
    def _():
        ref[...] = jnp.zeros_like(ref)

    ref[...] += jnp.broadcast_to(value, ref.shape)


def feed_near_kernel(blk, xa_ref, xb_ref, ca_ref, cb_ref, w_ref, v_ref, b_ref, ha_ref, hb_ref, da_ref, db_ref, sum_ref, x_ref, c_ref):
    rows = xa_ref.shape[0]
    stack(x_ref, xa_ref, xb_ref)
    stack(c_ref, ca_ref, cb_ref)
    sums = []
    for at in range(0, w_ref.shape[1], blk):
        cut = slice(at, at + blk)
        hidden, grad = feed_tile(x_ref[...], c_ref[...], w_ref[:, cut], v_ref[cut, :], b_ref[:, cut])
        low = grad.astype(BF16)
        ha_ref[:, cut] = hidden[:rows]
        hb_ref[:, cut] = hidden[rows:]
        da_ref[:, cut] = low[:rows]
        db_ref[:, cut] = low[rows:]
        sums.append(jnp.sum(grad, 0, keepdims=True))
    add_to(sum_ref, jnp.concatenate(sums, 1), pl.program_id(0) == 0)


def feed_far_kernel(steps, xa_ref, xb_ref, ca_ref, cb_ref, b_ref, ea_ref, eb_ref, u_ref, *rest):
    w_refs, z_refs, v_ref = rest[:steps], rest[steps : 2 * steps], rest[2 * steps]
    ga_ref, gb_ref, ha_ref, hb_ref, da_ref, db_ref, sum_ref, x_ref, c_ref, e_ref, low_ref = rest[-11:]
    i = pl.program_id(0)
    rows = xa_ref.shape[0]

    @pl.when(i == 0)
    def _():
        stack(x_ref, xa_ref, xb_ref)
        stack(c_ref, ca_ref, cb_ref)
        stack(e_ref, ea_ref, eb_ref)

    for k in range(steps):

        @pl.when(i == k)
        def _():
            hidden, grad = feed_tile(x_ref[...], c_ref[...], w_refs[k][...], v_ref[...], b_ref[...])
            low = grad.astype(BF16)
            ha_ref[...] = hidden[:rows]
            hb_ref[...] = hidden[rows:]
            da_ref[...] = low[:rows]
            db_ref[...] = low[rows:]
            low_ref[k] = low
            sum_ref[...] = jnp.broadcast_to(jnp.sum(grad, 0, keepdims=True), sum_ref.shape)

    @pl.when(i >= steps)
    def _():
        total = dot_nt(e_ref[...], u_ref[...])
        for k in range(steps):
            total = total + dot_nt(low_ref[k], z_refs[k][...])
        ga_ref[...] = total[:rows].astype(BF16)
        gb_ref[...] = total[rows:].astype(BF16)


def feed_near(chunk, first_row, x_own, x_other, c_own, c_other, w, v, bias):
    rows, width = x_own.shape
    hid = w.shape[1]
    base = first_row // chunk
    at = lambda i: (i, 0)
    at_all = lambda i: (base + i, 0)
    return call(
        functools.partial(feed_near_kernel, min(512, hid)),
        (rows // chunk,),
        [
            (x_own, (chunk, width), at),
            (x_other, (chunk, width), at),
            (c_own, (chunk, width), at_all),
            (c_other, (chunk, width), at_all),
            whole(w),
            whole(v),
            whole(bias),
        ],
        [((rows, hid), BF16, (chunk, hid), at)] * 4 + [((8, hid), F32, (8, hid), lambda i: (0, 0))],
        scratch=[pltpu.VMEM((2 * chunk, width), BF16)] * 2,
        vmem=56,
        flops=8 * rows * width * hid,
        moved=8 * width * hid + 8 * rows * width,
    )


def feed_far(chunk, index, first_row, x_own, x_other, c_own, c_other, w, v, bias, near_own, near_other, w_near, kept):
    rows, width = x_own.shape
    hid = w_near.shape[1]
    steps = len(w)
    blk = hid // steps
    out_blk = min(512, width)
    back = width // out_blk
    base = first_row // chunk
    at = lambda i: (index, 0)
    at_all = lambda i: (base + index, 0)
    tile = lambda i: jnp.minimum(i, steps - 1)
    after = lambda i: jnp.maximum(i - steps, 0)
    ins = [
        (x_own, (chunk, width), at),
        (x_other, (chunk, width), at),
        (c_own, (chunk, width), at_all),
        (c_other, (chunk, width), at_all),
        (bias, (1, blk), lambda i: (0, tile(i))),
        (near_own, (chunk, hid), at),
        (near_other, (chunk, hid), at),
        (w_near, (out_blk, hid), lambda i: (after(i), 0)),
    ]
    ins += [whole(p) for p in w]
    ins += [(p, (out_blk, blk), lambda i: (after(i), 0)) for p in w]
    ins += [(v, (blk, width), lambda i: (tile(i), 0))]
    outs = [((chunk, width), BF16, (chunk, out_blk), lambda i: (0, after(i)))] * 2
    outs += [((rows, hid), BF16, (chunk, blk), lambda i: (index, tile(i)))] * 4
    outs += [((8, hid), F32, (8, blk), lambda i: (0, tile(i)))]
    alias = {}
    arrays = [a for a, _, _ in ins]
    specs = [
        pl.BlockSpec(b, m, pipeline_mode=pl.Buffered(1)) if b == a.shape else pl.BlockSpec(b, m) for a, b, m in ins
    ]
    if kept is not None:
        for place, array in enumerate(kept):
            alias[len(arrays)] = 2 + place
            arrays.append(array)
            specs.append(pl.BlockSpec(memory_space=pl.ANY))
    result = pl.pallas_call(
        functools.partial(feed_far_kernel, steps),
        grid=(steps + back,),
        in_specs=specs,
        out_specs=[pl.BlockSpec(b, m) for _, _, b, m in outs],
        out_shape=[jax.ShapeDtypeStruct(s, d) for s, d, _, _ in outs],
        scratch_shapes=[
            pltpu.VMEM((2 * chunk, width), BF16),
            pltpu.VMEM((2 * chunk, width), BF16),
            pltpu.VMEM((2 * chunk, hid), BF16),
            pltpu.VMEM((steps, 2 * chunk, blk), BF16),
        ],
        input_output_aliases=alias,
        compiler_params=pltpu.CompilerParams(vmem_limit_bytes=56 * MIB),
        cost_estimate=pl.CostEstimate(
            flops=8 * 2 * chunk * width * hid, bytes_accessed=8 * width * hid + 24 * chunk * width, transcendentals=0
        ),
    )(*arrays)
    return result[:2], result[2:6], result[6]


def contract_kernel(count, *refs):
    near, far = refs[:count], refs[count : 2 * count]
    va_ref, vb_ref, own_ref, other_ref = refs[2 * count :]
    size = near[0].shape[0]
    for k in range(count):
        y_ref = own_ref if k < count // 2 else other_ref
        at = k % (count // 2) * size
        y_ref[at : at + size, :] = (dot(near[k][...], va_ref[...]) + dot(far[k][...], vb_ref[...])).astype(BF16)


def pair_grad_kernel(*refs):
    out_ref = refs[-1]
    count = (len(refs) - 1) // 2
    total = None
    for left, right in zip(refs[:count], refs[count:-1]):
        piece = dot_tn(left[...], right[...])
        total = piece if total is None else total + piece
    out_ref[...] = total.astype(BF16)


def second_back_kernel(count, *refs):
    firsts, seconds = refs[:count], refs[count : 2 * count]
    mid_ref, cot_ref, gain_ref, wk_ref, ws_ref, gm_ref, low_ref, keep_ref, send_ref, sums_ref = refs[2 * count :]
    size = firsts[0].shape[0]
    totals = [0.0, 0.0, 0.0, 0.0]
    for k in range(count):
        at = slice(k * size, (k + 1) * size)
        grad = firsts[k][...].astype(F32) + seconds[k][...].astype(F32)
        xhat, back = norm_back(mid_ref[at, :], grad, gain_ref[...])
        cot = cot_ref[at, :].astype(F32)
        total = cot + back
        gm_ref[at, :] = total
        low_ref[at, :] = total.astype(BF16)
        for n, value in enumerate((grad * xhat, grad, total, cot)):
            totals[n] = totals[n] + jnp.sum(value, 0, keepdims=True)
    send_ref[...] = dot_nt(low_ref[...], ws_ref[...]).astype(BF16)
    keep_ref[...] = dot_nt(low_ref[...], wk_ref[...]).astype(BF16)
    for n in range(4):
        sums_ref[n : n + 1, :] = totals[n]


def first_back_kernel(count, sides, *refs):
    acts, weights = refs[:count], refs[count : count + 2 * sides]
    kv_ref, kvw_ref, t_ref, gm_ref, gain_ref, out_ref, sums_ref, *scratch = refs[count + 2 * sides :]
    grad = balanced(acts, weights, dot_nt, False, scratch) + dot_nt(kv_ref[...], kvw_ref[...])
    xhat, back = norm_back(t_ref[...].astype(F32), grad, gain_ref[...])
    out_ref[...] = (gm_ref[...] + back).astype(BF16)

    @pl.when(pl.program_id(0) == 0)
    def _():
        sums_ref[...] = jnp.zeros_like(sums_ref)

    sums_ref[0:1, :] += jnp.sum(grad * xhat, 0, keepdims=True)
    sums_ref[1:2, :] += jnp.sum(grad, 0, keepdims=True)


def body(
    tokens,
    segment_lengths,
    pre_norm_gain,
    pre_norm_bias,
    query_weight,
    query_bias,
    key_value_weight,
    value_bias,
    output_weight,
    output_bias,
    mlp_norm_gain,
    mlp_norm_bias,
    expand_weight,
    expand_bias,
    contract_weight,
    contract_bias,
    cotangent,
):
    rows, width = tokens.shape
    n_heads, n_rows, n_dp = (lax.axis_size(a) for a in ("heads", "rows", "dp"))
    row_index = lax.axis_index("rows")
    core = lax.rem(row_index, 2)
    dim = key_value_weight.shape[1] // 2
    local_heads = query_weight.shape[1] // dim
    group = local_heads // 2
    cols = group * dim
    window = rows * n_rows
    scale = 1.0 / math.sqrt(dim)
    hid = expand_weight.shape[1]

    chips = n_rows // 2
    chip = row_index // 2
    dp_index = lax.axis_index("dp")

    def near(value):
        return lax.ppermute(value, "rows", [(i, i ^ 1) for i in range(n_rows)])

    def far(value):
        return lax.ppermute(value, "rows", [(i, i ^ 2) for i in range(n_rows)])

    def across(value):
        return lax.ppermute(value, "heads", [(0, 1), (1, 0)])

    def beside(value):
        return lax.ppermute(value, "dp", [(i, i ^ 1) for i in range(n_dp)])

    def line(vector):
        return vector.reshape(1, -1)

    def tie(*values):
        return lax.optimization_barrier(values)

    def add(*terms):
        return functools.reduce(lambda u, v: u + v, (t.astype(F32) for t in terms)).astype(BF16)

    def ordered(bit, mine, other, axis):
        return jnp.where(bit == 0, jnp.concatenate([mine, other], axis), jnp.concatenate([other, mine], axis))

    def heads_sum(value):
        if n_heads == 2:
            return value, across(value)
        total = lax.psum(value.astype(F32), "heads")
        high = total.astype(BF16)
        return high, (total - high.astype(F32)).astype(BF16)

    last = n_dp - 1

    class Chain:
        def __init__(self, value):
            self.value, self.size = value, value.shape[0] // n_dp
            self.up = self.down = self.out = None
            self.t = 0

        def piece(self, index):
            return lax.dynamic_slice_in_dim(self.value, jnp.clip(index, 0, last) * self.size, self.size, 0)

        def put(self, part, place):
            self.out = lax.dynamic_update_slice_in_dim(self.out, part, (place + last) * self.size, 0)

        def step(self):
            t, self.t = self.t, self.t + 1
            if t < last:
                up, down = self.piece(last + dp_index - t), self.piece(dp_index - last + t)
                if t > 0:
                    up, down = add(up, self.up), add(down, self.down)
                ends = range(t + 1)
            else:
                if t == last:
                    own = add(self.piece(dp_index), self.up, self.down)
                    self.out = jnp.zeros(((3 * n_dp - 2) * self.size,) + own.shape[1:], BF16)
                    self.put(own, dp_index)
                    up = down = own
                else:
                    up, down = self.up, self.down
                ends = range(t - last, last)
            self.up = lax.ppermute(up, "dp", [(i, i + 1) for i in ends])
            self.down = lax.ppermute(down, "dp", [(last - i, last - i - 1) for i in ends])
            if t >= last:
                self.put(self.up, dp_index - 1 - (t - last))
                self.put(self.down, dp_index + 1 + (t - last))

        def result(self):
            while self.t < 2 * last:
                self.step()
            return self.out[last * self.size : (last + n_dp) * self.size]

    def together(chains, behind):
        for chain, values in zip(chains + behind, held(chains + behind)):
            if chain.t == 0:
                (chain.value,) = values
            else:
                chain.up, chain.down = values
        for chain in chains:
            chain.step()

    def held(chains):
        flat = [v for c in chains for v in ([c.value] if c.t == 0 else [c.up, c.down])]
        flat = list(tie(*flat))
        return [[flat.pop(0) for _ in range(1 if c.t == 0 else 2)] for c in chains]

    def landed(chains, *values):
        for chain in chains:
            chain.up, chain.down, *values = tie(chain.up, chain.down, *values)
        return values

    def small_sum(value):
        for axis, size in (("rows", n_rows), ("dp", n_dp)):
            hop = 1
            while hop < size:
                value = value + lax.ppermute(value, axis, [(i, i ^ hop) for i in range(size)])
                hop *= 2
        return value

    keep_at, send_at = core * cols, (1 - core) * cols
    out_keep = lax.dynamic_slice_in_dim(output_weight, keep_at, cols, 0)
    out_send = lax.dynamic_slice_in_dim(output_weight, send_at, cols, 0)
    query_keep = lax.dynamic_slice_in_dim(query_weight, keep_at, cols, 1)
    query_send = lax.dynamic_slice_in_dim(query_weight, send_at, cols, 1)

    sides = 2 if n_heads == 2 else 1
    other_head = 1 - lax.axis_index("heads")

    def heads_acts(value):
        if n_heads == 2:
            return [value, across(value)]
        size = value.shape[1] // 2
        return [
            jnp.concatenate([lax.all_gather(v, "heads", axis=1, tiled=True) for v in (value[:, :size], value[:, size:])], 1)
        ]

    def heads_weights(keep, send, axis):
        whole_keep = lax.all_gather(keep, "heads", axis=axis, tiled=True)
        if n_heads > 2:
            return [whole_keep, near(whole_keep)]
        other = lax.dynamic_slice_in_dim(whole_keep, other_head * keep.shape[axis], keep.shape[axis], axis)
        return [keep, send, other, near(other)]

    expand_bias_far = far(expand_bias)
    cot_near = near(cotangent)

    blk = min(256, rows)
    grid = (rows // blk,)
    kv_bias = jnp.concatenate([jnp.zeros((dim,), F32), value_bias])
    normed_first, key_value = call(
        norm_kv_kernel,
        grid,
        [rows_of(tokens, blk), whole(line(pre_norm_gain)), whole(line(pre_norm_bias)), whole(key_value_weight), whole(line(kv_bias))],
        [
            ((rows, width), BF16, (blk, width), lambda i: (i, 0)),
            ((rows, 2 * dim), BF16, (blk, 2 * dim), lambda i: (i, 0)),
        ],
        flops=4 * rows * width * dim,
        moved=4 * rows * width,
    )
    far_kv = far(key_value)
    near_kv = near(key_value)
    far_kv, expand_start, contract_start = tie(far_kv, expand_weight, contract_weight)
    pieces = hid // min(512, hid)
    size = hid // pieces
    expand_far = [far(expand_start[:, :size])]
    columns = [[g + 2 * b for b in range(chips)] for g in range(2)]
    contract_both = lax.all_gather(contract_start, "rows", axis=0, tiled=True, axis_index_groups=columns)
    contract_far = lax.dynamic_slice_in_dim(contract_both, (1 - chip) * hid, hid, 0)
    pair_kv = ordered(core, key_value, near_kv, 0)
    far_pair = ordered(core, far_kv, near(far_kv), 0)
    kv_whole = ordered(chip, pair_kv, far_pair, 0)
    kv_turned = kv_whole.T

    query_a, query_for_near = call(
        project_kernel,
        grid,
        [
            (core.reshape(1), None, None),
            rows_of(normed_first, blk),
            (query_weight, (width, cols), lambda i, core: (0, core[0])),
            (line(query_bias), (1, cols), lambda i, core: (0, core[0])),
            (query_weight, (width, cols), lambda i, core: (0, 1 - core[0])),
            (line(query_bias), (1, cols), lambda i, core: (0, 1 - core[0])),
        ],
        [((rows, cols), BF16, (blk, cols), lambda i, *_: (i, 0))] * 2,
        prefetch=1,
        flops=4 * rows * width * cols,
        moved=2 * rows * width,
    )
    query_b = near(query_for_near)

    ends = jnp.cumsum(segment_lengths[0])
    own_place = row_index * rows
    near_place = (row_index + 1 - 2 * core) * rows
    steps = jnp.arange(rows, dtype=jnp.int32)
    places = jnp.concatenate([own_place + steps, near_place + steps])
    starts = jnp.max(jnp.where(ends[None, :] <= places[:, None], ends[None, :], 0), 1).astype(jnp.int32)

    def blocks_of(block):
        bq, bk = min(block[0], rows), min(block[1], window)
        first = places.reshape(-1, bq)[:, 0]
        start = starts.reshape(-1, bq)
        info = [first, start[:, 0] // bk, (first + bq - 1) // bk + 1, (start[:, -1] + bk - 1) // bk, (first + 1) // bk]
        return bq, bk, rows // bq, (jnp.stack(info).astype(jnp.int32), None, None)

    start_row = starts.reshape(1, -1)
    calls = 2 if group % 2 == 0 else 1
    part_heads = group // calls
    part_cols = part_heads * dim
    pairs_guess = 2 * rows * window // 4
    bq, bk, half, scalars = blocks_of(FORWARD_BLOCK)

    def at_a(n, half):
        return lambda i, *_: (jnp.minimum(i, half - 1), n)

    def at_b(n, half):
        return lambda i, *_: (jnp.maximum(i - half, 0), n)

    def attn_forward(n, info):
        return call(
            functools.partial(attn_forward_kernel, part_heads, half, bk, scale * LOG2E),
            (2 * half,),
            [
                (info, None, None),
                (query_a, (bq, part_cols), at_a(n, half)),
                (query_b, (bq, part_cols), at_b(n, half)),
                whole(kv_whole),
                (kv_turned, (dim, window), lambda i, *_: (1, 0)),
                (start_row, (1, bq), lambda i, *_: (0, i)),
            ],
            [
                ((rows, part_cols), BF16, (bq, part_cols), at_a(0, half)),
                ((rows, part_cols), BF16, (bq, part_cols), at_b(0, half)),
                ((part_heads, 2 * rows), F32, (part_heads, bq), lambda i, *_: (0, i)),
            ],
            scratch=[pltpu.VMEM((part_heads, bq), F32), pltpu.VMEM((part_heads, bq), F32), pltpu.VMEM((part_heads, dim, bq), F32)],
            prefetch=1,
            vmem=40,
            flops=16 * pairs_guess * part_cols,
            moved=8 * rows * part_cols,
        )

    attn, acts = [], []
    out_all = heads_weights(out_keep, out_send, 0)
    info = scalars[0]
    for n in range(calls):
        if n == 1:
            info, acts[0], expand_far[0] = tie(info, acts[0], expand_far[0])
        own, for_near, lse = attn_forward(n, info)
        if n == 0:
            expand_start, lse = tie(expand_start, lse)
            expand_far += [far(expand_start[:, k * size : (k + 1) * size]) for k in range(1, pieces)]
        other = near(for_near)
        attn.append((own, other, for_near, lse))
        acts.append(jnp.concatenate([own, other], 1))
    acts = [a for act in acts for a in heads_acts(act)]
    acts[-1], expand_far[-1] = tie(acts[-1], expand_far[-1])

    halves = 2
    part_rows = rows // halves
    wide = min(512, part_rows)
    chunk = min(256, part_rows)
    sub = part_rows // chunk
    down = lambda i: (i, 0)

    def output_part(j):
        base = j * part_rows // wide
        at = lambda i: (base + i, 0)
        return call(
            functools.partial(output_kernel, len(acts), sides),
            (part_rows // wide,),
            [(a, (wide, a.shape[1]), at) for a in acts]
            + [whole(w) for w in out_all]
            + [(tokens, (wide, width), at), whole(line(output_bias)), whole(line(mlp_norm_gain)), whole(line(mlp_norm_bias))],
            [((part_rows, width), F32, (wide, width), down), ((part_rows, width), BF16, (wide, width), down)],
            flops=2 * part_rows * width * width,
            moved=20 * part_rows * width,
            vmem=60,
            scratch=[
                pltpu.VMEM((sides, wide, width // sides), BF16),
                pltpu.VMEM((sides, width // sides, width), BF16),
            ]
            + [pltpu.VMEM((wide, width), F32)] * sides,
        )

    middles, seconds, others = [], [], []
    for j in range(halves):
        middle, normed_second = output_part(j)
        middles.append(middle)
        seconds.append(normed_second)
        others.append(near(normed_second))

    near_parts = [
        list(feed_near(
            chunk, j * part_rows, seconds[j], others[j], cotangent, cot_near, expand_weight, contract_weight, line(expand_bias)
        ))
        for j in range(halves)
    ]
    far_parts, far_sums, grads, sums_own = [], [], [], []
    for j in range(halves):
        kept = None
        for k in range(sub):
            far_bias = line(expand_bias_far)
            if sums_own:
                far_bias, sums_own[-1] = tie(far_bias, sums_own[-1])
            if len(grads) >= 3:
                far_bias, *grads[-3] = tie(far_bias, *grads[-3])
            (g_own, g_near), kept, bias_sum = feed_far(
                chunk,
                k,
                j * part_rows,
                seconds[j],
                others[j],
                cotangent,
                cot_near,
                expand_far,
                contract_far,
                far_bias,
                near_parts[j][2],
                near_parts[j][3],
                expand_weight,
                kept,
            )
            far_sums.append(bias_sum[0])
            sums_own.append(add(g_own, near(g_near)))
            grads.append(None)
            for m in range(len(grads)):
                if grads[m] is None and m < len(sums_own) - 1:
                    grads[m] = list(heads_sum(sums_own[m]))
        far_parts.append(list(kept))

    grads[-1] = list(heads_sum(sums_own[-1]))

    hblk = min(512, hid)
    n_blk = hid // hblk

    def contract_grad(parts, at, count):
        lefts = [(p[n], (part_rows, hblk), lambda i: (0, at + i)) for n in range(2) for p in parts]
        rights = [(c, (part_rows, width), lambda i, j=j: (j, 0)) for c in (cotangent, cot_near) for j in range(halves)]
        return call(
            pair_grad_kernel,
            (count,),
            lefts + rights,
            [((count * hblk, width), BF16, (hblk, width), down)],
            flops=4 * 2 * rows * width * hblk * count,
            moved=8 * width * rows,
            vmem=56,
        )[0]

    def expand_grad(parts, at, count):
        lefts = [(x, (part_rows, hblk), lambda i: (0, at + i)) for x in seconds + others]
        rights = [whole(p[n]) for n in (2, 3) for p in parts]
        return call(
            pair_grad_kernel,
            (count,),
            lefts + rights,
            [((count * hblk, hid), BF16, (hblk, hid), down)],
            flops=4 * 2 * rows * hblk * hid * count,
            moved=8 * width * rows,
            vmem=56,
        )[0]

    far_parts[1][3], *grads[1] = tie(far_parts[1][3], *grads[1])
    contract_send = contract_grad(far_parts, 0, n_blk)
    contract_moved = far(contract_send)
    expand_send = expand_grad(far_parts, 0, width // hblk)
    near_parts[1][3], expand_send, *grads[2] = tie(near_parts[1][3], expand_send, *grads[2])
    contract_own = contract_grad(near_parts, 0, n_blk)
    expand_own = expand_grad(near_parts, 0, width // hblk)
    bias_near = near_parts[0][4][0] + near_parts[1][4][0]
    bias_far = functools.reduce(lambda u, v: u + v, far_sums)
    expand_send, contract_moved = tie(expand_send, contract_moved)
    expand_moved = far(expand_send)
    grads[0][0], contract_own, expand_own = tie(grads[0][0], contract_own, expand_own)

    gms, lows, keeps, sends, sums = [], [], [], [], []
    for j in range(halves):
        terms = grads[j * sub : (j + 1) * sub]
        at = lambda i, j=j: (j, 0)
        gm, low, keep, send, part = call(
            functools.partial(second_back_kernel, sub),
            (1,),
            [whole(t[0]) for t in terms]
            + [whole(t[1]) for t in terms]
            + [
                whole(middles[j]),
                (cotangent, (part_rows, width), at),
                whole(line(mlp_norm_gain)),
                whole(out_keep),
                whole(out_send),
            ],
            [
                ((part_rows, width), F32, (part_rows, width), lambda i: (0, 0)),
                ((part_rows, width), BF16, (part_rows, width), lambda i: (0, 0)),
                ((part_rows, cols), BF16, (part_rows, cols), lambda i: (0, 0)),
                ((part_rows, cols), BF16, (part_rows, cols), lambda i: (0, 0)),
                ((8, width), F32, (8, width), lambda i: (0, 0)),
            ],
            flops=4 * part_rows * width * cols,
            moved=16 * part_rows * width + 4 * width * cols,
            vmem=58,
        )
        gms.append(gm)
        lows.append(low)
        keeps.append(keep)
        sends.append(near(send))
        sums.append(part[:4])
    grad_low = jnp.concatenate(lows)
    grad_middle = jnp.concatenate(gms)
    grad_a, grad_b = jnp.concatenate(keeps), jnp.concatenate(sends)
    mid_sums = functools.reduce(lambda u, v: u + v, sums)

    query_all = heads_weights(query_keep, query_send, 1)

    def dot_left(left, right):
        return dot_tn(left, right).astype(BF16)

    def chips_half(block):
        size = block.shape[0] // chips
        mine = lax.dynamic_slice_in_dim(block, chip * size, size, 0)
        other = lax.dynamic_slice_in_dim(block, (1 - chip) * size, size, 0)
        return mine, far(other)

    def all_blocks(total):
        pair = ordered(chip, total, far(total), 0)
        return pair, near(pair)

    contract_sum = add(contract_own, contract_moved)

    bq, bk, half, scalars = blocks_of(BACKWARD_BLOCK)

    def attn_backward(n, info):
        own, other, for_near, lse = attn[n]
        return call(
            functools.partial(attn_backward_kernel, part_heads, half, bk, scale, scale * LOG2E),
            (2 * half,),
            [
                (info, None, None),
                (query_a, (bq, part_cols), at_a(n, half)),
                (query_b, (bq, part_cols), at_b(n, half)),
                (grad_a, (bq, part_cols), at_a(n, half)),
                (grad_b, (bq, part_cols), at_b(n, half)),
                (own, (bq, part_cols), at_a(0, half)),
                (for_near, (bq, part_cols), at_b(0, half)),
                whole(kv_whole),
                (kv_turned, (dim, window), lambda i, *_: (0, 0)),
                (start_row, (1, bq), lambda i, *_: (0, i)),
                (lse, (part_heads, bq), lambda i, *_: (0, i)),
            ],
            [
                ((rows, part_cols), BF16, (bq, part_cols), at_a(0, half)),
                ((rows, part_cols), BF16, (bq, part_cols), at_b(0, half)),
                ((window, 2 * dim), F32, (window, 2 * dim), lambda i, *_: (0, 0)),
            ],
            scratch=[pltpu.VMEM((part_heads, dim, bq), F32)],
            prefetch=1,
            vmem=48,
            flops=40 * pairs_guess * part_cols,
            moved=16 * rows * part_cols,
        )

    back_acts, dq_own, dq_other, dkv = [], [], [], None
    info = scalars[0]
    for n in range(calls):
        if n == 0:
            info, contract_sum = tie(info, contract_sum)
            contract_total = lax.psum(contract_sum, "dp")
        if n == 1:
            info, back_acts[0], expand_moved = tie(info, back_acts[0], expand_moved)
        own, for_near, dkv_part = attn_backward(n, info)
        other = near(for_near)
        dq_own.append(own)
        dq_other.append(other)
        back_acts.append(jnp.concatenate([own, other], 1))
        dkv = dkv_part if dkv is None else dkv + dkv_part
    back_acts = [a for act in back_acts for a in heads_acts(act)]

    count = 2 * halves
    out_cols = min(512, width)
    near_parts[0][0], dkv = tie(near_parts[0][0], dkv)
    mlp_own, mlp_near = call(
        functools.partial(contract_kernel, count),
        (width // out_cols,),
        [whole(p[n]) for n in range(2) for p in near_parts]
        + [whole(p[n]) for n in range(2) for p in far_parts]
        + [(v, (hid, out_cols), lambda i: (0, i)) for v in (contract_weight, contract_far)],
        [((rows, width), BF16, (rows, out_cols), lambda i: (0, i))] * 2,
        flops=8 * rows * width * hid,
        moved=16 * rows * width,
        vmem=56,
    )

    dkv = dkv.reshape(chips, 2, rows, 2 * dim)

    def half_of(value, axis, bit):
        return lax.dynamic_index_in_dim(value, bit, axis, keepdims=False)

    core_sum = half_of(dkv, 1, core) + near(half_of(dkv, 1, 1 - core).astype(BF16)).astype(F32)
    chip_sum = add(half_of(core_sum, 0, chip), far(half_of(core_sum, 0, 1 - chip).astype(BF16)))
    first, second = heads_sum(chip_sum)
    grad_kv = add(first, second)

    input_grad, first_sums = call(
        functools.partial(first_back_kernel, len(back_acts), sides),
        (rows // wide,),
        [rows_of(a, wide) for a in back_acts]
        + [whole(w) for w in query_all]
        + [rows_of(grad_kv, wide), whole(key_value_weight)]
        + [rows_of(tokens, wide), rows_of(grad_middle, wide), whole(line(pre_norm_gain))],
        [((rows, width), BF16, (wide, width), down), ((8, width), F32, (8, width), lambda i: (0, 0))],
        flops=2 * rows * width * (width + 2 * dim),
        moved=20 * rows * width,
        vmem=60,
        scratch=[
            pltpu.VMEM((sides, wide, width // sides), BF16),
            pltpu.VMEM((sides, width, width // sides), BF16),
        ]
        + [pltpu.VMEM((wide, width), F32)] * sides,
    )

    mlp_first, mlp_second = heads_sum(add(mlp_own, near(mlp_near)))
    mlp_total = mlp_first.astype(F32) + mlp_second.astype(F32)
    layer_output = (jnp.concatenate(middles) + mlp_total + contract_bias).astype(BF16)

    own_all = jnp.concatenate([a[0] for a in attn], 1)
    other_all = jnp.concatenate([a[1] for a in attn], 1)
    out_half = add(*chips_half(add(dot_left(own_all, grad_low), near(dot_left(other_all, grad_low)))))
    expand_size = width // n_dp
    out_size = out_half.shape[0] * width // hid // n_dp
    joined = jnp.concatenate(
        [add(expand_own, expand_moved).reshape(n_dp, expand_size, hid), out_half.reshape(n_dp, out_size, hid)], 1
    )
    expand_chain = Chain(joined.reshape(-1, hid))
    kv_keep = lax.dynamic_slice_in_dim(grad_kv, core * dim, dim, 1)
    kv_send = lax.dynamic_slice_in_dim(grad_kv, (1 - core) * dim, dim, 1)
    query_sent = near(dot_left(normed_first, jnp.concatenate(dq_other + [kv_send], 1)))
    query_block = add(dot_left(normed_first, jnp.concatenate(dq_own + [kv_keep], 1)), query_sent)
    query_chain = Chain(add(*chips_half(query_block)))
    expand_chain.step()
    expand_chain.step()
    expand_chain.step()
    expand_chain.up, contract_total = tie(expand_chain.up, contract_total)
    for _ in range(3):
        together([expand_chain, query_chain], [])
    contract_weight_grad = contract_total.astype(F32)
    joined = expand_chain.result().reshape(n_dp, -1, hid)
    expand_weight_grad = joined[:, :expand_size].reshape(width, hid).astype(F32)
    out_block, out_block_near = all_blocks(joined[:, expand_size:].reshape(out_half.shape))
    output_weight_grad = ordered(core, out_block, out_block_near, 0).astype(F32)
    query_block, query_block_near = all_blocks(query_chain.result())
    query_weight_grad = ordered(core, query_block[:, :cols], query_block_near[:, :cols], 1).astype(F32)
    key_value_weight_grad = ordered(core, query_block[:, cols:], query_block_near[:, cols:], 1).astype(F32)

    dq_bias_keep = jnp.concatenate([jnp.sum(v.astype(F32), 0) for v in dq_own])
    dq_bias_send = jnp.concatenate([jnp.sum(v.astype(F32), 0) for v in dq_other])
    query_bias_part = ordered(core, dq_bias_keep, dq_bias_send, 0)
    value_bias_part = jnp.sum(grad_kv[:, dim:].astype(F32), 0)

    mid_total = lax.psum(mid_sums, ("dp", "rows"))
    late = small_sum(jnp.concatenate([first_sums[0], first_sums[1], query_bias_part, value_bias_part]))
    local = query_bias_part.shape[0]
    expand_bias_grad = bias_near + far(bias_far)
    hop = 1
    while hop < n_dp:
        expand_bias_grad = expand_bias_grad + lax.ppermute(expand_bias_grad, "dp", [(i, i ^ hop) for i in range(n_dp)])
        hop *= 2
    return (
        layer_output,
        input_grad,
        late[:width],
        late[width : 2 * width],
        query_weight_grad,
        late[2 * width : 2 * width + local],
        key_value_weight_grad,
        late[2 * width + local :],
        output_weight_grad,
        mid_total[2],
        mid_total[0],
        mid_total[1],
        expand_weight_grad,
        expand_bias_grad,
        contract_weight_grad,
        mid_total[3],
    )


def solution(mesh):
    both = P(("heads", "rows"))
    in_specs = (
        P(("dp", "rows"), None),
        P("dp", None),
        P(),
        P(),
        P(None, "heads"),
        P("heads"),
        P(),
        P(),
        P("heads", None),
        P(),
        P(),
        P(),
        P(None, ("heads", "rows")),
        both,
        P(("heads", "rows"), None),
        P(),
        P(("dp", "rows"), None),
    )
    out_specs = (
        P(("dp", "rows"), None),
        P(("dp", "rows"), None),
        P(),
        P(),
        P(None, "heads"),
        P("heads"),
        P(),
        P(),
        P("heads", None),
        P(),
        P(),
        P(),
        P(None, ("heads", "rows")),
        both,
        P(("heads", "rows"), None),
        P(),
    )
    return jax.shard_map(body, mesh=mesh, in_specs=in_specs, out_specs=out_specs, check_vma=False)
```

```python
import functools
import math

import jax
import jax.numpy as jnp
from jax import lax
from jax.experimental import pallas as pl
from jax.experimental.pallas import tpu as pltpu
from jax.sharding import PartitionSpec as P

NORM_EPSILON = 1e-05
FAR = -1e30
LOG2E = 1.4426950408889634
GELU_A = math.sqrt(2.0 / math.pi)
GELU_B = 0.044715
F32 = jnp.float32
BF16 = jnp.bfloat16
MIB = 1024 * 1024
FORWARD_BLOCK = (512, 1024)
BACKWARD_BLOCK = (256, 1024)


def dot(left, right):
    return jnp.dot(left, right, preferred_element_type=F32)


def dot_tn(left, right):
    return lax.dot_general(left, right, (((0,), (0,)), ((), ())), preferred_element_type=F32)


def dot_nt(left, right):
    return lax.dot_general(left, right, (((1,), (1,)), ((), ())), preferred_element_type=F32)


def call(kernel, grid, ins, outs, scratch=(), prefetch=0, vmem=48, flops=0, moved=0, alias=None):
    arrays = [a for a, _, _ in ins[prefetch:]]
    specs = [
        pl.BlockSpec(b, m, pipeline_mode=pl.Buffered(1)) if b == a.shape else pl.BlockSpec(b, m) for a, b, m in ins[prefetch:]
    ]
    scalars = [a for a, _, _ in ins[:prefetch]]
    return pl.pallas_call(
        kernel,
        grid_spec=pltpu.PrefetchScalarGridSpec(
            num_scalar_prefetch=prefetch,
            grid=grid,
            in_specs=specs,
            out_specs=[pl.BlockSpec(b, m) for _, _, b, m in outs],
            scratch_shapes=list(scratch),
        ),
        out_shape=[jax.ShapeDtypeStruct(s, d) for s, d, _, _ in outs],
        compiler_params=pltpu.CompilerParams(vmem_limit_bytes=vmem * MIB),
        cost_estimate=pl.CostEstimate(flops=int(flops), bytes_accessed=int(moved), transcendentals=0),
        input_output_aliases=alias or {},
    )(*scalars, *arrays)


def whole(array):
    zeros = (0,) * array.ndim
    return (array, array.shape, lambda *_: zeros)


def rows_of(array, block):
    return (array, (block, array.shape[1]), lambda i, *_: (i, 0))


def normed(values, gain, bias):
    mean = jnp.mean(values, -1, keepdims=True)
    centred = values - mean
    var = jnp.mean(centred * centred, -1, keepdims=True)
    return centred * lax.rsqrt(var + NORM_EPSILON) * gain + bias


def norm_back(values, grad, gain):
    mean = jnp.mean(values, -1, keepdims=True)
    centred = values - mean
    var = jnp.mean(centred * centred, -1, keepdims=True)
    inverse = lax.rsqrt(var + NORM_EPSILON)
    xhat = centred * inverse
    g = grad * gain
    g_mean = jnp.mean(g, -1, keepdims=True)
    gx_mean = jnp.mean(g * xhat, -1, keepdims=True)
    return xhat, (g - g_mean - xhat * gx_mean) * inverse


def norm_kv_kernel(t_ref, g_ref, b_ref, w_ref, wb_ref, n_ref, kv_ref):
    low = normed(t_ref[...].astype(F32), g_ref[...], b_ref[...]).astype(BF16)
    n_ref[...] = low
    kv_ref[...] = (dot(low, w_ref[...]) + wb_ref[...]).astype(BF16)


def project_kernel(core, n_ref, wa_ref, ba_ref, wb_ref, bb_ref, a_ref, b_ref):
    low = n_ref[...]
    b_ref[...] = (dot(low, wb_ref[...]) + bb_ref[...]).astype(BF16)
    a_ref[...] = (dot(low, wa_ref[...]) + ba_ref[...]).astype(BF16)


def attn_forward_kernel(heads, half, bk, scale2, info, qa_ref, qb_ref, kv_ref, vt_ref, st_ref, oa_ref, ob_ref, lse_ref, m_ref, l_ref, acc_ref):
    i = pl.program_id(0)
    first, low, high, clear_from, clear_to = (info[n, i] for n in range(5))
    bq, dim = qa_ref.shape[0], kv_ref.shape[1] // 2
    in_a = i < half
    start = st_ref[...]
    place = first + lax.broadcasted_iota(jnp.int32, (1, bq), 1)
    queries = jnp.where(in_a, qa_ref[...], qb_ref[...])
    m_ref[...] = jnp.full_like(m_ref, FAR)
    l_ref[...] = jnp.zeros_like(l_ref)
    acc_ref[...] = jnp.zeros_like(acc_ref)

    def step(block, masked):
        begin = pl.multiple_of(block * bk, bk)
        keys = kv_ref[pl.ds(begin, bk), :dim]
        values = vt_ref[:, pl.ds(begin, bk)]
        if masked:
            key_place = begin + lax.broadcasted_iota(jnp.int32, (bk, 1), 0)
            allowed = (key_place >= start) & (key_place <= place)
        for h in range(heads):
            s = dot_nt(keys, queries[:, h * dim : (h + 1) * dim])
            if masked:
                s = jnp.where(allowed, s, FAR)
            old = m_ref[h : h + 1, :]
            new = jnp.maximum(old, jnp.max(s, 0, keepdims=True) * scale2)
            p = jnp.exp2(s * scale2 - new)
            fix = jnp.exp2(old - new)
            l_ref[h : h + 1, :] = l_ref[h : h + 1, :] * fix + jnp.sum(p, 0, keepdims=True)
            m_ref[h : h + 1, :] = new
            acc_ref[h] = acc_ref[h] * fix + dot(values, p.astype(BF16))

    def body(block, carry):
        clear = (block >= clear_from) & (block < clear_to)

        @pl.when(clear)
        def _():
            step(block, False)

        @pl.when(jnp.logical_not(clear))
        def _():
            step(block, True)

        return carry

    lax.fori_loop(low, high, body, 0)
    outs = []
    for h in range(heads):
        total = l_ref[h : h + 1, :]
        outs.append((acc_ref[h] / total).T.astype(BF16))
    lse_ref[...] = m_ref[...] + jnp.log2(l_ref[...])

    @pl.when(in_a)
    def _():
        for h in range(heads):
            oa_ref[:, h * dim : (h + 1) * dim] = outs[h]

    @pl.when(jnp.logical_not(in_a))
    def _():
        for h in range(heads):
            ob_ref[:, h * dim : (h + 1) * dim] = outs[h]


def attn_backward_kernel(
    heads, half, bk, scale, scale2, info, qa_ref, qb_ref, ga_ref, gb_ref, oa_ref, ob_ref, kv_ref, kt_ref, st_ref, lse_ref, dqa_ref, dqb_ref, dkv_ref, dq_ref
):
    i = pl.program_id(0)
    first, low, high, clear_from, clear_to = (info[n, i] for n in range(5))
    bq, dim = qa_ref.shape[0], kv_ref.shape[1] // 2
    in_a = i < half

    @pl.when(i == 0)
    def _():
        dkv_ref[...] = jnp.zeros_like(dkv_ref)

    start = st_ref[...]
    place = first + lax.broadcasted_iota(jnp.int32, (1, bq), 1)
    queries = jnp.where(in_a, qa_ref[...], qb_ref[...])
    grads = jnp.where(in_a, ga_ref[...], gb_ref[...])
    outs = jnp.where(in_a, oa_ref[...], ob_ref[...])
    inner, lse = [], []
    for h in range(heads):
        cut = slice(h * dim, (h + 1) * dim)
        product = grads[:, cut].astype(F32) * outs[:, cut].astype(F32)
        inner.append(jnp.sum(product.T, 0, keepdims=True))
        lse.append(lse_ref[h : h + 1, :])
    dq_ref[...] = jnp.zeros_like(dq_ref)

    def step(block, masked):
        begin = pl.multiple_of(block * bk, bk)
        keys = kv_ref[pl.ds(begin, bk), :dim]
        values = kv_ref[pl.ds(begin, bk), dim:]
        keys_t = kt_ref[:, pl.ds(begin, bk)]
        if masked:
            key_place = begin + lax.broadcasted_iota(jnp.int32, (bk, 1), 0)
            allowed = (key_place >= start) & (key_place <= place)
        dk = None
        for h in range(heads):
            cut = slice(h * dim, (h + 1) * dim)
            s = dot_nt(keys, queries[:, cut])
            dp = dot_nt(values, grads[:, cut])
            p = jnp.exp2(s * scale2 - lse[h])
            if masked:
                p = jnp.where(allowed, p, 0.0)
            ds = (p * (dp - inner[h])).astype(BF16)
            dv_part = dot(p.astype(BF16), grads[:, cut])
            dk_part = dot(ds, queries[:, cut])
            dk, dv = (dk_part, dv_part) if dk is None else (dk + dk_part, dv + dv_part)
            dq_ref[h] += dot(keys_t, ds)
        dkv_ref[pl.ds(begin, bk), :dim] += dk * scale
        dkv_ref[pl.ds(begin, bk), dim:] += dv

    def body(block, carry):
        clear = (block >= clear_from) & (block < clear_to)

        @pl.when(clear)
        def _():
            step(block, False)

        @pl.when(jnp.logical_not(clear))
        def _():
            step(block, True)

        return carry

    lax.fori_loop(low, high, body, 0)

    def leave(ref):
        for h in range(heads):
            ref[:, h * dim : (h + 1) * dim] = (dq_ref[h] * scale).T.astype(BF16)

    @pl.when(in_a)
    def _():
        leave(dqa_ref)

    @pl.when(jnp.logical_not(in_a))
    def _():
        leave(dqb_ref)


def balanced(acts, weights, product, by_rows, scratch):
    act_ref, weight_ref, sums = scratch[0], scratch[1], scratch[2:]
    sides = len(sums)
    calls = len(acts) // sides
    cols = acts[0].shape[1] // 2
    for n in range(sides):

        @pl.when(pl.program_id(0) == 0)
        def _():
            keep, send = weights[2 * n], weights[2 * n + 1]
            if by_rows:
                size = keep.shape[0]
                weight_ref[n, :size, :] = keep[...]
                weight_ref[n, size:, :] = send[...]
            else:
                size = keep.shape[1]
                weight_ref[n, :, :size] = keep[...]
                weight_ref[n, :, size:] = send[...]

        for k in range(calls):
            act = acts[k * sides + n]
            act_ref[n, :, k * cols : (k + 1) * cols] = act[:, :cols]
            act_ref[n, :, (calls + k) * cols : (calls + k + 1) * cols] = act[:, cols:]
        sums[n][...] = product(act_ref[n], weight_ref[n])
    return functools.reduce(lambda u, v: u + v, [r[...] for r in sums])


def output_kernel(count, sides, *refs):
    acts, weights = refs[:count], refs[count : count + 2 * sides]
    t_ref, ob_ref, g_ref, b_ref, mid_ref, n_ref, *scratch = refs[count + 2 * sides :]
    near = balanced(acts, weights, dot, True, scratch)
    middle = t_ref[...].astype(F32) + near + ob_ref[...]
    mid_ref[...] = middle
    n_ref[...] = normed(middle, g_ref[...], b_ref[...]).astype(BF16)


def feed_tile(x, c, w, v, bias):
    before = dot(x, w) + bias
    grad = dot_nt(c, v)
    square = before * before
    t = jnp.tanh(before * (GELU_A + (GELU_A * GELU_B) * square))
    half = 0.5 + 0.5 * t
    slope = half + before * (half * (1.0 - t)) * (GELU_A + (3.0 * GELU_A * GELU_B) * square)
    return (before * half).astype(BF16), grad * slope


def stack(scratch, first, second):
    rows = first.shape[0]
    scratch[:rows, :] = first[...]
    scratch[rows:, :] = second[...]


def add_to(ref, value, fresh):
    @pl.when(fresh)
    def _():
        ref[...] = jnp.zeros_like(ref)

    ref[...] += jnp.broadcast_to(value, ref.shape)


def feed_near_kernel(blk, xa_ref, xb_ref, ca_ref, cb_ref, w_ref, v_ref, b_ref, ha_ref, hb_ref, da_ref, db_ref, sum_ref, x_ref, c_ref):
    rows = xa_ref.shape[0]
    stack(x_ref, xa_ref, xb_ref)
    stack(c_ref, ca_ref, cb_ref)
    sums = []
    for at in range(0, w_ref.shape[1], blk):
        cut = slice(at, at + blk)
        hidden, grad = feed_tile(x_ref[...], c_ref[...], w_ref[:, cut], v_ref[cut, :], b_ref[:, cut])
        low = grad.astype(BF16)
        ha_ref[:, cut] = hidden[:rows]
        hb_ref[:, cut] = hidden[rows:]
        da_ref[:, cut] = low[:rows]
        db_ref[:, cut] = low[rows:]
        sums.append(jnp.sum(grad, 0, keepdims=True))
    add_to(sum_ref, jnp.concatenate(sums, 1), pl.program_id(0) == 0)


def feed_far_kernel(steps, order, xa_ref, xb_ref, ca_ref, cb_ref, b_ref, ea_ref, eb_ref, u_ref, *rest):
    w_refs, z_refs, v_refs = rest[:steps], rest[steps : 2 * steps], rest[2 * steps : 3 * steps]
    ga_ref, gb_ref, ha_ref, hb_ref, da_ref, db_ref, sum_ref, x_ref, c_ref, e_ref, low_ref = rest[-11:]
    i = pl.program_id(0)
    rows = xa_ref.shape[0]

    @pl.when(i == 0)
    def _():
        stack(x_ref, xa_ref, xb_ref)
        stack(c_ref, ca_ref, cb_ref)
        stack(e_ref, ea_ref, eb_ref)

    for k in range(steps):

        @pl.when(i == k)
        def _():
            hidden, grad = feed_tile(x_ref[...], c_ref[...], w_refs[k][...], v_refs[k][...], b_ref[...])
            low = grad.astype(BF16)
            ha_ref[...] = hidden[:rows]
            hb_ref[...] = hidden[rows:]
            da_ref[...] = low[:rows]
            db_ref[...] = low[rows:]
            low_ref[k] = low
            sum_ref[...] = jnp.broadcast_to(jnp.sum(grad, 0, keepdims=True), sum_ref.shape)

    @pl.when(i >= steps)
    def _():
        total = dot_nt(e_ref[...], u_ref[...])
        for k in range(steps):
            total = total + dot_nt(low_ref[k], z_refs[k][...])
        ga_ref[...] = total[:rows].astype(BF16)
        gb_ref[...] = total[rows:].astype(BF16)


def feed_near(chunk, first_row, x_own, x_other, c_own, c_other, w, v, bias):
    rows, width = x_own.shape
    hid = w.shape[1]
    base = first_row // chunk
    at = lambda i: (i, 0)
    at_all = lambda i: (base + i, 0)
    return call(
        functools.partial(feed_near_kernel, min(512, hid)),
        (rows // chunk,),
        [
            (x_own, (chunk, width), at),
            (x_other, (chunk, width), at),
            (c_own, (chunk, width), at_all),
            (c_other, (chunk, width), at_all),
            whole(w),
            whole(v),
            whole(bias),
        ],
        [((rows, hid), BF16, (chunk, hid), at)] * 4 + [((8, hid), F32, (8, hid), lambda i: (0, 0))],
        scratch=[pltpu.VMEM((2 * chunk, width), BF16)] * 2,
        vmem=56,
        flops=8 * rows * width * hid,
        moved=8 * width * hid + 8 * rows * width,
    )


def feed_far(chunk, index, first_row, x_own, x_other, c_own, c_other, w, v, bias, near_own, near_other, w_near, kept, parity):
    rows, width = x_own.shape
    hid = w_near.shape[1]
    steps = len(w)
    blk = hid // steps
    out_blk = min(512, width)
    back = width // out_blk
    base = first_row // chunk
    at = lambda i, p: (index, 0)
    at_all = lambda i, p: (base + index, 0)
    tile = lambda i, p: lax.rem(jnp.minimum(i, steps - 1) + p[0], steps)
    after = lambda i: jnp.maximum(i - steps, 0)
    ins = [
        (x_own, (chunk, width), at),
        (x_other, (chunk, width), at),
        (c_own, (chunk, width), at_all),
        (c_other, (chunk, width), at_all),
        (bias, (1, blk), lambda i, p: (0, tile(i, p))),
        (near_own, (chunk, hid), at),
        (near_other, (chunk, hid), at),
        (w_near, (out_blk, hid), lambda i, p: (after(i), 0)),
    ]
    ins += [whole(p) for p in w]
    ins += [(u, (out_blk, blk), lambda i, p: (after(i), 0)) for u in w]
    ins += [whole(p) for p in v]
    outs = [((chunk, width), BF16, (chunk, out_blk), lambda i, p: (0, after(i)))] * 2
    outs += [((rows, hid), BF16, (chunk, blk), lambda i, p: (index, tile(i, p)))] * 4
    outs += [((8, hid), F32, (8, blk), lambda i, p: (0, tile(i, p)))]
    alias = {}
    arrays = [a for a, _, _ in ins]
    specs = [
        pl.BlockSpec(b, m, pipeline_mode=pl.Buffered(1)) if b == a.shape else pl.BlockSpec(b, m) for a, b, m in ins
    ]
    if kept is not None:
        for place, array in enumerate(kept):
            alias[len(arrays) + 1] = 2 + place
            arrays.append(array)
            specs.append(pl.BlockSpec(memory_space=pl.ANY))
    result = pl.pallas_call(
        functools.partial(feed_far_kernel, steps),
        grid_spec=pltpu.PrefetchScalarGridSpec(
            num_scalar_prefetch=1,
            grid=(steps + back,),
            in_specs=specs,
            out_specs=[pl.BlockSpec(b, m) for _, _, b, m in outs],
            scratch_shapes=[
                pltpu.VMEM((2 * chunk, width), BF16),
                pltpu.VMEM((2 * chunk, width), BF16),
                pltpu.VMEM((2 * chunk, hid), BF16),
                pltpu.VMEM((steps, 2 * chunk, blk), BF16),
            ],
        ),
        out_shape=[jax.ShapeDtypeStruct(s, d) for s, d, _, _ in outs],
        input_output_aliases=alias,
        compiler_params=pltpu.CompilerParams(vmem_limit_bytes=56 * MIB),
        cost_estimate=pl.CostEstimate(
            flops=8 * 2 * chunk * width * hid, bytes_accessed=8 * width * hid + 24 * chunk * width, transcendentals=0
        ),
    )(parity.reshape(1), *arrays)
    return result[:2], result[2:6], result[6]


def contract_kernel(count, pieces, parity, *refs):
    near, far = refs[:count], refs[count : count + count * pieces]
    va_ref, *vb_refs = refs[count + count * pieces : count + count * pieces + pieces + 1]
    own_ref, other_ref = refs[-2:]
    size = near[0].shape[0]
    for k in range(count):
        y_ref = own_ref if k < count // 2 else other_ref
        at = k % (count // 2) * size
        total = dot(near[k][...], va_ref[...])
        for n in range(pieces):
            total = total + dot(far[k * pieces + n][...], vb_refs[n][...])
        y_ref[at : at + size, :] = total.astype(BF16)


def pair_grad_kernel(*refs):
    out_ref = refs[-1]
    count = (len(refs) - 1) // 2
    total = None
    for left, right in zip(refs[:count], refs[count:-1]):
        piece = dot_tn(left[...], right[...])
        total = piece if total is None else total + piece
    out_ref[...] = total.astype(BF16)


def second_back_kernel(count, *refs):
    firsts, seconds = refs[:count], refs[count : 2 * count]
    mid_ref, cot_ref, gain_ref, wk_ref, ws_ref, gm_ref, low_ref, keep_ref, send_ref, sums_ref = refs[2 * count :]
    size = firsts[0].shape[0]
    totals = [0.0, 0.0, 0.0, 0.0]
    for k in range(count):
        at = slice(k * size, (k + 1) * size)
        grad = firsts[k][...].astype(F32) + seconds[k][...].astype(F32)
        xhat, back = norm_back(mid_ref[at, :], grad, gain_ref[...])
        cot = cot_ref[at, :].astype(F32)
        total = cot + back
        gm_ref[at, :] = total
        low_ref[at, :] = total.astype(BF16)
        for n, value in enumerate((grad * xhat, grad, total, cot)):
            totals[n] = totals[n] + jnp.sum(value, 0, keepdims=True)
    send_ref[...] = dot_nt(low_ref[...], ws_ref[...]).astype(BF16)
    keep_ref[...] = dot_nt(low_ref[...], wk_ref[...]).astype(BF16)
    for n in range(4):
        sums_ref[n : n + 1, :] = totals[n]


def first_back_kernel(count, sides, *refs):
    acts, weights = refs[:count], refs[count : count + 2 * sides]
    kv_ref, kvw_ref, t_ref, gm_ref, gain_ref, out_ref, sums_ref, *scratch = refs[count + 2 * sides :]
    grad = balanced(acts, weights, dot_nt, False, scratch) + dot_nt(kv_ref[...], kvw_ref[...])
    xhat, back = norm_back(t_ref[...].astype(F32), grad, gain_ref[...])
    out_ref[...] = (gm_ref[...] + back).astype(BF16)

    @pl.when(pl.program_id(0) == 0)
    def _():
        sums_ref[...] = jnp.zeros_like(sums_ref)

    sums_ref[0:1, :] += jnp.sum(grad * xhat, 0, keepdims=True)
    sums_ref[1:2, :] += jnp.sum(grad, 0, keepdims=True)


def side_by_side_kernel(core, mine_ref, near_ref, query_ref, kv_ref):
    first = core[0] == 0
    mine, near = mine_ref[...].astype(F32), near_ref[...].astype(F32)
    cols = query_ref.shape[1] // 2
    left, right = jnp.where(first, mine, near), jnp.where(first, near, mine)
    query_ref[:, :cols] = left[:, :cols]
    query_ref[:, cols:] = right[:, :cols]
    kv_ref[:, : kv_ref.shape[1] // 2] = left[:, cols:]
    kv_ref[:, kv_ref.shape[1] // 2 :] = right[:, cols:]


def body(
    tokens,
    segment_lengths,
    pre_norm_gain,
    pre_norm_bias,
    query_weight,
    query_bias,
    key_value_weight,
    value_bias,
    output_weight,
    output_bias,
    mlp_norm_gain,
    mlp_norm_bias,
    expand_weight,
    expand_bias,
    contract_weight,
    contract_bias,
    cotangent,
):
    rows, width = tokens.shape
    n_heads, n_rows, n_dp = (lax.axis_size(a) for a in ("heads", "rows", "dp"))
    row_index = lax.axis_index("rows")
    core = lax.rem(row_index, 2)
    dim = key_value_weight.shape[1] // 2
    local_heads = query_weight.shape[1] // dim
    group = local_heads // 2
    cols = group * dim
    window = rows * n_rows
    scale = 1.0 / math.sqrt(dim)
    hid = expand_weight.shape[1]

    chips = n_rows // 2
    chip = row_index // 2
    dp_index = lax.axis_index("dp")

    def near(value):
        return lax.ppermute(value, "rows", [(i, i ^ 1) for i in range(n_rows)])

    def far(value):
        return lax.ppermute(value, "rows", [(i, i ^ 2) for i in range(n_rows)])

    def across(value):
        return lax.ppermute(value, "heads", [(0, 1), (1, 0)])

    def beside(value):
        return lax.ppermute(value, "dp", [(i, i ^ 1) for i in range(n_dp)])

    def line(vector):
        return vector.reshape(1, -1)

    def tie(*values):
        return lax.optimization_barrier(values)

    def add(*terms):
        return functools.reduce(lambda u, v: u + v, (t.astype(F32) for t in terms)).astype(BF16)

    def ordered(bit, mine, other, axis):
        return jnp.where(bit == 0, jnp.concatenate([mine, other], axis), jnp.concatenate([other, mine], axis))

    def heads_sum(value):
        if n_heads == 2:
            return value, across(value)
        total = lax.psum(value.astype(F32), "heads")
        high = total.astype(BF16)
        return high, (total - high.astype(F32)).astype(BF16)

    last = n_dp - 1

    class Chain:
        def __init__(self, value):
            self.value, self.size = value, value.shape[0] // n_dp
            self.up = self.down = self.out = None
            self.t = 0

        def piece(self, index):
            return lax.dynamic_slice_in_dim(self.value, jnp.clip(index, 0, last) * self.size, self.size, 0)

        def put(self, part, place):
            self.out = lax.dynamic_update_slice_in_dim(self.out, part, (place + last) * self.size, 0)

        def step(self):
            t, self.t = self.t, self.t + 1
            if t < last:
                up, down = self.piece(last + dp_index - t), self.piece(dp_index - last + t)
                if t > 0:
                    up, down = add(up, self.up), add(down, self.down)
                ends = range(t + 1)
            else:
                if t == last:
                    own = add(self.piece(dp_index), self.up, self.down)
                    self.out = jnp.zeros(((3 * n_dp - 2) * self.size,) + own.shape[1:], BF16)
                    self.put(own, dp_index)
                    up = down = own
                else:
                    up, down = self.up, self.down
                ends = range(t - last, last)
            self.up = lax.ppermute(up, "dp", [(i, i + 1) for i in ends])
            self.down = lax.ppermute(down, "dp", [(last - i, last - i - 1) for i in ends])
            if t >= last:
                self.put(self.up, dp_index - 1 - (t - last))
                self.put(self.down, dp_index + 1 + (t - last))

        def result(self):
            while self.t < 2 * last:
                self.step()
            return self.out[last * self.size : (last + n_dp) * self.size]

    def together(chains, behind):
        for chain, values in zip(chains + behind, held(chains + behind)):
            if chain.t == 0:
                (chain.value,) = values
            else:
                chain.up, chain.down = values
        for chain in chains:
            chain.step()

    def held(chains):
        flat = [v for c in chains for v in ([c.value] if c.t == 0 else [c.up, c.down])]
        flat = list(tie(*flat))
        return [[flat.pop(0) for _ in range(1 if c.t == 0 else 2)] for c in chains]

    def landed(chains, *values):
        for chain in chains:
            chain.up, chain.down, *values = tie(chain.up, chain.down, *values)
        return values

    def small_sum(value):
        for axis, size in (("rows", n_rows), ("dp", n_dp)):
            hop = 1
            while hop < size:
                value = value + lax.ppermute(value, axis, [(i, i ^ hop) for i in range(size)])
                hop *= 2
        return value

    keep_at, send_at = core * cols, (1 - core) * cols
    query_keep = lax.dynamic_slice_in_dim(query_weight, keep_at, cols, 1)
    query_send = lax.dynamic_slice_in_dim(query_weight, send_at, cols, 1)

    sides = 2 if n_heads == 2 else 1
    other_head = 1 - lax.axis_index("heads")

    def heads_acts(value):
        if n_heads == 2:
            return [value, across(value)]
        size = value.shape[1] // 2
        return [
            jnp.concatenate([lax.all_gather(v, "heads", axis=1, tiled=True) for v in (value[:, :size], value[:, size:])], 1)
        ]

    def heads_weights(keep, send, axis):
        whole_keep = lax.all_gather(keep, "heads", axis=axis, tiled=True)
        if n_heads > 2:
            return [whole_keep, near(whole_keep)]
        other = lax.dynamic_slice_in_dim(whole_keep, other_head * keep.shape[axis], keep.shape[axis], axis)
        return [keep, send, other, near(other)]

    expand_bias_far = far(expand_bias)
    cot_near = near(cotangent)

    blk = min(256, rows)
    grid = (rows // blk,)
    kv_bias = jnp.concatenate([jnp.zeros((dim,), F32), value_bias])
    normed_first, key_value = call(
        norm_kv_kernel,
        grid,
        [rows_of(tokens, blk), whole(line(pre_norm_gain)), whole(line(pre_norm_bias)), whole(key_value_weight), whole(line(kv_bias))],
        [
            ((rows, width), BF16, (blk, width), lambda i: (i, 0)),
            ((rows, 2 * dim), BF16, (blk, 2 * dim), lambda i: (i, 0)),
        ],
        flops=4 * rows * width * dim,
        moved=4 * rows * width,
    )
    output_weight, key_value = tie(output_weight, key_value)
    out_keep = lax.dynamic_slice_in_dim(output_weight, keep_at, cols, 0)
    out_send = lax.dynamic_slice_in_dim(output_weight, send_at, cols, 0)
    far_kv = far(key_value)
    near_kv = near(key_value)
    far_kv, expand_start, contract_start = tie(far_kv, expand_weight, contract_weight)
    pieces = hid // min(512, hid)
    size = hid // pieces
    helped = pieces == 2 and n_dp % 2 == 0
    parity = lax.rem(dp_index, 2) if helped else jnp.int32(0)
    if helped:
        expand_far = [far(lax.dynamic_slice_in_dim(expand_start, parity * size, size, 1))]
    else:
        expand_far = [far(expand_start[:, k * size : (k + 1) * size]) for k in range(pieces)]
    contract_start, expand_far[0] = tie(contract_start, expand_far[0])
    if helped:
        contract_far = [far(lax.dynamic_slice_in_dim(contract_start, parity * size, size, 0))]
    else:
        contract_far = [far(contract_start[k * size : (k + 1) * size]) for k in range(pieces)]
    pair_kv = ordered(core, key_value, near_kv, 0)
    far_pair = ordered(core, far_kv, near(far_kv), 0)
    kv_whole = ordered(chip, pair_kv, far_pair, 0)
    kv_turned = kv_whole.T

    query_a, query_for_near = call(
        project_kernel,
        grid,
        [
            (core.reshape(1), None, None),
            rows_of(normed_first, blk),
            (query_weight, (width, cols), lambda i, core: (0, core[0])),
            (line(query_bias), (1, cols), lambda i, core: (0, core[0])),
            (query_weight, (width, cols), lambda i, core: (0, 1 - core[0])),
            (line(query_bias), (1, cols), lambda i, core: (0, 1 - core[0])),
        ],
        [((rows, cols), BF16, (blk, cols), lambda i, *_: (i, 0))] * 2,
        prefetch=1,
        flops=4 * rows * width * cols,
        moved=2 * rows * width,
    )
    query_b = near(query_for_near)

    ends = jnp.cumsum(segment_lengths[0])
    own_place = row_index * rows
    near_place = (row_index + 1 - 2 * core) * rows
    steps = jnp.arange(rows, dtype=jnp.int32)
    places = jnp.concatenate([own_place + steps, near_place + steps])
    starts = jnp.max(jnp.where(ends[None, :] <= places[:, None], ends[None, :], 0), 1).astype(jnp.int32)

    def blocks_of(block):
        bq, bk = min(block[0], rows), min(block[1], window)
        first = places.reshape(-1, bq)[:, 0]
        start = starts.reshape(-1, bq)
        info = [first, start[:, 0] // bk, (first + bq - 1) // bk + 1, (start[:, -1] + bk - 1) // bk, (first + 1) // bk]
        return bq, bk, rows // bq, (jnp.stack(info).astype(jnp.int32), None, None)

    start_row = starts.reshape(1, -1)
    calls = 2 if group % 2 == 0 else 1
    part_heads = group // calls
    part_cols = part_heads * dim
    pairs_guess = 2 * rows * window // 4
    bq, bk, half, scalars = blocks_of(FORWARD_BLOCK)

    def at_a(n, half):
        return lambda i, *_: (jnp.minimum(i, half - 1), n)

    def at_b(n, half):
        return lambda i, *_: (jnp.maximum(i - half, 0), n)

    def attn_forward(n, info):
        return call(
            functools.partial(attn_forward_kernel, part_heads, half, bk, scale * LOG2E),
            (2 * half,),
            [
                (info, None, None),
                (query_a, (bq, part_cols), at_a(n, half)),
                (query_b, (bq, part_cols), at_b(n, half)),
                whole(kv_whole),
                (kv_turned, (dim, window), lambda i, *_: (1, 0)),
                (start_row, (1, bq), lambda i, *_: (0, i)),
            ],
            [
                ((rows, part_cols), BF16, (bq, part_cols), at_a(0, half)),
                ((rows, part_cols), BF16, (bq, part_cols), at_b(0, half)),
                ((part_heads, 2 * rows), F32, (part_heads, bq), lambda i, *_: (0, i)),
            ],
            scratch=[pltpu.VMEM((part_heads, bq), F32), pltpu.VMEM((part_heads, bq), F32), pltpu.VMEM((part_heads, dim, bq), F32)],
            prefetch=1,
            vmem=40,
            flops=16 * pairs_guess * part_cols,
            moved=8 * rows * part_cols,
        )

    attn, acts = [], []
    if n_heads == 2:
        out_other = across(out_keep)
    else:
        out_all = heads_weights(out_keep, out_send, 0)
    info = scalars[0]
    for n in range(calls):
        if n == 1:
            if n_heads == 2:
                info, out_other = tie(info, out_other)
            info, expand_far[0] = tie(info, expand_far[0])
        own, for_near, lse = attn_forward(n, info)
        if n == 1:
            own, for_near, acts[0][-1] = tie(own, for_near, acts[0][-1])
        other = near(for_near)
        attn.append((own, other, for_near, lse))
        act = jnp.concatenate([own, other], 1)
        if n == 0 and calls > 1:
            info, act, cot_near = tie(info, act, cot_near)
        acts.append(heads_acts(act))
    acts = [a for act in acts for a in act]
    if n_heads == 2:
        out_all = [out_keep, out_send, out_other, near(out_other)]
    if helped:
        expand_far.append(beside(expand_far[0]))
    acts[-1], contract_far[0], expand_far[-1] = tie(acts[-1], contract_far[0], expand_far[-1])
    if helped:
        contract_far.append(beside(contract_far[0]))

    halves = 2
    part_rows = rows // halves
    wide = min(512, part_rows)
    chunk = min(256, part_rows)
    sub = part_rows // chunk
    down = lambda i: (i, 0)

    def output_part(j):
        base = j * part_rows // wide
        at = lambda i: (base + i, 0)
        return call(
            functools.partial(output_kernel, len(acts), sides),
            (part_rows // wide,),
            [(a, (wide, a.shape[1]), at) for a in acts]
            + [whole(w) for w in out_all]
            + [(tokens, (wide, width), at), whole(line(output_bias)), whole(line(mlp_norm_gain)), whole(line(mlp_norm_bias))],
            [((part_rows, width), F32, (wide, width), down), ((part_rows, width), BF16, (wide, width), down)],
            flops=2 * part_rows * width * width,
            moved=20 * part_rows * width,
            vmem=60,
            scratch=[
                pltpu.VMEM((sides, wide, width // sides), BF16),
                pltpu.VMEM((sides, width // sides, width), BF16),
            ]
            + [pltpu.VMEM((wide, width), F32)] * sides,
        )

    middles, seconds, others = [], [], []
    for j in range(halves):
        middle, normed_second = output_part(j)
        middles.append(middle)
        seconds.append(normed_second)
        others.append(near(normed_second))

    near_parts = [
        list(feed_near(
            chunk, j * part_rows, seconds[j], others[j], cotangent, cot_near, expand_weight, contract_weight, line(expand_bias)
        ))
        for j in range(halves)
    ]
    far_parts, far_sums, grads, sums_own = [], [], [], []
    for j in range(halves):
        kept = None
        for k in range(sub):
            far_bias = line(expand_bias_far)
            if sums_own:
                far_bias, sums_own[-1] = tie(far_bias, sums_own[-1])
            if len(grads) >= 3:
                far_bias, *grads[-3] = tie(far_bias, *grads[-3])
            (g_own, g_near), kept, bias_sum = feed_far(
                chunk,
                k,
                j * part_rows,
                seconds[j],
                others[j],
                cotangent,
                cot_near,
                expand_far,
                contract_far,
                far_bias,
                near_parts[j][2],
                near_parts[j][3],
                expand_weight,
                kept,
                parity,
            )
            far_sums.append(bias_sum[0])
            sums_own.append(add(g_own, near(g_near)))
            grads.append(None)
            for m in range(len(grads)):
                if grads[m] is None and m < len(sums_own) - 1:
                    grads[m] = list(heads_sum(sums_own[m]))
        far_parts.append(list(kept))

    grads[-1] = list(heads_sum(sums_own[-1]))

    hblk = min(512, hid)
    n_blk = hid // hblk

    def contract_grad(parts, at, count):
        lefts = [(p[n], (part_rows, hblk), lambda i: (0, at + i)) for n in range(2) for p in parts]
        rights = [(c, (part_rows, width), lambda i, j=j: (j, 0)) for c in (cotangent, cot_near) for j in range(halves)]
        return call(
            pair_grad_kernel,
            (count,),
            lefts + rights,
            [((count * hblk, width), BF16, (hblk, width), down)],
            flops=4 * 2 * rows * width * hblk * count,
            moved=8 * width * rows,
            vmem=56,
        )[0]

    def expand_grad(parts, at, count):
        lefts = [(x, (part_rows, hblk), lambda i: (0, at + i)) for x in seconds + others]
        rights = [whole(p[n]) for n in (2, 3) for p in parts]
        return call(
            pair_grad_kernel,
            (count,),
            lefts + rights,
            [((count * hblk, hid), BF16, (hblk, hid), down)],
            flops=4 * 2 * rows * hblk * hid * count,
            moved=8 * width * rows,
            vmem=56,
        )[0]

    far_parts[1][3], *grads[1] = tie(far_parts[1][3], *grads[1])
    contract_send = contract_grad(far_parts, 0, n_blk)
    contract_moved = far(contract_send)
    expand_send = expand_grad(far_parts, 0, width // hblk)
    near_parts[1][3], expand_send, *grads[2] = tie(near_parts[1][3], expand_send, *grads[2])
    contract_own = contract_grad(near_parts, 0, n_blk)
    expand_own = expand_grad(near_parts, 0, width // hblk)
    bias_near = near_parts[0][4][0] + near_parts[1][4][0]
    bias_far = functools.reduce(lambda u, v: u + v, far_sums)
    expand_send, contract_moved = tie(expand_send, contract_moved)
    expand_moved = far(expand_send)
    grads[0][0], contract_own, expand_own = tie(grads[0][0], contract_own, expand_own)

    gms, lows, keeps, sends, sums = [], [], [], [], []
    for j in range(halves):
        terms = grads[j * sub : (j + 1) * sub]
        at = lambda i, j=j: (j, 0)
        gm, low, keep, send, part = call(
            functools.partial(second_back_kernel, sub),
            (1,),
            [whole(t[0]) for t in terms]
            + [whole(t[1]) for t in terms]
            + [
                whole(middles[j]),
                (cotangent, (part_rows, width), at),
                whole(line(mlp_norm_gain)),
                whole(out_keep),
                whole(out_send),
            ],
            [
                ((part_rows, width), F32, (part_rows, width), lambda i: (0, 0)),
                ((part_rows, width), BF16, (part_rows, width), lambda i: (0, 0)),
                ((part_rows, cols), BF16, (part_rows, cols), lambda i: (0, 0)),
                ((part_rows, cols), BF16, (part_rows, cols), lambda i: (0, 0)),
                ((8, width), F32, (8, width), lambda i: (0, 0)),
            ],
            flops=4 * part_rows * width * cols,
            moved=16 * part_rows * width + 4 * width * cols,
            vmem=58,
        )
        gms.append(gm)
        lows.append(low)
        keeps.append(keep)
        sends.append(near(send))
        sums.append(part[:4])
    grad_middle = jnp.concatenate(gms)
    grad_a, grad_b = jnp.concatenate(keeps), jnp.concatenate(sends)
    mid_sums = functools.reduce(lambda u, v: u + v, sums)

    if n_heads == 2:
        query_late, lows[-1] = tie(query_keep, lows[-1])
        query_other = across(query_late)
        query_all = [query_keep, query_send, query_other, near(query_other)]
    else:
        query_all = heads_weights(query_keep, query_send, 1)

    grad_low = jnp.concatenate(lows)

    def dot_left(left, right):
        return dot_tn(left, right).astype(BF16)

    def chips_half(block):
        size = block.shape[0] // chips
        mine = lax.dynamic_slice_in_dim(block, chip * size, size, 0)
        other = lax.dynamic_slice_in_dim(block, (1 - chip) * size, size, 0)
        return mine, far(other)

    def all_blocks(total):
        pair = ordered(chip, total, far(total), 0)
        return pair, near(pair)

    contract_sum = add(contract_own, contract_moved)

    bq, bk, half, scalars = blocks_of(BACKWARD_BLOCK)

    def attn_backward(n, info):
        own, other, for_near, lse = attn[n]
        return call(
            functools.partial(attn_backward_kernel, part_heads, half, bk, scale, scale * LOG2E),
            (2 * half,),
            [
                (info, None, None),
                (query_a, (bq, part_cols), at_a(n, half)),
                (query_b, (bq, part_cols), at_b(n, half)),
                (grad_a, (bq, part_cols), at_a(n, half)),
                (grad_b, (bq, part_cols), at_b(n, half)),
                (own, (bq, part_cols), at_a(0, half)),
                (for_near, (bq, part_cols), at_b(0, half)),
                whole(kv_whole),
                (kv_turned, (dim, window), lambda i, *_: (0, 0)),
                (start_row, (1, bq), lambda i, *_: (0, i)),
                (lse, (part_heads, bq), lambda i, *_: (0, i)),
            ],
            [
                ((rows, part_cols), BF16, (bq, part_cols), at_a(0, half)),
                ((rows, part_cols), BF16, (bq, part_cols), at_b(0, half)),
                ((window, 2 * dim), F32, (window, 2 * dim), lambda i, *_: (0, 0)),
            ],
            scratch=[pltpu.VMEM((part_heads, dim, bq), F32)],
            prefetch=1,
            vmem=48,
            flops=pairs_guess,
            moved=rows,
        )

    own_all = jnp.concatenate([a[0] for a in attn], 1)
    other_all = jnp.concatenate([a[1] for a in attn], 1)
    out_half = add(*chips_half(add(dot_left(own_all, grad_low), near(dot_left(other_all, grad_low)))))
    expand_size = width // n_dp
    out_size = out_half.shape[0] * width // hid // n_dp
    joined = jnp.concatenate(
        [add(expand_own, expand_moved).reshape(n_dp, expand_size, hid), out_half.reshape(n_dp, out_size, hid)], 1
    )
    joined = joined.reshape(-1, hid)

    def feed_output(first_input):
        count = 2 * halves
        out_cols = min(512, width)
        blocks = [
            (p[n], (part_rows, size), lambda i, shift, k=k: (0, lax.rem(k + shift[0], pieces)))
            for n in range(2)
            for p in far_parts
            for k in range(pieces)
        ]
        return call(
            functools.partial(contract_kernel, count, pieces),
            (width // out_cols,),
            [(parity.reshape(1), None, None)]
            + [whole(p) for p in [first_input, near_parts[1][0], near_parts[0][1], near_parts[1][1]]]
            + blocks
            + [(v, (v.shape[0], out_cols), lambda i, *_: (0, i)) for v in [contract_weight] + contract_far],
            [((rows, width), BF16, (rows, out_cols), lambda i, *_: (0, i))] * 2,
            flops=rows,
            moved=rows,
            vmem=56,
            prefetch=1,
        )

    back_acts, dq_own, dq_other, dkv = [], [], [], None
    info = scalars[0]
    for n in range(calls):
        if n == 0:
            info, contract_sum = tie(info, contract_sum)
            contract_half = contract_sum.shape[0] // 2
            contract_first = lax.psum(contract_sum[:contract_half], "dp")
        own, for_near, dkv_part = attn_backward(n, info)
        if n == 0:
            mlp_start, dkv_part = tie(near_parts[0][0], dkv_part)
            mlp_own, mlp_near = feed_output(mlp_start)
            info, mlp_own, query_all[-2] = tie(info, mlp_own, query_all[-2])
        if n == calls - 1:
            for_near, contract_first = tie(for_near, contract_first)
            contract_rest, contract_first = tie(contract_sum[contract_half:], contract_first)
            contract_second = lax.psum(contract_rest, "dp")
            for_near, joined = tie(for_near, joined)
            expand_chain = Chain(joined)
            expand_chain.step()
        other = near(for_near)
        dq_own.append(own)
        dq_other.append(other)
        back_acts.append(jnp.concatenate([own, other], 1))
        if n == 0 and calls > 1:
            info, back_acts[0] = tie(info, back_acts[0])
        dkv = dkv_part if dkv is None else dkv + dkv_part
    back_acts = [a for act in back_acts for a in heads_acts(act)]

    dkv = dkv.reshape(chips, 2, rows, 2 * dim)

    def half_of(value, axis, bit):
        return lax.dynamic_index_in_dim(value, bit, axis, keepdims=False)

    core_sum = half_of(dkv, 1, core) + near(half_of(dkv, 1, 1 - core).astype(BF16)).astype(F32)
    chip_sum = add(half_of(core_sum, 0, chip), far(half_of(core_sum, 0, 1 - chip).astype(BF16)))
    first, second = heads_sum(chip_sum)
    grad_kv = add(first, second)

    kv_keep = lax.dynamic_slice_in_dim(grad_kv, core * dim, dim, 1)
    kv_send = lax.dynamic_slice_in_dim(grad_kv, (1 - core) * dim, dim, 1)
    query_sent = near(dot_left(normed_first, jnp.concatenate(dq_other + [kv_send], 1)))
    query_block = add(dot_left(normed_first, jnp.concatenate(dq_own + [kv_keep], 1)), query_sent)
    query_chain = Chain(add(*chips_half(query_block)))
    expand_chain.step()
    grad_kv, expand_chain.up, expand_chain.down = tie(grad_kv, expand_chain.up, expand_chain.down)
    input_grad, first_sums = call(
        functools.partial(first_back_kernel, len(back_acts), sides),
        (rows // wide,),
        [rows_of(a, wide) for a in back_acts]
        + [whole(w) for w in query_all]
        + [rows_of(grad_kv, wide), whole(key_value_weight)]
        + [rows_of(tokens, wide), rows_of(grad_middle, wide), whole(line(pre_norm_gain))],
        [((rows, width), BF16, (wide, width), down), ((8, width), F32, (8, width), lambda i: (0, 0))],
        flops=2 * rows * width * (width + 2 * dim),
        moved=20 * rows * width,
        vmem=60,
        scratch=[
            pltpu.VMEM((sides, wide, width // sides), BF16),
            pltpu.VMEM((sides, width, width // sides), BF16),
        ]
        + [pltpu.VMEM((wide, width), F32)] * sides,
    )

    mlp_sum, first_sums = tie(add(mlp_own, near(mlp_near)), first_sums)
    mlp_first, mlp_second = heads_sum(mlp_sum)
    mlp_total = mlp_first.astype(F32) + mlp_second.astype(F32)
    layer_output = (jnp.concatenate(middles) + mlp_total + contract_bias).astype(BF16)

    expand_chain.step()
    expand_chain.up, input_grad, contract_second = tie(expand_chain.up, input_grad, contract_second)
    contract_weight_grad = jnp.concatenate([contract_first, contract_second]).astype(F32)
    for k in range(3):
        if k == 2:
            expand_chain.up, contract_weight_grad = tie(expand_chain.up, contract_weight_grad)
        together([expand_chain, query_chain], [])
    joined = expand_chain.result().reshape(n_dp, -1, hid)
    expand_weight_grad = joined[:, :expand_size].reshape(width, hid).astype(F32)
    dq_bias_keep = jnp.concatenate([jnp.sum(v.astype(F32), 0) for v in dq_own])
    dq_bias_send = jnp.concatenate([jnp.sum(v.astype(F32), 0) for v in dq_other])
    query_bias_part = ordered(core, dq_bias_keep, dq_bias_send, 0)
    value_bias_part = jnp.sum(grad_kv[:, dim:].astype(F32), 0)

    places_of_units = jnp.arange(n_rows)[:, None]
    units = jnp.where(places_of_units == row_index, bias_near, 0.0) + jnp.where(
        places_of_units == jnp.bitwise_xor(row_index, 2), bias_far, 0.0
    )
    shorts = [mid_sums, first_sums[:2], query_bias_part, value_bias_part, units]
    short_sums = small_sum(jnp.concatenate([v.reshape(-1) for v in shorts]))
    query_chain.up, expand_weight_grad, layer_output, short_sums = tie(
        query_chain.up, expand_weight_grad, layer_output, short_sums
    )
    out_block, out_block_near = all_blocks(joined[:, expand_size:].reshape(out_half.shape))
    output_weight_grad = ordered(core, out_block, out_block_near, 0).astype(F32)
    query_block, query_block_near = all_blocks(query_chain.result())
    query_weight_grad, key_value_weight_grad = call(
        side_by_side_kernel,
        (width // min(512, width),),
        [
            (core.reshape(1), None, None),
            (query_block, (min(512, width), cols + dim), lambda i, *_: (i, 0)),
            (query_block_near, (min(512, width), cols + dim), lambda i, *_: (i, 0)),
        ],
        [
            ((width, 2 * cols), F32, (min(512, width), 2 * cols), lambda i, *_: (i, 0)),
            ((width, 2 * dim), F32, (min(512, width), 2 * dim), lambda i, *_: (i, 0)),
        ],
        prefetch=1,
        moved=12 * width * (cols + dim),
    )

    short_totals, at = [], 0
    for v in shorts:
        short_totals.append(short_sums[at : at + v.size].reshape(v.shape))
        at += v.size
    mid_total, first_total, query_bias_grad, value_bias_grad, units = short_totals
    expand_bias_grad = lax.dynamic_index_in_dim(units, row_index, 0, keepdims=False)
    return (
        layer_output,
        input_grad,
        first_total[0],
        first_total[1],
        query_weight_grad,
        query_bias_grad,
        key_value_weight_grad,
        value_bias_grad,
        output_weight_grad,
        mid_total[2],
        mid_total[0],
        mid_total[1],
        expand_weight_grad,
        expand_bias_grad,
        contract_weight_grad,
        mid_total[3],
    )


def solution(mesh):
    both = P(("heads", "rows"))
    in_specs = (
        P(("dp", "rows"), None),
        P("dp", None),
        P(),
        P(),
        P(None, "heads"),
        P("heads"),
        P(),
        P(),
        P("heads", None),
        P(),
        P(),
        P(),
        P(None, ("heads", "rows")),
        both,
        P(("heads", "rows"), None),
        P(),
        P(("dp", "rows"), None),
    )
    out_specs = (
        P(("dp", "rows"), None),
        P(("dp", "rows"), None),
        P(),
        P(),
        P(None, "heads"),
        P("heads"),
        P(),
        P(),
        P("heads", None),
        P(),
        P(),
        P(),
        P(None, ("heads", "rows")),
        both,
        P(("heads", "rows"), None),
        P(),
    )
    return jax.shard_map(body, mesh=mesh, in_specs=in_specs, out_specs=out_specs, check_vma=False)
```

```python
import functools
import math

import jax
import jax.numpy as jnp
from jax import lax
from jax.experimental import pallas as pl
from jax.experimental.pallas import tpu as pltpu
from jax.sharding import PartitionSpec as P

NORM_EPSILON = 1e-05
FAR = -1e30
LOG2E = 1.4426950408889634
GELU_A = math.sqrt(2.0 / math.pi)
GELU_B = 0.044715
F32 = jnp.float32
BF16 = jnp.bfloat16
MIB = 1024 * 1024
FORWARD_BLOCK = (512, 1024)
BACKWARD_BLOCK = (256, 1024)


def dot(left, right):
    return jnp.dot(left, right, preferred_element_type=F32)


def dot_tn(left, right):
    return lax.dot_general(left, right, (((0,), (0,)), ((), ())), preferred_element_type=F32)


def dot_nt(left, right):
    return lax.dot_general(left, right, (((1,), (1,)), ((), ())), preferred_element_type=F32)


def call(kernel, grid, ins, outs, scratch=(), prefetch=0, vmem=48, flops=0, moved=0, alias=None):
    arrays = [a for a, _, _ in ins[prefetch:]]
    specs = [
        pl.BlockSpec(b, m, pipeline_mode=pl.Buffered(1)) if b == a.shape else pl.BlockSpec(b, m) for a, b, m in ins[prefetch:]
    ]
    scalars = [a for a, _, _ in ins[:prefetch]]
    return pl.pallas_call(
        kernel,
        grid_spec=pltpu.PrefetchScalarGridSpec(
            num_scalar_prefetch=prefetch,
            grid=grid,
            in_specs=specs,
            out_specs=[pl.BlockSpec(b, m) for _, _, b, m in outs],
            scratch_shapes=list(scratch),
        ),
        out_shape=[jax.ShapeDtypeStruct(s, d) for s, d, _, _ in outs],
        compiler_params=pltpu.CompilerParams(vmem_limit_bytes=vmem * MIB),
        cost_estimate=pl.CostEstimate(flops=int(flops), bytes_accessed=int(moved), transcendentals=0),
        input_output_aliases=alias or {},
    )(*scalars, *arrays)


def whole(array):
    zeros = (0,) * array.ndim
    return (array, array.shape, lambda *_: zeros)


def rows_of(array, block):
    return (array, (block, array.shape[1]), lambda i, *_: (i, 0))


def normed(values, gain, bias):
    mean = jnp.mean(values, -1, keepdims=True)
    centred = values - mean
    var = jnp.mean(centred * centred, -1, keepdims=True)
    return centred * lax.rsqrt(var + NORM_EPSILON) * gain + bias


def norm_back(values, grad, gain):
    mean = jnp.mean(values, -1, keepdims=True)
    centred = values - mean
    var = jnp.mean(centred * centred, -1, keepdims=True)
    inverse = lax.rsqrt(var + NORM_EPSILON)
    xhat = centred * inverse
    g = grad * gain
    g_mean = jnp.mean(g, -1, keepdims=True)
    gx_mean = jnp.mean(g * xhat, -1, keepdims=True)
    return xhat, (g - g_mean - xhat * gx_mean) * inverse


def norm_kv_kernel(t_ref, g_ref, b_ref, w_ref, wb_ref, n_ref, kv_ref):
    low = normed(t_ref[...].astype(F32), g_ref[...], b_ref[...]).astype(BF16)
    n_ref[...] = low
    kv_ref[...] = (dot(low, w_ref[...]) + wb_ref[...]).astype(BF16)


def project_kernel(core, n_ref, wa_ref, ba_ref, wb_ref, bb_ref, a_ref, b_ref):
    low = n_ref[...]
    b_ref[...] = (dot(low, wb_ref[...]) + bb_ref[...]).astype(BF16)
    a_ref[...] = (dot(low, wa_ref[...]) + ba_ref[...]).astype(BF16)


def attn_forward_kernel(heads, half, bk, scale2, info, qa_ref, qb_ref, kv_ref, vt_ref, st_ref, oa_ref, ob_ref, lse_ref, m_ref, l_ref, acc_ref):
    i = pl.program_id(0)
    first, low, high, clear_from, clear_to = (info[n, i] for n in range(5))
    bq, dim = qa_ref.shape[0], kv_ref.shape[1] // 2
    in_a = i < half
    start = st_ref[...]
    place = first + lax.broadcasted_iota(jnp.int32, (1, bq), 1)
    queries = jnp.where(in_a, qa_ref[...], qb_ref[...])
    m_ref[...] = jnp.full_like(m_ref, FAR)
    l_ref[...] = jnp.zeros_like(l_ref)
    acc_ref[...] = jnp.zeros_like(acc_ref)

    def step(block, masked):
        begin = pl.multiple_of(block * bk, bk)
        keys = kv_ref[pl.ds(begin, bk), :dim]
        values = vt_ref[:, pl.ds(begin, bk)]
        if masked:
            key_place = begin + lax.broadcasted_iota(jnp.int32, (bk, 1), 0)
            allowed = (key_place >= start) & (key_place <= place)
        for h in range(heads):
            s = dot_nt(keys, queries[:, h * dim : (h + 1) * dim])
            if masked:
                s = jnp.where(allowed, s, FAR)
            old = m_ref[h : h + 1, :]
            new = jnp.maximum(old, jnp.max(s, 0, keepdims=True) * scale2)
            p = jnp.exp2(s * scale2 - new)
            fix = jnp.exp2(old - new)
            l_ref[h : h + 1, :] = l_ref[h : h + 1, :] * fix + jnp.sum(p, 0, keepdims=True)
            m_ref[h : h + 1, :] = new
            acc_ref[h] = acc_ref[h] * fix + dot(values, p.astype(BF16))

    def body(block, carry):
        clear = (block >= clear_from) & (block < clear_to)

        @pl.when(clear)
        def _():
            step(block, False)

        @pl.when(jnp.logical_not(clear))
        def _():
            step(block, True)

        return carry

    lax.fori_loop(low, high, body, 0)
    outs = []
    for h in range(heads):
        total = l_ref[h : h + 1, :]
        outs.append((acc_ref[h] / total).T.astype(BF16))
    lse_ref[...] = m_ref[...] + jnp.log2(l_ref[...])

    @pl.when(in_a)
    def _():
        for h in range(heads):
            oa_ref[:, h * dim : (h + 1) * dim] = outs[h]

    @pl.when(jnp.logical_not(in_a))
    def _():
        for h in range(heads):
            ob_ref[:, h * dim : (h + 1) * dim] = outs[h]


def attn_backward_kernel(
    heads, half, bk, scale, scale2, info, qa_ref, qb_ref, ga_ref, gb_ref, oa_ref, ob_ref, kv_ref, kt_ref, st_ref, lse_ref, dqa_ref, dqb_ref, dkv_ref, dq_ref
):
    i = pl.program_id(0)
    first, low, high, clear_from, clear_to = (info[n, i] for n in range(5))
    bq, dim = qa_ref.shape[0], kv_ref.shape[1] // 2
    in_a = i < half

    @pl.when(i == 0)
    def _():
        dkv_ref[...] = jnp.zeros_like(dkv_ref)

    start = st_ref[...]
    place = first + lax.broadcasted_iota(jnp.int32, (1, bq), 1)
    queries = jnp.where(in_a, qa_ref[...], qb_ref[...])
    grads = jnp.where(in_a, ga_ref[...], gb_ref[...])
    outs = jnp.where(in_a, oa_ref[...], ob_ref[...])
    inner, lse = [], []
    for h in range(heads):
        cut = slice(h * dim, (h + 1) * dim)
        product = grads[:, cut].astype(F32) * outs[:, cut].astype(F32)
        inner.append(jnp.sum(product.T, 0, keepdims=True))
        lse.append(lse_ref[h : h + 1, :])
    dq_ref[...] = jnp.zeros_like(dq_ref)

    def step(block, masked):
        begin = pl.multiple_of(block * bk, bk)
        keys = kv_ref[pl.ds(begin, bk), :dim]
        values = kv_ref[pl.ds(begin, bk), dim:]
        keys_t = kt_ref[:, pl.ds(begin, bk)]
        if masked:
            key_place = begin + lax.broadcasted_iota(jnp.int32, (bk, 1), 0)
            allowed = (key_place >= start) & (key_place <= place)
        dk = None
        for h in range(heads):
            cut = slice(h * dim, (h + 1) * dim)
            s = dot_nt(keys, queries[:, cut])
            dp = dot_nt(values, grads[:, cut])
            p = jnp.exp2(s * scale2 - lse[h])
            if masked:
                p = jnp.where(allowed, p, 0.0)
            ds = (p * (dp - inner[h])).astype(BF16)
            dv_part = dot(p.astype(BF16), grads[:, cut])
            dk_part = dot(ds, queries[:, cut])
            dk, dv = (dk_part, dv_part) if dk is None else (dk + dk_part, dv + dv_part)
            dq_ref[h] += dot(keys_t, ds)
        dkv_ref[pl.ds(begin, bk), :dim] += dk * scale
        dkv_ref[pl.ds(begin, bk), dim:] += dv

    def body(block, carry):
        clear = (block >= clear_from) & (block < clear_to)

        @pl.when(clear)
        def _():
            step(block, False)

        @pl.when(jnp.logical_not(clear))
        def _():
            step(block, True)

        return carry

    lax.fori_loop(low, high, body, 0)

    def leave(ref):
        for h in range(heads):
            ref[:, h * dim : (h + 1) * dim] = (dq_ref[h] * scale).T.astype(BF16)

    @pl.when(in_a)
    def _():
        leave(dqa_ref)

    @pl.when(jnp.logical_not(in_a))
    def _():
        leave(dqb_ref)


def balanced(acts, weights, product, by_rows, scratch):
    act_ref, weight_ref, sums = scratch[0], scratch[1], scratch[2:]
    sides = len(sums)
    calls = len(acts) // sides
    cols = acts[0].shape[1] // 2
    for n in range(sides):

        @pl.when(pl.program_id(0) == 0)
        def _():
            keep, send = weights[2 * n], weights[2 * n + 1]
            if by_rows:
                size = keep.shape[0]
                weight_ref[n, :size, :] = keep[...]
                weight_ref[n, size:, :] = send[...]
            else:
                size = keep.shape[1]
                weight_ref[n, :, :size] = keep[...]
                weight_ref[n, :, size:] = send[...]

        for k in range(calls):
            act = acts[k * sides + n]
            act_ref[n, :, k * cols : (k + 1) * cols] = act[:, :cols]
            act_ref[n, :, (calls + k) * cols : (calls + k + 1) * cols] = act[:, cols:]
        sums[n][...] = product(act_ref[n], weight_ref[n])
    return functools.reduce(lambda u, v: u + v, [r[...] for r in sums])


def output_kernel(count, sides, *refs):
    acts, weights = refs[:count], refs[count : count + 2 * sides]
    t_ref, ob_ref, g_ref, b_ref, mid_ref, n_ref, *scratch = refs[count + 2 * sides :]
    near = balanced(acts, weights, dot, True, scratch)
    middle = t_ref[...].astype(F32) + near + ob_ref[...]
    mid_ref[...] = middle
    n_ref[...] = normed(middle, g_ref[...], b_ref[...]).astype(BF16)


def feed_tile(x, c, w, v, bias):
    before = dot(x, w) + bias
    grad = dot_nt(c, v)
    square = before * before
    t = jnp.tanh(before * (GELU_A + (GELU_A * GELU_B) * square))
    half = 0.5 + 0.5 * t
    slope = half + before * (half * (1.0 - t)) * (GELU_A + (3.0 * GELU_A * GELU_B) * square)
    return (before * half).astype(BF16), grad * slope


def stack(scratch, first, second):
    rows = first.shape[0]
    scratch[:rows, :] = first[...]
    scratch[rows:, :] = second[...]


def add_to(ref, value, fresh):
    @pl.when(fresh)
    def _():
        ref[...] = jnp.zeros_like(ref)

    ref[...] += jnp.broadcast_to(value, ref.shape)


def feed_near_kernel(blk, xa_ref, xb_ref, ca_ref, cb_ref, w_ref, v_ref, b_ref, ha_ref, hb_ref, da_ref, db_ref, sum_ref, x_ref, c_ref):
    rows = xa_ref.shape[0]
    stack(x_ref, xa_ref, xb_ref)
    stack(c_ref, ca_ref, cb_ref)
    sums = []
    for at in range(0, w_ref.shape[1], blk):
        cut = slice(at, at + blk)
        hidden, grad = feed_tile(x_ref[...], c_ref[...], w_ref[:, cut], v_ref[cut, :], b_ref[:, cut])
        low = grad.astype(BF16)
        ha_ref[:, cut] = hidden[:rows]
        hb_ref[:, cut] = hidden[rows:]
        da_ref[:, cut] = low[:rows]
        db_ref[:, cut] = low[rows:]
        sums.append(jnp.sum(grad, 0, keepdims=True))
    add_to(sum_ref, jnp.concatenate(sums, 1), pl.program_id(0) == 0)


def feed_far_kernel(steps, back, order, xa_ref, xb_ref, ca_ref, cb_ref, b_ref, ea_ref, eb_ref, u_ref, *rest):
    w_refs, z_refs, v_refs = rest[:steps], rest[steps : 2 * steps], rest[2 * steps : 3 * steps]
    ga_ref, gb_ref, ha_ref, hb_ref, da_ref, db_ref, sum_ref, x_ref, c_ref, e_ref, low_ref = rest[-11:]
    i = lax.rem(pl.program_id(0), steps + back)
    rows = xa_ref.shape[0]

    @pl.when(i == 0)
    def _():
        stack(x_ref, xa_ref, xb_ref)
        stack(c_ref, ca_ref, cb_ref)
        stack(e_ref, ea_ref, eb_ref)

    for k in range(steps):

        @pl.when(i == k)
        def _():
            hidden, grad = feed_tile(x_ref[...], c_ref[...], w_refs[k][...], v_refs[k][...], b_ref[...])
            low = grad.astype(BF16)
            ha_ref[...] = hidden[:rows]
            hb_ref[...] = hidden[rows:]
            da_ref[...] = low[:rows]
            db_ref[...] = low[rows:]
            low_ref[k] = low
            sum_ref[...] = jnp.broadcast_to(jnp.sum(grad, 0, keepdims=True), sum_ref.shape)

    @pl.when(i >= steps)
    def _():
        total = dot_nt(e_ref[...], u_ref[...])
        for k in range(steps):
            total = total + dot_nt(low_ref[k], z_refs[k][...])
        ga_ref[...] = total[:rows].astype(BF16)
        gb_ref[...] = total[rows:].astype(BF16)


def feed_near(chunk, first_row, x_own, x_other, c_own, c_other, w, v, bias):
    rows, width = x_own.shape
    hid = w.shape[1]
    base = first_row // chunk
    at = lambda i: (i, 0)
    at_all = lambda i: (base + i, 0)
    return call(
        functools.partial(feed_near_kernel, min(512, hid)),
        (rows // chunk,),
        [
            (x_own, (chunk, width), at),
            (x_other, (chunk, width), at),
            (c_own, (chunk, width), at_all),
            (c_other, (chunk, width), at_all),
            whole(w),
            whole(v),
            whole(bias),
        ],
        [((rows, hid), BF16, (chunk, hid), at)] * 4 + [((8, hid), F32, (8, hid), lambda i: (0, 0))],
        scratch=[pltpu.VMEM((2 * chunk, width), BF16)] * 2,
        vmem=56,
        flops=8 * rows * width * hid,
        moved=8 * width * hid + 8 * rows * width,
    )


def feed_far(chunk, first_row, x_own, x_other, c_own, c_other, w, v, bias, near_own, near_other, w_near, parity):
    rows, width = x_own.shape
    hid = w_near.shape[1]
    steps = len(w)
    blk = hid // steps
    out_blk = min(512, width)
    back = width // out_blk
    per = steps + back
    count = rows // chunk
    base = first_row // chunk
    at = lambda i, p: (i // per, 0)
    at_all = lambda i, p: (base + i // per, 0)
    tile = lambda i, p: lax.rem(jnp.minimum(lax.rem(i, per), steps - 1) + p[0], steps)
    after = lambda i: jnp.maximum(lax.rem(i, per) - steps, 0)
    ins = [
        (parity.reshape(1), None, None),
        (x_own, (chunk, width), at),
        (x_other, (chunk, width), at),
        (c_own, (chunk, width), at_all),
        (c_other, (chunk, width), at_all),
        (bias, (1, blk), lambda i, p: (0, tile(i, p))),
        (near_own, (chunk, hid), at),
        (near_other, (chunk, hid), at),
        (w_near, (out_blk, hid), lambda i, p: (after(i), 0)),
    ]
    ins += [whole(p) for p in w]
    ins += [(u, (out_blk, blk), lambda i, p: (after(i), 0)) for u in w]
    ins += [whole(p) for p in v]
    outs = [((rows, width), BF16, (chunk, out_blk), lambda i, p: (i // per, after(i)))] * 2
    outs += [((rows, hid), BF16, (chunk, blk), lambda i, p: (i // per, tile(i, p)))] * 4
    outs += [((8 * count, hid), F32, (8, blk), lambda i, p: (i // per, tile(i, p)))]
    result = call(
        functools.partial(feed_far_kernel, steps, back),
        (count * per,),
        ins,
        outs,
        scratch=[
            pltpu.VMEM((2 * chunk, width), BF16),
            pltpu.VMEM((2 * chunk, width), BF16),
            pltpu.VMEM((2 * chunk, hid), BF16),
            pltpu.VMEM((steps, 2 * chunk, blk), BF16),
        ],
        prefetch=1,
        vmem=56,
        flops=rows,
        moved=rows,
    )
    return result[:2], result[2:6], jnp.sum(result[6].reshape(count, 8, hid)[:, 0], 0)


def contract_kernel(count, pieces, parity, *refs):
    near, far = refs[:count], refs[count : count + count * pieces]
    va_ref, *vb_refs = refs[count + count * pieces : count + count * pieces + pieces + 1]
    own_ref, other_ref = refs[-2:]
    size = near[0].shape[0]
    for k in range(count):
        y_ref = own_ref if k < count // 2 else other_ref
        at = k % (count // 2) * size
        total = dot(near[k][...], va_ref[...])
        for n in range(pieces):
            total = total + dot(far[k * pieces + n][...], vb_refs[n][...])
        y_ref[at : at + size, :] = total.astype(BF16)


def pair_grad_kernel(*refs):
    out_ref = refs[-1]
    count = (len(refs) - 1) // 2
    total = None
    for left, right in zip(refs[:count], refs[count:-1]):
        piece = dot_tn(left[...], right[...])
        total = piece if total is None else total + piece
    out_ref[...] = total.astype(BF16)


def second_back_kernel(count, *refs):
    firsts, seconds = refs[:count], refs[count : 2 * count]
    mid_ref, cot_ref, gain_ref, wk_ref, ws_ref, gm_ref, low_ref, keep_ref, send_ref, sums_ref = refs[2 * count :]
    size = firsts[0].shape[0]
    totals = [0.0, 0.0, 0.0, 0.0]
    for k in range(count):
        at = slice(k * size, (k + 1) * size)
        grad = firsts[k][...].astype(F32) + seconds[k][...].astype(F32)
        xhat, back = norm_back(mid_ref[at, :], grad, gain_ref[...])
        cot = cot_ref[at, :].astype(F32)
        total = cot + back
        gm_ref[at, :] = total
        low_ref[at, :] = total.astype(BF16)
        for n, value in enumerate((grad * xhat, grad, total, cot)):
            totals[n] = totals[n] + jnp.sum(value, 0, keepdims=True)
    send_ref[...] = dot_nt(low_ref[...], ws_ref[...]).astype(BF16)
    keep_ref[...] = dot_nt(low_ref[...], wk_ref[...]).astype(BF16)
    for n in range(4):
        sums_ref[n : n + 1, :] = totals[n]


def first_back_kernel(count, sides, *refs):
    acts, weights = refs[:count], refs[count : count + 2 * sides]
    kv_ref, kvw_ref, t_ref, gm_ref, gain_ref, out_ref, sums_ref, *scratch = refs[count + 2 * sides :]
    grad = balanced(acts, weights, dot_nt, False, scratch) + dot_nt(kv_ref[...], kvw_ref[...])
    xhat, back = norm_back(t_ref[...].astype(F32), grad, gain_ref[...])
    out_ref[...] = (gm_ref[...] + back).astype(BF16)

    @pl.when(pl.program_id(0) == 0)
    def _():
        sums_ref[...] = jnp.zeros_like(sums_ref)

    sums_ref[0:1, :] += jnp.sum(grad * xhat, 0, keepdims=True)
    sums_ref[1:2, :] += jnp.sum(grad, 0, keepdims=True)


def side_by_side_kernel(core, mine_ref, near_ref, query_ref, kv_ref):
    first = core[0] == 0
    mine, near = mine_ref[...].astype(F32), near_ref[...].astype(F32)
    cols = query_ref.shape[1] // 2
    left, right = jnp.where(first, mine, near), jnp.where(first, near, mine)
    query_ref[:, :cols] = left[:, :cols]
    query_ref[:, cols:] = right[:, :cols]
    kv_ref[:, : kv_ref.shape[1] // 2] = left[:, cols:]
    kv_ref[:, kv_ref.shape[1] // 2 :] = right[:, cols:]


def body(
    tokens,
    segment_lengths,
    pre_norm_gain,
    pre_norm_bias,
    query_weight,
    query_bias,
    key_value_weight,
    value_bias,
    output_weight,
    output_bias,
    mlp_norm_gain,
    mlp_norm_bias,
    expand_weight,
    expand_bias,
    contract_weight,
    contract_bias,
    cotangent,
):
    rows, width = tokens.shape
    n_heads, n_rows, n_dp = (lax.axis_size(a) for a in ("heads", "rows", "dp"))
    row_index = lax.axis_index("rows")
    core = lax.rem(row_index, 2)
    dim = key_value_weight.shape[1] // 2
    local_heads = query_weight.shape[1] // dim
    group = local_heads // 2
    cols = group * dim
    window = rows * n_rows
    scale = 1.0 / math.sqrt(dim)
    hid = expand_weight.shape[1]

    chips = n_rows // 2
    chip = row_index // 2
    dp_index = lax.axis_index("dp")

    def near(value):
        return lax.ppermute(value, "rows", [(i, i ^ 1) for i in range(n_rows)])

    def far(value):
        return lax.ppermute(value, "rows", [(i, i ^ 2) for i in range(n_rows)])

    def across(value):
        return lax.ppermute(value, "heads", [(0, 1), (1, 0)])

    def beside(value):
        return lax.ppermute(value, "dp", [(i, i ^ 1) for i in range(n_dp)])

    def line(vector):
        return vector.reshape(1, -1)

    def tie(*values):
        return lax.optimization_barrier(values)

    def add(*terms):
        return functools.reduce(lambda u, v: u + v, (t.astype(F32) for t in terms)).astype(BF16)

    def ordered(bit, mine, other, axis):
        return jnp.where(bit == 0, jnp.concatenate([mine, other], axis), jnp.concatenate([other, mine], axis))

    def heads_sum(value):
        if n_heads == 2:
            return value, across(value)
        total = lax.psum(value.astype(F32), "heads")
        high = total.astype(BF16)
        return high, (total - high.astype(F32)).astype(BF16)

    last = n_dp - 1

    class Chain:
        def __init__(self, value):
            self.value, self.size = value, value.shape[0] // n_dp
            self.up = self.down = self.out = None
            self.t = 0

        def prepare(self):
            self.out = jnp.zeros(((3 * n_dp - 2) * self.size,) + self.value.shape[1:], BF16)

        def piece(self, index):
            return lax.dynamic_slice_in_dim(self.value, jnp.clip(index, 0, last) * self.size, self.size, 0)

        def put(self, part, place):
            self.out = lax.dynamic_update_slice_in_dim(self.out, part, (place + last) * self.size, 0)

        def step(self):
            t, self.t = self.t, self.t + 1
            if t < last:
                up, down = self.piece(last + dp_index - t), self.piece(dp_index - last + t)
                if t > 0:
                    up, down = add(up, self.up), add(down, self.down)
                ends = range(t + 1)
            else:
                if t == last:
                    own = add(self.piece(dp_index), self.up, self.down)
                    if self.out is None:
                        self.prepare()
                    self.put(own, dp_index)
                    up = down = own
                else:
                    up, down = self.up, self.down
                ends = range(t - last, last)
            self.up = lax.ppermute(up, "dp", [(i, i + 1) for i in ends])
            self.down = lax.ppermute(down, "dp", [(last - i, last - i - 1) for i in ends])
            if t >= last:
                self.put(self.up, dp_index - 1 - (t - last))
                self.put(self.down, dp_index + 1 + (t - last))

        def result(self):
            while self.t < 2 * last:
                self.step()
            return self.out[last * self.size : (last + n_dp) * self.size]

    def together(chains, behind):
        for chain, values in zip(chains + behind, held(chains + behind)):
            if chain.t == 0:
                (chain.value,) = values
            else:
                chain.up, chain.down = values
        for chain in chains:
            chain.step()

    def held(chains):
        flat = [v for c in chains for v in ([c.value] if c.t == 0 else [c.up, c.down])]
        flat = list(tie(*flat))
        return [[flat.pop(0) for _ in range(1 if c.t == 0 else 2)] for c in chains]

    def landed(chains, *values):
        for chain in chains:
            chain.up, chain.down, *values = tie(chain.up, chain.down, *values)
        return values

    hops = [(axis, size, 1 << k) for axis, size in (("rows", n_rows), ("dp", n_dp)) for k in range(size.bit_length() - 1)]

    def hop_sum(value):
        if not hops:
            return value
        axis, size, hop = hops.pop(0)
        return value + lax.ppermute(value, axis, [(i, i ^ hop) for i in range(size)])

    keep_at, send_at = core * cols, (1 - core) * cols
    query_keep = lax.dynamic_slice_in_dim(query_weight, keep_at, cols, 1)
    query_send = lax.dynamic_slice_in_dim(query_weight, send_at, cols, 1)

    sides = 2 if n_heads == 2 else 1
    other_head = 1 - lax.axis_index("heads")

    def heads_acts(value):
        if n_heads == 2:
            return [value, across(value)]
        size = value.shape[1] // 2
        return [
            jnp.concatenate([lax.all_gather(v, "heads", axis=1, tiled=True) for v in (value[:, :size], value[:, size:])], 1)
        ]

    def heads_weights(keep, send, axis):
        whole_keep = lax.all_gather(keep, "heads", axis=axis, tiled=True)
        if n_heads > 2:
            return [whole_keep, near(whole_keep)]
        other = lax.dynamic_slice_in_dim(whole_keep, other_head * keep.shape[axis], keep.shape[axis], axis)
        return [keep, send, other, near(other)]

    expand_bias_far = far(expand_bias)
    cot_near = near(cotangent)

    blk = min(256, rows)
    grid = (rows // blk,)
    kv_bias = jnp.concatenate([jnp.zeros((dim,), F32), value_bias])
    normed_first, key_value = call(
        norm_kv_kernel,
        grid,
        [rows_of(tokens, blk), whole(line(pre_norm_gain)), whole(line(pre_norm_bias)), whole(key_value_weight), whole(line(kv_bias))],
        [
            ((rows, width), BF16, (blk, width), lambda i: (i, 0)),
            ((rows, 2 * dim), BF16, (blk, 2 * dim), lambda i: (i, 0)),
        ],
        flops=4 * rows * width * dim,
        moved=4 * rows * width,
    )
    output_weight, key_value = tie(output_weight, key_value)
    out_keep = lax.dynamic_slice_in_dim(output_weight, keep_at, cols, 0)
    out_send = lax.dynamic_slice_in_dim(output_weight, send_at, cols, 0)
    far_kv = far(key_value)
    near_kv = near(key_value)
    far_kv, expand_start, contract_start = tie(far_kv, expand_weight, contract_weight)
    pieces = hid // min(512, hid)
    size = hid // pieces
    helped = pieces == 2 and n_dp % 2 == 0
    parity = lax.rem(dp_index, 2) if helped else jnp.int32(0)
    if helped:
        expand_far = [far(lax.dynamic_slice_in_dim(expand_start, parity * size, size, 1))]
    else:
        expand_far = [far(expand_start[:, k * size : (k + 1) * size]) for k in range(pieces)]
    contract_start, expand_far[0] = tie(contract_start, expand_far[0])
    if helped:
        contract_far = [far(lax.dynamic_slice_in_dim(contract_start, parity * size, size, 0))]
    else:
        contract_far = [far(contract_start[k * size : (k + 1) * size]) for k in range(pieces)]
    pair_kv = ordered(core, key_value, near_kv, 0)
    far_pair = ordered(core, far_kv, near(far_kv), 0)
    kv_whole = ordered(chip, pair_kv, far_pair, 0)
    kv_turned = kv_whole.T

    query_a, query_for_near = call(
        project_kernel,
        grid,
        [
            (core.reshape(1), None, None),
            rows_of(normed_first, blk),
            (query_weight, (width, cols), lambda i, core: (0, core[0])),
            (line(query_bias), (1, cols), lambda i, core: (0, core[0])),
            (query_weight, (width, cols), lambda i, core: (0, 1 - core[0])),
            (line(query_bias), (1, cols), lambda i, core: (0, 1 - core[0])),
        ],
        [((rows, cols), BF16, (blk, cols), lambda i, *_: (i, 0))] * 2,
        prefetch=1,
        flops=4 * rows * width * cols,
        moved=2 * rows * width,
    )
    query_b = near(query_for_near)

    ends = jnp.cumsum(segment_lengths[0])
    own_place = row_index * rows
    near_place = (row_index + 1 - 2 * core) * rows
    steps = jnp.arange(rows, dtype=jnp.int32)
    places = jnp.concatenate([own_place + steps, near_place + steps])
    starts = jnp.max(jnp.where(ends[None, :] <= places[:, None], ends[None, :], 0), 1).astype(jnp.int32)

    def blocks_of(block):
        bq, bk = min(block[0], rows), min(block[1], window)
        first = places.reshape(-1, bq)[:, 0]
        start = starts.reshape(-1, bq)
        info = [first, start[:, 0] // bk, (first + bq - 1) // bk + 1, (start[:, -1] + bk - 1) // bk, (first + 1) // bk]
        return bq, bk, rows // bq, (jnp.stack(info).astype(jnp.int32), None, None)

    start_row = starts.reshape(1, -1)
    calls = 2 if group % 2 == 0 else 1
    part_heads = group // calls
    part_cols = part_heads * dim
    pairs_guess = 2 * rows * window // 4
    bq, bk, half, scalars = blocks_of(FORWARD_BLOCK)

    def at_a(n, half):
        return lambda i, *_: (jnp.minimum(i, half - 1), n)

    def at_b(n, half):
        return lambda i, *_: (jnp.maximum(i - half, 0), n)

    def attn_forward(n, info):
        return call(
            functools.partial(attn_forward_kernel, part_heads, half, bk, scale * LOG2E),
            (2 * half,),
            [
                (info, None, None),
                (query_a, (bq, part_cols), at_a(n, half)),
                (query_b, (bq, part_cols), at_b(n, half)),
                whole(kv_whole),
                (kv_turned, (dim, window), lambda i, *_: (1, 0)),
                (start_row, (1, bq), lambda i, *_: (0, i)),
            ],
            [
                ((rows, part_cols), BF16, (bq, part_cols), at_a(0, half)),
                ((rows, part_cols), BF16, (bq, part_cols), at_b(0, half)),
                ((part_heads, 2 * rows), F32, (part_heads, bq), lambda i, *_: (0, i)),
            ],
            scratch=[pltpu.VMEM((part_heads, bq), F32), pltpu.VMEM((part_heads, bq), F32), pltpu.VMEM((part_heads, dim, bq), F32)],
            prefetch=1,
            vmem=40,
            flops=16 * pairs_guess * part_cols,
            moved=8 * rows * part_cols,
        )

    attn, acts = [], []
    if n_heads == 2:
        out_other = across(out_keep)
    else:
        out_all = heads_weights(out_keep, out_send, 0)
    info = scalars[0]
    for n in range(calls):
        if n == 1:
            if n_heads == 2:
                info, out_other = tie(info, out_other)
            info, expand_far[0] = tie(info, expand_far[0])
        own, for_near, lse = attn_forward(n, info)
        if n == 1:
            own, for_near, acts[0][-1] = tie(own, for_near, acts[0][-1])
        other = near(for_near)
        attn.append((own, other, for_near, lse))
        act = jnp.concatenate([own, other], 1)
        if n == 0 and calls > 1:
            info, act, cot_near = tie(info, act, cot_near)
        acts.append(heads_acts(act))
    acts = [a for act in acts for a in act]
    if n_heads == 2:
        out_all = [out_keep, out_send, out_other, near(out_other)]
    if helped:
        expand_far.append(beside(expand_far[0]))
    acts[-1], contract_far[0], expand_far[-1] = tie(acts[-1], contract_far[0], expand_far[-1])
    if helped:
        contract_far.append(beside(contract_far[0]))

    halves = 2
    part_rows = rows // halves
    wide = min(512, part_rows)
    chunk = min(256, part_rows)
    sub = part_rows // chunk
    down = lambda i: (i, 0)

    def output_part(j):
        base = j * part_rows // wide
        at = lambda i: (base + i, 0)
        return call(
            functools.partial(output_kernel, len(acts), sides),
            (part_rows // wide,),
            [(a, (wide, a.shape[1]), at) for a in acts]
            + [whole(w) for w in out_all]
            + [(tokens, (wide, width), at), whole(line(output_bias)), whole(line(mlp_norm_gain)), whole(line(mlp_norm_bias))],
            [((part_rows, width), F32, (wide, width), down), ((part_rows, width), BF16, (wide, width), down)],
            flops=2 * part_rows * width * width,
            moved=20 * part_rows * width,
            vmem=60,
            scratch=[
                pltpu.VMEM((sides, wide, width // sides), BF16),
                pltpu.VMEM((sides, width // sides, width), BF16),
            ]
            + [pltpu.VMEM((wide, width), F32)] * sides,
        )

    middles, seconds, others = [], [], []
    for j in range(halves):
        middle, normed_second = output_part(j)
        middles.append(middle)
        seconds.append(normed_second)
        others.append(near(normed_second))

    near_parts = [
        list(feed_near(
            chunk, j * part_rows, seconds[j], others[j], cotangent, cot_near, expand_weight, contract_weight, line(expand_bias)
        ))
        for j in range(halves)
    ]
    far_parts, far_sums, grads = [], [], []
    far_bias = line(expand_bias_far)
    far_bias, near_parts[1][0] = tie(far_bias, near_parts[1][0])
    for j in range(halves):
        (g_own, g_near), kept, bias_sum = feed_far(
            chunk,
            j * part_rows,
            seconds[j],
            others[j],
            cotangent,
            cot_near,
            expand_far,
            contract_far,
            far_bias,
            near_parts[j][2],
            near_parts[j][3],
            expand_weight,
            parity,
        )
        far_sums.append(bias_sum)
        far_parts.append(list(kept))
        g_sum = add(g_own, near(g_near))
        if j == 0:
            far_bias, g_sum = tie(far_bias, g_sum)
        grads.append(list(heads_sum(g_sum)))

    hblk = min(512, hid)
    n_blk = hid // hblk

    def contract_grad(parts, at, count):
        lefts = [(p[n], (part_rows, hblk), lambda i: (0, at + i)) for n in range(2) for p in parts]
        rights = [(c, (part_rows, width), lambda i, j=j: (j, 0)) for c in (cotangent, cot_near) for j in range(halves)]
        return call(
            pair_grad_kernel,
            (count,),
            lefts + rights,
            [((count * hblk, width), BF16, (hblk, width), down)],
            flops=rows,
            moved=rows,
            vmem=56,
        )[0]

    def expand_grad(parts, at, count):
        lefts = [(x, (part_rows, hblk), lambda i: (0, at + i)) for x in seconds + others]
        rights = [whole(p[n]) for n in (2, 3) for p in parts]
        return call(
            pair_grad_kernel,
            (count,),
            lefts + rights,
            [((count * hblk, hid), BF16, (hblk, hid), down)],
            flops=rows,
            moved=rows,
            vmem=56,
        )[0]

    contract_send = contract_grad(far_parts, 0, n_blk)
    contract_moved = far(contract_send)
    far_parts[1][3], *grads[0] = tie(far_parts[1][3], *grads[0])
    expand_send = expand_grad(far_parts, 0, width // hblk)
    near_parts[1][0], contract_send, expand_send = tie(near_parts[1][0], contract_send, expand_send)
    near_parts[1][3], *grads[1] = tie(near_parts[1][3], *grads[1])
    query_late, *grads[1] = tie(query_keep, *grads[1])
    contract_own = contract_grad(near_parts, 0, n_blk)
    expand_own = expand_grad(near_parts, 0, width // hblk)
    bias_near = near_parts[0][4][0] + near_parts[1][4][0]
    bias_far = functools.reduce(lambda u, v: u + v, far_sums)
    expand_send, contract_moved = tie(expand_send, contract_moved)
    expand_moved = far(expand_send)
    grads[0][0], contract_own, expand_own = tie(grads[0][0], contract_own, expand_own)

    gms, lows, keeps, sends, sums = [], [], [], [], []
    for j in range(halves):
        terms = grads[j : j + 1]
        at = lambda i, j=j: (j, 0)
        gm, low, keep, send, part = call(
            functools.partial(second_back_kernel, 1),
            (1,),
            [whole(t[0]) for t in terms]
            + [whole(t[1]) for t in terms]
            + [
                whole(middles[j]),
                (cotangent, (part_rows, width), at),
                whole(line(mlp_norm_gain)),
                whole(out_keep),
                whole(out_send),
            ],
            [
                ((part_rows, width), F32, (part_rows, width), lambda i: (0, 0)),
                ((part_rows, width), BF16, (part_rows, width), lambda i: (0, 0)),
                ((part_rows, cols), BF16, (part_rows, cols), lambda i: (0, 0)),
                ((part_rows, cols), BF16, (part_rows, cols), lambda i: (0, 0)),
                ((8, width), F32, (8, width), lambda i: (0, 0)),
            ],
            flops=4 * part_rows * width * cols,
            moved=16 * part_rows * width + 4 * width * cols,
            vmem=58,
        )
        gms.append(gm)
        lows.append(low)
        keeps.append(keep)
        sends.append(near(send))
        sums.append(part[:4])
    grad_middle = jnp.concatenate(gms)
    grad_a, grad_b = jnp.concatenate(keeps), jnp.concatenate(sends)
    mid_sums = functools.reduce(lambda u, v: u + v, sums)

    if n_heads == 2:
        query_other = across(query_late)
        query_all = [query_keep, query_send, query_other, near(query_other)]
    else:
        query_all = heads_weights(query_keep, query_send, 1)

    grad_low = jnp.concatenate(lows)

    def dot_left(left, right):
        return dot_tn(left, right).astype(BF16)

    def chips_half(block):
        size = block.shape[0] // chips
        mine = lax.dynamic_slice_in_dim(block, chip * size, size, 0)
        other = lax.dynamic_slice_in_dim(block, (1 - chip) * size, size, 0)
        return mine, far(other)

    def all_blocks(total):
        pair = ordered(chip, total, far(total), 0)
        return pair, near(pair)

    contract_sum = add(contract_own, contract_moved)

    bq, bk, half, scalars = blocks_of(BACKWARD_BLOCK)

    def attn_backward(n, info):
        own, other, for_near, lse = attn[n]
        return call(
            functools.partial(attn_backward_kernel, part_heads, half, bk, scale, scale * LOG2E),
            (2 * half,),
            [
                (info, None, None),
                (query_a, (bq, part_cols), at_a(n, half)),
                (query_b, (bq, part_cols), at_b(n, half)),
                (grad_a, (bq, part_cols), at_a(n, half)),
                (grad_b, (bq, part_cols), at_b(n, half)),
                (own, (bq, part_cols), at_a(0, half)),
                (for_near, (bq, part_cols), at_b(0, half)),
                whole(kv_whole),
                (kv_turned, (dim, window), lambda i, *_: (0, 0)),
                (start_row, (1, bq), lambda i, *_: (0, i)),
                (lse, (part_heads, bq), lambda i, *_: (0, i)),
            ],
            [
                ((rows, part_cols), BF16, (bq, part_cols), at_a(0, half)),
                ((rows, part_cols), BF16, (bq, part_cols), at_b(0, half)),
                ((window, 2 * dim), F32, (window, 2 * dim), lambda i, *_: (0, 0)),
            ],
            scratch=[pltpu.VMEM((part_heads, dim, bq), F32)],
            prefetch=1,
            vmem=48,
            flops=pairs_guess,
            moved=rows,
        )

    own_all = jnp.concatenate([a[0] for a in attn], 1)
    other_all = jnp.concatenate([a[1] for a in attn], 1)
    out_sum = add(dot_left(own_all, grad_low), near(dot_left(other_all, grad_low)))
    expand_size = width // n_dp
    out_size = out_sum.shape[0] // chips * width // hid // n_dp
    def feed_output(first_input):
        count = 2 * halves
        out_cols = min(512, width)
        blocks = [
            (p[n], (part_rows, size), lambda i, shift, k=k: (0, lax.rem(k + shift[0], pieces)))
            for n in range(2)
            for p in far_parts
            for k in range(pieces)
        ]
        return call(
            functools.partial(contract_kernel, count, pieces),
            (width // out_cols,),
            [(parity.reshape(1), None, None)]
            + [whole(p) for p in [first_input, near_parts[1][0], near_parts[0][1], near_parts[1][1]]]
            + blocks
            + [(v, (v.shape[0], out_cols), lambda i, *_: (0, i)) for v in [contract_weight] + contract_far],
            [((rows, width), BF16, (rows, out_cols), lambda i, *_: (0, i))] * 2,
            flops=rows,
            moved=rows,
            vmem=56,
            prefetch=1,
        )

    back_acts, dq_own, dq_other, dkv = [], [], [], None
    info = scalars[0]
    for n in range(calls):
        if n == 0:
            info, contract_sum, out_sum = tie(info, contract_sum, out_sum)
            out_half = add(*chips_half(out_sum))
            contract_half = contract_sum.shape[0] // 2
            contract_first = lax.psum(contract_sum[:contract_half], "dp")
        own, for_near, dkv_part = attn_backward(n, info)
        if n == 0:
            mlp_start, dkv_part = tie(near_parts[0][0], dkv_part)
            mlp_own, mlp_near = feed_output(mlp_start)
            info, mlp_own, query_all[-1] = tie(info, mlp_own, query_all[-1])
        if n == calls - 1:
            for_near, contract_first = tie(for_near, contract_first)
            contract_rest, contract_first = tie(contract_sum[contract_half:], contract_first)
            contract_second = lax.psum(contract_rest, "dp")
            joined = jnp.concatenate(
                [add(expand_own, expand_moved).reshape(n_dp, expand_size, hid), out_half.reshape(n_dp, out_size, hid)], 1
            )
            joined = joined.reshape(-1, hid)
            for_near, joined = tie(for_near, joined)
            expand_chain = Chain(joined)
            expand_chain.step()
            expand_chain.prepare()
            expand_chain.up, expand_chain.out = tie(expand_chain.up, expand_chain.out)
        other = near(for_near)
        dq_own.append(own)
        dq_other.append(other)
        back_acts.append(jnp.concatenate([own, other], 1))
        if n == 0 and calls > 1:
            info, back_acts[0] = tie(info, back_acts[0])
        dkv = dkv_part if dkv is None else dkv + dkv_part
    back_acts = [a for act in back_acts for a in heads_acts(act)]

    dkv = dkv.reshape(chips, 2, rows, 2 * dim)

    def half_of(value, axis, bit):
        return lax.dynamic_index_in_dim(value, bit, axis, keepdims=False)

    core_sum = half_of(dkv, 1, core) + near(half_of(dkv, 1, 1 - core).astype(BF16)).astype(F32)
    chip_sum = add(half_of(core_sum, 0, chip), far(half_of(core_sum, 0, 1 - chip).astype(BF16)))
    first, second = heads_sum(chip_sum)
    grad_kv = add(first, second)

    kv_keep = lax.dynamic_slice_in_dim(grad_kv, core * dim, dim, 1)
    kv_send = lax.dynamic_slice_in_dim(grad_kv, (1 - core) * dim, dim, 1)
    query_sent = near(dot_left(normed_first, jnp.concatenate(dq_other + [kv_send], 1)))
    query_block = add(dot_left(normed_first, jnp.concatenate(dq_own + [kv_keep], 1)), query_sent)
    query_chain = Chain(add(*chips_half(query_block)))
    expand_chain.step()
    grad_kv, expand_chain.up, expand_chain.down = tie(grad_kv, expand_chain.up, expand_chain.down)
    input_grad, first_sums = call(
        functools.partial(first_back_kernel, len(back_acts), sides),
        (rows // wide,),
        [rows_of(a, wide) for a in back_acts]
        + [whole(w) for w in query_all]
        + [rows_of(grad_kv, wide), whole(key_value_weight)]
        + [rows_of(tokens, wide), rows_of(grad_middle, wide), whole(line(pre_norm_gain))],
        [((rows, width), BF16, (wide, width), down), ((8, width), F32, (8, width), lambda i: (0, 0))],
        flops=2 * rows * width * (width + 2 * dim),
        moved=20 * rows * width,
        vmem=60,
        scratch=[
            pltpu.VMEM((sides, wide, width // sides), BF16),
            pltpu.VMEM((sides, width, width // sides), BF16),
        ]
        + [pltpu.VMEM((wide, width), F32)] * sides,
    )

    mlp_sum, first_sums = tie(add(mlp_own, near(mlp_near)), first_sums)
    mlp_first, mlp_second = heads_sum(mlp_sum)
    mlp_total = mlp_first.astype(F32) + mlp_second.astype(F32)
    layer_output = (jnp.concatenate(middles) + mlp_total + contract_bias).astype(BF16)

    expand_chain.step()
    expand_chain.up, input_grad, contract_second = tie(expand_chain.up, input_grad, contract_second)
    contract_weight_grad = jnp.concatenate([contract_first, contract_second]).astype(F32)
    dq_bias_keep = jnp.concatenate([jnp.sum(v.astype(F32), 0) for v in dq_own])
    dq_bias_send = jnp.concatenate([jnp.sum(v.astype(F32), 0) for v in dq_other])
    query_bias_part = ordered(core, dq_bias_keep, dq_bias_send, 0)
    value_bias_part = jnp.sum(grad_kv[:, dim:].astype(F32), 0)

    places_of_units = jnp.arange(n_rows)[:, None]
    units = jnp.where(places_of_units == row_index, bias_near, 0.0) + jnp.where(
        places_of_units == jnp.bitwise_xor(row_index, 2), bias_far, 0.0
    )
    shorts = [mid_sums, first_sums[:2], query_bias_part, value_bias_part, units]
    short_sums = jnp.concatenate([v.reshape(-1) for v in shorts])
    for k in range(3):
        if k == 2:
            expand_chain.up, contract_weight_grad = tie(expand_chain.up, contract_weight_grad)
        expand_chain.up, short_sums = tie(expand_chain.up, short_sums)
        together([expand_chain, query_chain], [])
        short_sums = hop_sum(short_sums)
    joined = expand_chain.result().reshape(n_dp, -1, hid)
    expand_weight_grad = joined[:, :expand_size].reshape(width, hid).astype(F32)
    query_chain.up, expand_weight_grad, layer_output, short_sums = tie(
        query_chain.up, expand_weight_grad, layer_output, short_sums
    )
    query_chain.step()
    short_sums = hop_sum(short_sums)
    while hops:
        short_sums = hop_sum(short_sums)
    query_chain.up, short_sums = tie(query_chain.up, short_sums)
    out_total = joined[:, expand_size:].reshape(out_half.shape)
    out_block = ordered(chip, out_total, far(out_total), 0)
    query_chain.step()
    query_chain.up, out_block = tie(query_chain.up, out_block)
    out_block_near = near(out_block)
    output_weight_grad = ordered(core, out_block, out_block_near, 0).astype(F32)
    query_block, query_block_near = all_blocks(query_chain.result())
    query_weight_grad, key_value_weight_grad = call(
        side_by_side_kernel,
        (width // min(512, width),),
        [
            (core.reshape(1), None, None),
            (query_block, (min(512, width), cols + dim), lambda i, *_: (i, 0)),
            (query_block_near, (min(512, width), cols + dim), lambda i, *_: (i, 0)),
        ],
        [
            ((width, 2 * cols), F32, (min(512, width), 2 * cols), lambda i, *_: (i, 0)),
            ((width, 2 * dim), F32, (min(512, width), 2 * dim), lambda i, *_: (i, 0)),
        ],
        prefetch=1,
        moved=12 * width * (cols + dim),
    )

    short_totals, at = [], 0
    for v in shorts:
        short_totals.append(short_sums[at : at + v.size].reshape(v.shape))
        at += v.size
    mid_total, first_total, query_bias_grad, value_bias_grad, units = short_totals
    expand_bias_grad = lax.dynamic_index_in_dim(units, row_index, 0, keepdims=False)
    return (
        layer_output,
        input_grad,
        first_total[0],
        first_total[1],
        query_weight_grad,
        query_bias_grad,
        key_value_weight_grad,
        value_bias_grad,
        output_weight_grad,
        mid_total[2],
        mid_total[0],
        mid_total[1],
        expand_weight_grad,
        expand_bias_grad,
        contract_weight_grad,
        mid_total[3],
    )


def solution(mesh):
    both = P(("heads", "rows"))
    in_specs = (
        P(("dp", "rows"), None),
        P("dp", None),
        P(),
        P(),
        P(None, "heads"),
        P("heads"),
        P(),
        P(),
        P("heads", None),
        P(),
        P(),
        P(),
        P(None, ("heads", "rows")),
        both,
        P(("heads", "rows"), None),
        P(),
        P(("dp", "rows"), None),
    )
    out_specs = (
        P(("dp", "rows"), None),
        P(("dp", "rows"), None),
        P(),
        P(),
        P(None, "heads"),
        P("heads"),
        P(),
        P(),
        P("heads", None),
        P(),
        P(),
        P(),
        P(None, ("heads", "rows")),
        both,
        P(("heads", "rows"), None),
        P(),
    )
    return jax.shard_map(body, mesh=mesh, in_specs=in_specs, out_specs=out_specs, check_vma=False)
```

```python
import functools
import math

import jax
import jax.numpy as jnp
from jax import lax
from jax.experimental import pallas as pl
from jax.experimental.pallas import tpu as pltpu
from jax.sharding import PartitionSpec as P

NORM_EPSILON = 1e-05
FAR = -1e30
LOG2E = 1.4426950408889634
GELU_A = math.sqrt(2.0 / math.pi)
GELU_B = 0.044715
F32 = jnp.float32
BF16 = jnp.bfloat16
MIB = 1024 * 1024
FORWARD_BLOCK = (512, 1024)
BACKWARD_BLOCK = (256, 1024)


def dot(left, right):
    return jnp.dot(left, right, preferred_element_type=F32)


def dot_tn(left, right):
    return lax.dot_general(left, right, (((0,), (0,)), ((), ())), preferred_element_type=F32)


def dot_nt(left, right):
    return lax.dot_general(left, right, (((1,), (1,)), ((), ())), preferred_element_type=F32)


def call(kernel, grid, ins, outs, scratch=(), prefetch=0, vmem=48, flops=0, moved=0, alias=None):
    arrays = [a for a, _, _ in ins[prefetch:]]
    specs = [
        pl.BlockSpec(b, m, pipeline_mode=pl.Buffered(1)) if b == a.shape else pl.BlockSpec(b, m) for a, b, m in ins[prefetch:]
    ]
    scalars = [a for a, _, _ in ins[:prefetch]]
    return pl.pallas_call(
        kernel,
        grid_spec=pltpu.PrefetchScalarGridSpec(
            num_scalar_prefetch=prefetch,
            grid=grid,
            in_specs=specs,
            out_specs=[pl.BlockSpec(b, m) for _, _, b, m in outs],
            scratch_shapes=list(scratch),
        ),
        out_shape=[jax.ShapeDtypeStruct(s, d) for s, d, _, _ in outs],
        compiler_params=pltpu.CompilerParams(vmem_limit_bytes=vmem * MIB),
        cost_estimate=pl.CostEstimate(flops=int(flops), bytes_accessed=int(moved), transcendentals=0),
        input_output_aliases=alias or {},
    )(*scalars, *arrays)


def whole(array):
    zeros = (0,) * array.ndim
    return (array, array.shape, lambda *_: zeros)


def rows_of(array, block):
    return (array, (block, array.shape[1]), lambda i, *_: (i, 0))


def normed(values, gain, bias):
    mean = jnp.mean(values, -1, keepdims=True)
    centred = values - mean
    var = jnp.mean(centred * centred, -1, keepdims=True)
    return centred * lax.rsqrt(var + NORM_EPSILON) * gain + bias


def norm_back(values, grad, gain):
    mean = jnp.mean(values, -1, keepdims=True)
    centred = values - mean
    var = jnp.mean(centred * centred, -1, keepdims=True)
    inverse = lax.rsqrt(var + NORM_EPSILON)
    xhat = centred * inverse
    g = grad * gain
    g_mean = jnp.mean(g, -1, keepdims=True)
    gx_mean = jnp.mean(g * xhat, -1, keepdims=True)
    return xhat, (g - g_mean - xhat * gx_mean) * inverse


def norm_kv_kernel(t_ref, g_ref, b_ref, w_ref, wb_ref, n_ref, kv_ref):
    low = normed(t_ref[...].astype(F32), g_ref[...], b_ref[...]).astype(BF16)
    n_ref[...] = low
    kv_ref[...] = (dot(low, w_ref[...]) + wb_ref[...]).astype(BF16)


def project_kernel(core, n_ref, wa_ref, ba_ref, wb_ref, bb_ref, a_ref, b_ref):
    low = n_ref[...]
    b_ref[...] = (dot(low, wb_ref[...]) + bb_ref[...]).astype(BF16)
    a_ref[...] = (dot(low, wa_ref[...]) + ba_ref[...]).astype(BF16)


def attn_forward_kernel(heads, half, bk, scale2, info, qa_ref, qb_ref, kv_ref, vt_ref, st_ref, oa_ref, ob_ref, lse_ref, m_ref, l_ref, acc_ref):
    i = pl.program_id(0)
    first, low, high, clear_from, clear_to = (info[n, i] for n in range(5))
    bq, dim = qa_ref.shape[0], kv_ref.shape[1] // 2
    in_a = i < half
    start = st_ref[...]
    place = first + lax.broadcasted_iota(jnp.int32, (1, bq), 1)
    queries = jnp.where(in_a, qa_ref[...], qb_ref[...])
    m_ref[...] = jnp.full_like(m_ref, FAR)
    l_ref[...] = jnp.zeros_like(l_ref)
    acc_ref[...] = jnp.zeros_like(acc_ref)

    def step(block, masked):
        begin = pl.multiple_of(block * bk, bk)
        keys = kv_ref[pl.ds(begin, bk), :dim]
        values = vt_ref[:, pl.ds(begin, bk)]
        if masked:
            key_place = begin + lax.broadcasted_iota(jnp.int32, (bk, 1), 0)
            allowed = (key_place >= start) & (key_place <= place)
        for h in range(heads):
            s = dot_nt(keys, queries[:, h * dim : (h + 1) * dim])
            if masked:
                s = jnp.where(allowed, s, FAR)
            old = m_ref[h : h + 1, :]
            new = jnp.maximum(old, jnp.max(s, 0, keepdims=True) * scale2)
            p = jnp.exp2(s * scale2 - new)
            fix = jnp.exp2(old - new)
            l_ref[h : h + 1, :] = l_ref[h : h + 1, :] * fix + jnp.sum(p, 0, keepdims=True)
            m_ref[h : h + 1, :] = new
            acc_ref[h] = acc_ref[h] * fix + dot(values, p.astype(BF16))

    def body(block, carry):
        clear = (block >= clear_from) & (block < clear_to)

        @pl.when(clear)
        def _():
            step(block, False)

        @pl.when(jnp.logical_not(clear))
        def _():
            step(block, True)

        return carry

    lax.fori_loop(low, high, body, 0)
    outs = []
    for h in range(heads):
        total = l_ref[h : h + 1, :]
        outs.append((acc_ref[h] / total).T.astype(BF16))
    lse_ref[...] = m_ref[...] + jnp.log2(l_ref[...])

    @pl.when(in_a)
    def _():
        for h in range(heads):
            oa_ref[:, h * dim : (h + 1) * dim] = outs[h]

    @pl.when(jnp.logical_not(in_a))
    def _():
        for h in range(heads):
            ob_ref[:, h * dim : (h + 1) * dim] = outs[h]


def attn_backward_kernel(
    heads, half, bk, scale, scale2, info, qa_ref, qb_ref, ga_ref, gb_ref, oa_ref, ob_ref, kv_ref, kt_ref, st_ref, lse_ref, dqa_ref, dqb_ref, dkv_ref, dq_ref
):
    i = pl.program_id(0)
    first, low, high, clear_from, clear_to = (info[n, i] for n in range(5))
    bq, dim = qa_ref.shape[0], kv_ref.shape[1] // 2
    in_a = i < half

    @pl.when(i == 0)
    def _():
        dkv_ref[...] = jnp.zeros_like(dkv_ref)

    start = st_ref[...]
    place = first + lax.broadcasted_iota(jnp.int32, (1, bq), 1)
    queries = jnp.where(in_a, qa_ref[...], qb_ref[...])
    grads = jnp.where(in_a, ga_ref[...], gb_ref[...])
    outs = jnp.where(in_a, oa_ref[...], ob_ref[...])
    inner, lse = [], []
    for h in range(heads):
        cut = slice(h * dim, (h + 1) * dim)
        product = grads[:, cut].astype(F32) * outs[:, cut].astype(F32)
        inner.append(jnp.sum(product.T, 0, keepdims=True))
        lse.append(lse_ref[h : h + 1, :])
    dq_ref[...] = jnp.zeros_like(dq_ref)

    def step(block, masked):
        begin = pl.multiple_of(block * bk, bk)
        keys = kv_ref[pl.ds(begin, bk), :dim]
        values = kv_ref[pl.ds(begin, bk), dim:]
        keys_t = kt_ref[:, pl.ds(begin, bk)]
        if masked:
            key_place = begin + lax.broadcasted_iota(jnp.int32, (bk, 1), 0)
            allowed = (key_place >= start) & (key_place <= place)
        dk = None
        for h in range(heads):
            cut = slice(h * dim, (h + 1) * dim)
            s = dot_nt(keys, queries[:, cut])
            dp = dot_nt(values, grads[:, cut])
            p = jnp.exp2(s * scale2 - lse[h])
            if masked:
                p = jnp.where(allowed, p, 0.0)
            ds = (p * (dp - inner[h])).astype(BF16)
            dv_part = dot(p.astype(BF16), grads[:, cut])
            dk_part = dot(ds, queries[:, cut])
            dk, dv = (dk_part, dv_part) if dk is None else (dk + dk_part, dv + dv_part)
            dq_ref[h] += dot(keys_t, ds)
        dkv_ref[pl.ds(begin, bk), :dim] += dk * scale
        dkv_ref[pl.ds(begin, bk), dim:] += dv

    def body(block, carry):
        clear = (block >= clear_from) & (block < clear_to)

        @pl.when(clear)
        def _():
            step(block, False)

        @pl.when(jnp.logical_not(clear))
        def _():
            step(block, True)

        return carry

    lax.fori_loop(low, high, body, 0)

    def leave(ref):
        for h in range(heads):
            ref[:, h * dim : (h + 1) * dim] = (dq_ref[h] * scale).T.astype(BF16)

    @pl.when(in_a)
    def _():
        leave(dqa_ref)

    @pl.when(jnp.logical_not(in_a))
    def _():
        leave(dqb_ref)


def balanced(acts, weights, product, by_rows, scratch):
    act_ref, weight_ref, sums = scratch[0], scratch[1], scratch[2:]
    sides = len(sums)
    calls = len(acts) // sides
    cols = acts[0].shape[1] // 2
    for n in range(sides):

        @pl.when(pl.program_id(0) == 0)
        def _():
            keep, send = weights[2 * n], weights[2 * n + 1]
            if by_rows:
                size = keep.shape[0]
                weight_ref[n, :size, :] = keep[...]
                weight_ref[n, size:, :] = send[...]
            else:
                size = keep.shape[1]
                weight_ref[n, :, :size] = keep[...]
                weight_ref[n, :, size:] = send[...]

        for k in range(calls):
            act = acts[k * sides + n]
            act_ref[n, :, k * cols : (k + 1) * cols] = act[:, :cols]
            act_ref[n, :, (calls + k) * cols : (calls + k + 1) * cols] = act[:, cols:]
        sums[n][...] = product(act_ref[n], weight_ref[n])
    return functools.reduce(lambda u, v: u + v, [r[...] for r in sums])


def output_kernel(count, sides, *refs):
    acts, weights = refs[:count], refs[count : count + 2 * sides]
    t_ref, ob_ref, g_ref, b_ref, mid_ref, n_ref, *scratch = refs[count + 2 * sides :]
    near = balanced(acts, weights, dot, True, scratch)
    middle = t_ref[...].astype(F32) + near + ob_ref[...]
    mid_ref[...] = middle
    n_ref[...] = normed(middle, g_ref[...], b_ref[...]).astype(BF16)


def feed_tile(x, c, w, v, bias):
    before = dot(x, w) + bias
    grad = dot_nt(c, v)
    square = before * before
    t = jnp.tanh(before * (GELU_A + (GELU_A * GELU_B) * square))
    half = 0.5 + 0.5 * t
    slope = half + before * (half * (1.0 - t)) * (GELU_A + (3.0 * GELU_A * GELU_B) * square)
    return (before * half).astype(BF16), grad * slope


def stack(scratch, first, second):
    rows = first.shape[0]
    scratch[:rows, :] = first[...]
    scratch[rows:, :] = second[...]


def add_to(ref, value, fresh):
    @pl.when(fresh)
    def _():
        ref[...] = jnp.zeros_like(ref)

    ref[...] += jnp.broadcast_to(value, ref.shape)


def feed_near_kernel(blk, xa_ref, xb_ref, ca_ref, cb_ref, w_ref, v_ref, b_ref, ha_ref, hb_ref, da_ref, db_ref, sum_ref, x_ref, c_ref):
    rows = xa_ref.shape[0]
    stack(x_ref, xa_ref, xb_ref)
    stack(c_ref, ca_ref, cb_ref)
    sums = []
    for at in range(0, w_ref.shape[1], blk):
        cut = slice(at, at + blk)
        hidden, grad = feed_tile(x_ref[...], c_ref[...], w_ref[:, cut], v_ref[cut, :], b_ref[:, cut])
        low = grad.astype(BF16)
        ha_ref[:, cut] = hidden[:rows]
        hb_ref[:, cut] = hidden[rows:]
        da_ref[:, cut] = low[:rows]
        db_ref[:, cut] = low[rows:]
        sums.append(jnp.sum(grad, 0, keepdims=True))
    add_to(sum_ref, jnp.concatenate(sums, 1), pl.program_id(0) == 0)


def feed_far_kernel(steps, back, order, xa_ref, xb_ref, ca_ref, cb_ref, b_ref, ea_ref, eb_ref, u_ref, *rest):
    w_refs, z_refs, v_refs = rest[:steps], rest[steps : 2 * steps], rest[2 * steps : 3 * steps]
    ga_ref, gb_ref, ha_ref, hb_ref, da_ref, db_ref, sum_ref, x_ref, c_ref, e_ref, low_ref = rest[-11:]
    i = lax.rem(pl.program_id(0), steps + back)
    rows = xa_ref.shape[0]

    @pl.when(i == 0)
    def _():
        stack(x_ref, xa_ref, xb_ref)
        stack(c_ref, ca_ref, cb_ref)
        stack(e_ref, ea_ref, eb_ref)

    for k in range(steps):

        @pl.when(i == k)
        def _():
            hidden, grad = feed_tile(x_ref[...], c_ref[...], w_refs[k][...], v_refs[k][...], b_ref[...])
            low = grad.astype(BF16)
            ha_ref[...] = hidden[:rows]
            hb_ref[...] = hidden[rows:]
            da_ref[...] = low[:rows]
            db_ref[...] = low[rows:]
            low_ref[k] = low
            sum_ref[...] = jnp.broadcast_to(jnp.sum(grad, 0, keepdims=True), sum_ref.shape)

    @pl.when(i >= steps)
    def _():
        total = dot_nt(e_ref[...], u_ref[...])
        for k in range(steps):
            total = total + dot_nt(low_ref[k], z_refs[k][...])
        ga_ref[...] = total[:rows].astype(BF16)
        gb_ref[...] = total[rows:].astype(BF16)


def feed_near(chunk, first_row, x_own, x_other, c_own, c_other, w, v, bias):
    rows, width = x_own.shape
    hid = w.shape[1]
    base = first_row // chunk
    at = lambda i: (i, 0)
    at_all = lambda i: (base + i, 0)
    return call(
        functools.partial(feed_near_kernel, min(512, hid)),
        (rows // chunk,),
        [
            (x_own, (chunk, width), at),
            (x_other, (chunk, width), at),
            (c_own, (chunk, width), at_all),
            (c_other, (chunk, width), at_all),
            whole(w),
            whole(v),
            whole(bias),
        ],
        [((rows, hid), BF16, (chunk, hid), at)] * 4 + [((8, hid), F32, (8, hid), lambda i: (0, 0))],
        scratch=[pltpu.VMEM((2 * chunk, width), BF16)] * 2,
        vmem=56,
        flops=8 * rows * width * hid,
        moved=8 * width * hid + 8 * rows * width,
    )


def feed_far(chunk, first_row, x_own, x_other, c_own, c_other, w, v, bias, near_own, near_other, w_near, parity):
    rows, width = x_own.shape
    hid = w_near.shape[1]
    steps = len(w)
    blk = hid // steps
    out_blk = min(512, width)
    back = width // out_blk
    per = steps + back
    count = rows // chunk
    base = first_row // chunk
    at = lambda i, p: (i // per, 0)
    at_all = lambda i, p: (base + i // per, 0)
    tile = lambda i, p: lax.rem(jnp.minimum(lax.rem(i, per), steps - 1) + p[0], steps)
    after = lambda i: jnp.maximum(lax.rem(i, per) - steps, 0)
    ins = [
        (parity.reshape(1), None, None),
        (x_own, (chunk, width), at),
        (x_other, (chunk, width), at),
        (c_own, (chunk, width), at_all),
        (c_other, (chunk, width), at_all),
        (bias, (1, blk), lambda i, p: (0, tile(i, p))),
        (near_own, (chunk, hid), at),
        (near_other, (chunk, hid), at),
        (w_near, (out_blk, hid), lambda i, p: (after(i), 0)),
    ]
    ins += [whole(p) for p in w]
    ins += [(u, (out_blk, blk), lambda i, p: (after(i), 0)) for u in w]
    ins += [whole(p) for p in v]
    outs = [((rows, width), BF16, (chunk, out_blk), lambda i, p: (i // per, after(i)))] * 2
    outs += [((rows, hid), BF16, (chunk, blk), lambda i, p: (i // per, tile(i, p)))] * 4
    outs += [((8 * count, hid), F32, (8, blk), lambda i, p: (i // per, tile(i, p)))]
    result = call(
        functools.partial(feed_far_kernel, steps, back),
        (count * per,),
        ins,
        outs,
        scratch=[
            pltpu.VMEM((2 * chunk, width), BF16),
            pltpu.VMEM((2 * chunk, width), BF16),
            pltpu.VMEM((2 * chunk, hid), BF16),
            pltpu.VMEM((steps, 2 * chunk, blk), BF16),
        ],
        prefetch=1,
        vmem=56,
        flops=rows,
        moved=rows,
    )
    return result[:2], result[2:6], jnp.sum(result[6].reshape(count, 8, hid)[:, 0], 0)


def contract_kernel(count, pieces, parity, *refs):
    near, far = refs[:count], refs[count : count + count * pieces]
    va_ref, *vb_refs = refs[count + count * pieces : count + count * pieces + pieces + 1]
    own_ref, other_ref = refs[-2:]
    size = near[0].shape[0]
    for k in range(count):
        y_ref = own_ref if k < count // 2 else other_ref
        at = k % (count // 2) * size
        total = dot(near[k][...], va_ref[...])
        for n in range(pieces):
            total = total + dot(far[k * pieces + n][...], vb_refs[n][...])
        y_ref[at : at + size, :] = total.astype(BF16)


def pair_grad_kernel(*refs):
    out_ref = refs[-1]
    count = (len(refs) - 1) // 2
    total = None
    for left, right in zip(refs[:count], refs[count:-1]):
        piece = dot_tn(left[...], right[...])
        total = piece if total is None else total + piece
    out_ref[...] = total.astype(BF16)


def second_back_kernel(count, *refs):
    firsts, seconds = refs[:count], refs[count : 2 * count]
    mid_ref, cot_ref, gain_ref, wk_ref, ws_ref, gm_ref, low_ref, keep_ref, send_ref, sums_ref = refs[2 * count :]
    size = firsts[0].shape[0]
    totals = [0.0, 0.0, 0.0, 0.0]
    for k in range(count):
        at = slice(k * size, (k + 1) * size)
        grad = firsts[k][...].astype(F32) + seconds[k][...].astype(F32)
        xhat, back = norm_back(mid_ref[at, :], grad, gain_ref[...])
        cot = cot_ref[at, :].astype(F32)
        total = cot + back
        gm_ref[at, :] = total
        low_ref[at, :] = total.astype(BF16)
        for n, value in enumerate((grad * xhat, grad, total, cot)):
            totals[n] = totals[n] + jnp.sum(value, 0, keepdims=True)
    send_ref[...] = dot_nt(low_ref[...], ws_ref[...]).astype(BF16)
    keep_ref[...] = dot_nt(low_ref[...], wk_ref[...]).astype(BF16)
    for n in range(4):
        sums_ref[n : n + 1, :] = totals[n]


def first_back_kernel(count, sides, *refs):
    acts, weights = refs[:count], refs[count : count + 2 * sides]
    kv_ref, kvw_ref, t_ref, gm_ref, gain_ref, out_ref, sums_ref, *scratch = refs[count + 2 * sides :]
    grad = balanced(acts, weights, dot_nt, False, scratch) + dot_nt(kv_ref[...], kvw_ref[...])
    xhat, back = norm_back(t_ref[...].astype(F32), grad, gain_ref[...])
    out_ref[...] = (gm_ref[...] + back).astype(BF16)

    @pl.when(pl.program_id(0) == 0)
    def _():
        sums_ref[...] = jnp.zeros_like(sums_ref)

    sums_ref[0:1, :] += jnp.sum(grad * xhat, 0, keepdims=True)
    sums_ref[1:2, :] += jnp.sum(grad, 0, keepdims=True)


def side_by_side_kernel(core, mine_ref, near_ref, query_ref, kv_ref):
    first = core[0] == 0
    mine, near = mine_ref[...].astype(F32), near_ref[...].astype(F32)
    cols = query_ref.shape[1] // 2
    left, right = jnp.where(first, mine, near), jnp.where(first, near, mine)
    query_ref[:, :cols] = left[:, :cols]
    query_ref[:, cols:] = right[:, :cols]
    kv_ref[:, : kv_ref.shape[1] // 2] = left[:, cols:]
    kv_ref[:, kv_ref.shape[1] // 2 :] = right[:, cols:]


def body(
    tokens,
    segment_lengths,
    pre_norm_gain,
    pre_norm_bias,
    query_weight,
    query_bias,
    key_value_weight,
    value_bias,
    output_weight,
    output_bias,
    mlp_norm_gain,
    mlp_norm_bias,
    expand_weight,
    expand_bias,
    contract_weight,
    contract_bias,
    cotangent,
):
    rows, width = tokens.shape
    n_heads, n_rows, n_dp = (lax.axis_size(a) for a in ("heads", "rows", "dp"))
    row_index = lax.axis_index("rows")
    core = lax.rem(row_index, 2)
    dim = key_value_weight.shape[1] // 2
    local_heads = query_weight.shape[1] // dim
    group = local_heads // 2
    cols = group * dim
    window = rows * n_rows
    scale = 1.0 / math.sqrt(dim)
    hid = expand_weight.shape[1]

    chips = n_rows // 2
    chip = row_index // 2
    dp_index = lax.axis_index("dp")

    def near(value):
        return lax.ppermute(value, "rows", [(i, i ^ 1) for i in range(n_rows)])

    def far(value):
        return lax.ppermute(value, "rows", [(i, i ^ 2) for i in range(n_rows)])

    def across(value):
        return lax.ppermute(value, "heads", [(0, 1), (1, 0)])

    def beside(value):
        return lax.ppermute(value, "dp", [(i, i ^ 1) for i in range(n_dp)])

    def line(vector):
        return vector.reshape(1, -1)

    def tie(*values):
        return lax.optimization_barrier(values)

    def add(*terms):
        return functools.reduce(lambda u, v: u + v, (t.astype(F32) for t in terms)).astype(BF16)

    def ordered(bit, mine, other, axis):
        return jnp.where(bit == 0, jnp.concatenate([mine, other], axis), jnp.concatenate([other, mine], axis))

    def heads_sum(value):
        if n_heads == 2:
            return value, across(value)
        total = lax.psum(value.astype(F32), "heads")
        high = total.astype(BF16)
        return high, (total - high.astype(F32)).astype(BF16)

    last = n_dp - 1

    class Chain:
        def __init__(self, value):
            self.value, self.size = value, value.shape[0] // n_dp
            self.up = self.down = self.out = None
            self.t = 0

        def prepare(self):
            self.out = jnp.zeros(((3 * n_dp - 2) * self.size,) + self.value.shape[1:], BF16)

        def piece(self, index):
            return lax.dynamic_slice_in_dim(self.value, jnp.clip(index, 0, last) * self.size, self.size, 0)

        def put(self, part, place):
            self.out = lax.dynamic_update_slice_in_dim(self.out, part, (place + last) * self.size, 0)

        def step(self):
            t, self.t = self.t, self.t + 1
            if t < last:
                up, down = self.piece(last + dp_index - t), self.piece(dp_index - last + t)
                if t > 0:
                    up, down = add(up, self.up), add(down, self.down)
                ends = range(t + 1)
            else:
                if t == last:
                    own = add(self.piece(dp_index), self.up, self.down)
                    if self.out is None:
                        self.prepare()
                    self.put(own, dp_index)
                    up = down = own
                else:
                    up, down = self.up, self.down
                ends = range(t - last, last)
            self.up = lax.ppermute(up, "dp", [(i, i + 1) for i in ends])
            self.down = lax.ppermute(down, "dp", [(last - i, last - i - 1) for i in ends])
            if t >= last:
                self.put(self.up, dp_index - 1 - (t - last))
                self.put(self.down, dp_index + 1 + (t - last))

        def result(self):
            while self.t < 2 * last:
                self.step()
            return self.out[last * self.size : (last + n_dp) * self.size]

    def together(chains, behind):
        for chain, values in zip(chains + behind, held(chains + behind)):
            if chain.t == 0:
                (chain.value,) = values
            else:
                chain.up, chain.down = values
        for chain in chains:
            chain.step()

    def held(chains):
        flat = [v for c in chains for v in ([c.value] if c.t == 0 else [c.up, c.down])]
        flat = list(tie(*flat))
        return [[flat.pop(0) for _ in range(1 if c.t == 0 else 2)] for c in chains]

    def landed(chains, *values):
        for chain in chains:
            chain.up, chain.down, *values = tie(chain.up, chain.down, *values)
        return values

    hops = [(axis, size, 1 << k) for axis, size in (("rows", n_rows), ("dp", n_dp)) for k in range(size.bit_length() - 1)]

    def hop_sum(value):
        if not hops:
            return value
        axis, size, hop = hops.pop(0)
        return value + lax.ppermute(value, axis, [(i, i ^ hop) for i in range(size)])

    keep_at, send_at = core * cols, (1 - core) * cols
    query_keep = lax.dynamic_slice_in_dim(query_weight, keep_at, cols, 1)
    query_send = lax.dynamic_slice_in_dim(query_weight, send_at, cols, 1)

    sides = 2 if n_heads == 2 else 1
    other_head = 1 - lax.axis_index("heads")

    def heads_acts(value):
        if n_heads == 2:
            return [value, across(value)]
        size = value.shape[1] // 2
        return [
            jnp.concatenate([lax.all_gather(v, "heads", axis=1, tiled=True) for v in (value[:, :size], value[:, size:])], 1)
        ]

    def heads_weights(keep, send, axis):
        whole_keep = lax.all_gather(keep, "heads", axis=axis, tiled=True)
        if n_heads > 2:
            return [whole_keep, near(whole_keep)]
        other = lax.dynamic_slice_in_dim(whole_keep, other_head * keep.shape[axis], keep.shape[axis], axis)
        return [keep, send, other, near(other)]

    expand_bias_far = far(expand_bias)
    cot_near = near(cotangent)

    blk = min(256, rows)
    grid = (rows // blk,)
    kv_bias = jnp.concatenate([jnp.zeros((dim,), F32), value_bias])
    normed_first, key_value = call(
        norm_kv_kernel,
        grid,
        [rows_of(tokens, blk), whole(line(pre_norm_gain)), whole(line(pre_norm_bias)), whole(key_value_weight), whole(line(kv_bias))],
        [
            ((rows, width), BF16, (blk, width), lambda i: (i, 0)),
            ((rows, 2 * dim), BF16, (blk, 2 * dim), lambda i: (i, 0)),
        ],
        flops=4 * rows * width * dim,
        moved=4 * rows * width,
    )
    output_weight, key_value = tie(output_weight, key_value)
    out_keep = lax.dynamic_slice_in_dim(output_weight, keep_at, cols, 0)
    out_send = lax.dynamic_slice_in_dim(output_weight, send_at, cols, 0)
    far_kv = far(key_value)
    near_kv = near(key_value)
    far_kv, expand_start, contract_start = tie(far_kv, expand_weight, contract_weight)
    pieces = hid // min(512, hid)
    size = hid // pieces
    helped = pieces == 2 and n_dp % 2 == 0
    parity = lax.rem(dp_index, 2) if helped else jnp.int32(0)
    if helped:
        expand_far = [far(lax.dynamic_slice_in_dim(expand_start, parity * size, size, 1))]
    else:
        expand_far = [far(expand_start[:, k * size : (k + 1) * size]) for k in range(pieces)]
    contract_start, expand_far[0] = tie(contract_start, expand_far[0])
    if helped:
        contract_far = [far(lax.dynamic_slice_in_dim(contract_start, parity * size, size, 0))]
    else:
        contract_far = [far(contract_start[k * size : (k + 1) * size]) for k in range(pieces)]
    pair_kv = ordered(core, key_value, near_kv, 0)
    far_pair = ordered(core, far_kv, near(far_kv), 0)
    kv_whole = ordered(chip, pair_kv, far_pair, 0)
    kv_turned = kv_whole.T

    query_a, query_for_near = call(
        project_kernel,
        grid,
        [
            (core.reshape(1), None, None),
            rows_of(normed_first, blk),
            (query_weight, (width, cols), lambda i, core: (0, core[0])),
            (line(query_bias), (1, cols), lambda i, core: (0, core[0])),
            (query_weight, (width, cols), lambda i, core: (0, 1 - core[0])),
            (line(query_bias), (1, cols), lambda i, core: (0, 1 - core[0])),
        ],
        [((rows, cols), BF16, (blk, cols), lambda i, *_: (i, 0))] * 2,
        prefetch=1,
        flops=4 * rows * width * cols,
        moved=2 * rows * width,
    )
    query_b = near(query_for_near)

    ends = jnp.cumsum(segment_lengths[0])
    own_place = row_index * rows
    near_place = (row_index + 1 - 2 * core) * rows
    steps = jnp.arange(rows, dtype=jnp.int32)
    places = jnp.concatenate([own_place + steps, near_place + steps])
    starts = jnp.max(jnp.where(ends[None, :] <= places[:, None], ends[None, :], 0), 1).astype(jnp.int32)

    def blocks_of(block):
        bq, bk = min(block[0], rows), min(block[1], window)
        first = places.reshape(-1, bq)[:, 0]
        start = starts.reshape(-1, bq)
        info = [first, start[:, 0] // bk, (first + bq - 1) // bk + 1, (start[:, -1] + bk - 1) // bk, (first + 1) // bk]
        return bq, bk, rows // bq, (jnp.stack(info).astype(jnp.int32), None, None)

    start_row = starts.reshape(1, -1)
    calls = 2 if group % 2 == 0 else 1
    part_heads = group // calls
    part_cols = part_heads * dim
    pairs_guess = 2 * rows * window // 4
    bq, bk, half, scalars = blocks_of(FORWARD_BLOCK)

    def at_a(n, half):
        return lambda i, *_: (jnp.minimum(i, half - 1), n)

    def at_b(n, half):
        return lambda i, *_: (jnp.maximum(i - half, 0), n)

    def attn_forward(n, info):
        return call(
            functools.partial(attn_forward_kernel, part_heads, half, bk, scale * LOG2E),
            (2 * half,),
            [
                (info, None, None),
                (query_a, (bq, part_cols), at_a(n, half)),
                (query_b, (bq, part_cols), at_b(n, half)),
                whole(kv_whole),
                (kv_turned, (dim, window), lambda i, *_: (1, 0)),
                (start_row, (1, bq), lambda i, *_: (0, i)),
            ],
            [
                ((rows, part_cols), BF16, (bq, part_cols), at_a(0, half)),
                ((rows, part_cols), BF16, (bq, part_cols), at_b(0, half)),
                ((part_heads, 2 * rows), F32, (part_heads, bq), lambda i, *_: (0, i)),
            ],
            scratch=[pltpu.VMEM((part_heads, bq), F32), pltpu.VMEM((part_heads, bq), F32), pltpu.VMEM((part_heads, dim, bq), F32)],
            prefetch=1,
            vmem=40,
            flops=16 * pairs_guess * part_cols,
            moved=8 * rows * part_cols,
        )

    attn, acts = [], []
    if n_heads == 2:
        out_other = across(out_keep)
    else:
        out_all = heads_weights(out_keep, out_send, 0)
    info = scalars[0]
    for n in range(calls):
        if n == 1:
            if n_heads == 2:
                info, out_other = tie(info, out_other)
            info, expand_far[0] = tie(info, expand_far[0])
        own, for_near, lse = attn_forward(n, info)
        if n == 1:
            own, for_near, acts[0][-1] = tie(own, for_near, acts[0][-1])
        other = near(for_near)
        attn.append((own, other, for_near, lse))
        act = jnp.concatenate([own, other], 1)
        if n == 0 and calls > 1:
            info, act, cot_near = tie(info, act, cot_near)
        acts.append(heads_acts(act))
    acts = [a for act in acts for a in act]
    if n_heads == 2:
        out_all = [out_keep, out_send, out_other, near(out_other)]
    if helped:
        expand_far.append(beside(expand_far[0]))
    acts[-1], contract_far[0], expand_far[-1] = tie(acts[-1], contract_far[0], expand_far[-1])
    if helped:
        contract_far.append(beside(contract_far[0]))

    halves = 2
    part_rows = rows // halves
    wide = min(512, part_rows)
    chunk = min(256, part_rows)
    sub = part_rows // chunk
    down = lambda i: (i, 0)

    def output_part(j):
        base = j * part_rows // wide
        at = lambda i: (base + i, 0)
        return call(
            functools.partial(output_kernel, len(acts), sides),
            (part_rows // wide,),
            [(a, (wide, a.shape[1]), at) for a in acts]
            + [whole(w) for w in out_all]
            + [(tokens, (wide, width), at), whole(line(output_bias)), whole(line(mlp_norm_gain)), whole(line(mlp_norm_bias))],
            [((part_rows, width), F32, (wide, width), down), ((part_rows, width), BF16, (wide, width), down)],
            flops=2 * part_rows * width * width,
            moved=20 * part_rows * width,
            vmem=60,
            scratch=[
                pltpu.VMEM((sides, wide, width // sides), BF16),
                pltpu.VMEM((sides, width // sides, width), BF16),
            ]
            + [pltpu.VMEM((wide, width), F32)] * sides,
        )

    middles, seconds, others = [], [], []
    for j in range(halves):
        middle, normed_second = output_part(j)
        middles.append(middle)
        seconds.append(normed_second)
        others.append(near(normed_second))

    near_parts = [
        list(feed_near(
            chunk, j * part_rows, seconds[j], others[j], cotangent, cot_near, expand_weight, contract_weight, line(expand_bias)
        ))
        for j in range(halves)
    ]
    far_parts, far_sums, grads = [], [], []
    far_bias = line(expand_bias_far)
    far_bias, near_parts[1][0] = tie(far_bias, near_parts[1][0])
    for j in range(halves):
        (g_own, g_near), kept, bias_sum = feed_far(
            chunk,
            j * part_rows,
            seconds[j],
            others[j],
            cotangent,
            cot_near,
            expand_far,
            contract_far,
            far_bias,
            near_parts[j][2],
            near_parts[j][3],
            expand_weight,
            parity,
        )
        far_sums.append(bias_sum)
        far_parts.append(list(kept))
        g_sum = add(g_own, near(g_near))
        if j == 0:
            far_bias, g_sum = tie(far_bias, g_sum)
        grads.append(list(heads_sum(g_sum)))

    hblk = min(512, hid)
    n_blk = hid // hblk

    def contract_grad(parts, at, count):
        lefts = [(p[n], (part_rows, hblk), lambda i: (0, at + i)) for n in range(2) for p in parts]
        rights = [(c, (part_rows, width), lambda i, j=j: (j, 0)) for c in (cotangent, cot_near) for j in range(halves)]
        return call(
            pair_grad_kernel,
            (count,),
            lefts + rights,
            [((count * hblk, width), BF16, (hblk, width), down)],
            flops=rows,
            moved=rows,
            vmem=56,
        )[0]

    def expand_grad(parts, at, count):
        lefts = [(x, (part_rows, hblk), lambda i: (0, at + i)) for x in seconds + others]
        rights = [whole(p[n]) for n in (2, 3) for p in parts]
        return call(
            pair_grad_kernel,
            (count,),
            lefts + rights,
            [((count * hblk, hid), BF16, (hblk, hid), down)],
            flops=rows,
            moved=rows,
            vmem=56,
        )[0]

    contract_send = contract_grad(far_parts, 0, n_blk)
    contract_moved = far(contract_send)
    far_parts[1][3], *grads[0] = tie(far_parts[1][3], *grads[0])
    expand_send = expand_grad(far_parts, 0, width // hblk)
    near_parts[1][0], contract_send, expand_send = tie(near_parts[1][0], contract_send, expand_send)
    near_parts[1][3], *grads[1] = tie(near_parts[1][3], *grads[1])
    query_late, *grads[1] = tie(query_keep, *grads[1])
    contract_own = contract_grad(near_parts, 0, n_blk)
    expand_own = expand_grad(near_parts, 0, width // hblk)
    bias_near = near_parts[0][4][0] + near_parts[1][4][0]
    bias_far = functools.reduce(lambda u, v: u + v, far_sums)
    expand_send, contract_moved = tie(expand_send, contract_moved)
    expand_moved = far(expand_send)
    grads[0][0], contract_own, expand_own = tie(grads[0][0], contract_own, expand_own)

    gms, lows, keeps, sends, sums = [], [], [], [], []
    for j in range(halves):
        terms = grads[j : j + 1]
        at = lambda i, j=j: (j, 0)
        gm, low, keep, send, part = call(
            functools.partial(second_back_kernel, 1),
            (1,),
            [whole(t[0]) for t in terms]
            + [whole(t[1]) for t in terms]
            + [
                whole(middles[j]),
                (cotangent, (part_rows, width), at),
                whole(line(mlp_norm_gain)),
                whole(out_keep),
                whole(out_send),
            ],
            [
                ((part_rows, width), F32, (part_rows, width), lambda i: (0, 0)),
                ((part_rows, width), BF16, (part_rows, width), lambda i: (0, 0)),
                ((part_rows, cols), BF16, (part_rows, cols), lambda i: (0, 0)),
                ((part_rows, cols), BF16, (part_rows, cols), lambda i: (0, 0)),
                ((8, width), F32, (8, width), lambda i: (0, 0)),
            ],
            flops=4 * part_rows * width * cols,
            moved=16 * part_rows * width + 4 * width * cols,
            vmem=58,
        )
        gms.append(gm)
        lows.append(low)
        keeps.append(keep)
        sends.append(near(send))
        sums.append(part[:4])
    grad_middle = jnp.concatenate(gms)
    grad_a, grad_b = jnp.concatenate(keeps), jnp.concatenate(sends)
    mid_sums = functools.reduce(lambda u, v: u + v, sums)

    if n_heads == 2:
        query_other = across(query_late)
        query_all = [query_keep, query_send, query_other, near(query_other)]
    else:
        query_all = heads_weights(query_keep, query_send, 1)

    grad_low = jnp.concatenate(lows)

    def dot_left(left, right):
        return dot_tn(left, right).astype(BF16)

    def chips_half(block):
        size = block.shape[0] // chips
        mine = lax.dynamic_slice_in_dim(block, chip * size, size, 0)
        other = lax.dynamic_slice_in_dim(block, (1 - chip) * size, size, 0)
        return mine, far(other)

    def all_blocks(total):
        pair = ordered(chip, total, far(total), 0)
        return pair, near(pair)

    contract_sum = add(contract_own, contract_moved)

    bq, bk, half, scalars = blocks_of(BACKWARD_BLOCK)

    def attn_backward(n, info):
        own, other, for_near, lse = attn[n]
        return call(
            functools.partial(attn_backward_kernel, part_heads, half, bk, scale, scale * LOG2E),
            (2 * half,),
            [
                (info, None, None),
                (query_a, (bq, part_cols), at_a(n, half)),
                (query_b, (bq, part_cols), at_b(n, half)),
                (grad_a, (bq, part_cols), at_a(n, half)),
                (grad_b, (bq, part_cols), at_b(n, half)),
                (own, (bq, part_cols), at_a(0, half)),
                (for_near, (bq, part_cols), at_b(0, half)),
                whole(kv_whole),
                (kv_turned, (dim, window), lambda i, *_: (0, 0)),
                (start_row, (1, bq), lambda i, *_: (0, i)),
                (lse, (part_heads, bq), lambda i, *_: (0, i)),
            ],
            [
                ((rows, part_cols), BF16, (bq, part_cols), at_a(0, half)),
                ((rows, part_cols), BF16, (bq, part_cols), at_b(0, half)),
                ((window, 2 * dim), F32, (window, 2 * dim), lambda i, *_: (0, 0)),
            ],
            scratch=[pltpu.VMEM((part_heads, dim, bq), F32)],
            prefetch=1,
            vmem=48,
            flops=pairs_guess,
            moved=rows,
        )

    own_all = jnp.concatenate([a[0] for a in attn], 1)
    other_all = jnp.concatenate([a[1] for a in attn], 1)
    out_sum = add(dot_left(own_all, grad_low), near(dot_left(other_all, grad_low)))
    expand_size = width // n_dp
    out_size = out_sum.shape[0] // chips * width // hid // n_dp
    def feed_output(first_input):
        count = 2 * halves
        out_cols = min(512, width)
        blocks = [
            (p[n], (part_rows, size), lambda i, shift, k=k: (0, lax.rem(k + shift[0], pieces)))
            for n in range(2)
            for p in far_parts
            for k in range(pieces)
        ]
        return call(
            functools.partial(contract_kernel, count, pieces),
            (width // out_cols,),
            [(parity.reshape(1), None, None)]
            + [whole(p) for p in [first_input, near_parts[1][0], near_parts[0][1], near_parts[1][1]]]
            + blocks
            + [(v, (v.shape[0], out_cols), lambda i, *_: (0, i)) for v in [contract_weight] + contract_far],
            [((rows, width), BF16, (rows, out_cols), lambda i, *_: (0, i))] * 2,
            flops=rows,
            moved=rows,
            vmem=56,
            prefetch=1,
        )

    back_acts, dq_own, dq_other, dkv = [], [], [], None
    info = scalars[0]
    for n in range(calls):
        if n == 0:
            info, contract_sum, out_sum = tie(info, contract_sum, out_sum)
            out_half = add(*chips_half(out_sum))
            contract_half = contract_sum.shape[0] // 2
            contract_first = lax.psum(contract_sum[:contract_half], "dp")
        own, for_near, dkv_part = attn_backward(n, info)
        if n == 0:
            mlp_start, dkv_part = tie(near_parts[0][0], dkv_part)
            mlp_own, mlp_near = feed_output(mlp_start)
            info, mlp_own, query_all[-1] = tie(info, mlp_own, query_all[-1])
        if n == calls - 1:
            for_near, contract_first = tie(for_near, contract_first)
            contract_rest, contract_first = tie(contract_sum[contract_half:], contract_first)
            contract_second = lax.psum(contract_rest, "dp")
            joined = jnp.concatenate(
                [add(expand_own, expand_moved).reshape(n_dp, expand_size, hid), out_half.reshape(n_dp, out_size, hid)], 1
            )
            joined = joined.reshape(-1, hid)
            for_near, joined = tie(for_near, joined)
            expand_chain = Chain(joined)
            expand_chain.step()
            expand_chain.prepare()
            expand_chain.up, expand_chain.out = tie(expand_chain.up, expand_chain.out)
        other = near(for_near)
        dq_own.append(own)
        dq_other.append(other)
        back_acts.append(jnp.concatenate([own, other], 1))
        if n == 0 and calls > 1:
            info, back_acts[0] = tie(info, back_acts[0])
        dkv = dkv_part if dkv is None else dkv + dkv_part
    back_acts = [a for act in back_acts for a in heads_acts(act)]

    dkv = dkv.reshape(chips, 2, rows, 2 * dim)

    def half_of(value, axis, bit):
        return lax.dynamic_index_in_dim(value, bit, axis, keepdims=False)

    core_sum = half_of(dkv, 1, core) + near(half_of(dkv, 1, 1 - core).astype(BF16)).astype(F32)
    chip_sum = add(half_of(core_sum, 0, chip), far(half_of(core_sum, 0, 1 - chip).astype(BF16)))
    first, second = heads_sum(chip_sum)
    grad_kv = add(first, second)

    kv_keep = lax.dynamic_slice_in_dim(grad_kv, core * dim, dim, 1)
    kv_send = lax.dynamic_slice_in_dim(grad_kv, (1 - core) * dim, dim, 1)
    query_sent = near(dot_left(normed_first, jnp.concatenate(dq_other + [kv_send], 1)))
    query_block = add(dot_left(normed_first, jnp.concatenate(dq_own + [kv_keep], 1)), query_sent)
    query_chain = Chain(add(*chips_half(query_block)))
    expand_chain.step()
    grad_kv, expand_chain.up, expand_chain.down = tie(grad_kv, expand_chain.up, expand_chain.down)
    input_grad, first_sums = call(
        functools.partial(first_back_kernel, len(back_acts), sides),
        (rows // wide,),
        [rows_of(a, wide) for a in back_acts]
        + [whole(w) for w in query_all]
        + [rows_of(grad_kv, wide), whole(key_value_weight)]
        + [rows_of(tokens, wide), rows_of(grad_middle, wide), whole(line(pre_norm_gain))],
        [((rows, width), BF16, (wide, width), down), ((8, width), F32, (8, width), lambda i: (0, 0))],
        flops=2 * rows * width * (width + 2 * dim),
        moved=20 * rows * width,
        vmem=60,
        scratch=[
            pltpu.VMEM((sides, wide, width // sides), BF16),
            pltpu.VMEM((sides, width, width // sides), BF16),
        ]
        + [pltpu.VMEM((wide, width), F32)] * sides,
    )

    mlp_sum, first_sums = tie(add(mlp_own, near(mlp_near)), first_sums)
    mlp_first, mlp_second = heads_sum(mlp_sum)
    mlp_total = mlp_first.astype(F32) + mlp_second.astype(F32)
    layer_output = (jnp.concatenate(middles) + mlp_total + contract_bias).astype(BF16)

    expand_chain.step()
    expand_chain.up, input_grad = tie(expand_chain.up, input_grad)
    dq_bias_keep = jnp.concatenate([jnp.sum(v.astype(F32), 0) for v in dq_own])
    dq_bias_send = jnp.concatenate([jnp.sum(v.astype(F32), 0) for v in dq_other])
    query_bias_part = ordered(core, dq_bias_keep, dq_bias_send, 0)
    value_bias_part = jnp.sum(grad_kv[:, dim:].astype(F32), 0)

    places_of_units = jnp.arange(n_rows)[:, None]
    units = jnp.where(places_of_units == row_index, bias_near, 0.0) + jnp.where(
        places_of_units == jnp.bitwise_xor(row_index, 2), bias_far, 0.0
    )
    shorts = [mid_sums, first_sums[:2], query_bias_part, value_bias_part, units]
    short_sums = jnp.concatenate([v.reshape(-1) for v in shorts])
    for k in range(3):
        if k == 1:
            expand_chain.up, contract_second = tie(expand_chain.up, contract_second)
            contract_weight_grad = jnp.concatenate([contract_first, contract_second]).astype(F32)
        if k == 2:
            expand_chain.up, contract_weight_grad = tie(expand_chain.up, contract_weight_grad)
        expand_chain.up, short_sums = tie(expand_chain.up, short_sums)
        together([expand_chain, query_chain], [])
        short_sums = hop_sum(short_sums)
    joined = expand_chain.result().reshape(n_dp, -1, hid)
    expand_weight_grad = joined[:, :expand_size].reshape(width, hid).astype(F32)
    query_chain.up, expand_weight_grad, layer_output, short_sums = tie(
        query_chain.up, expand_weight_grad, layer_output, short_sums
    )
    query_chain.step()
    short_sums = hop_sum(short_sums)
    while hops:
        short_sums = hop_sum(short_sums)
    query_chain.up, short_sums = tie(query_chain.up, short_sums)
    out_total = joined[:, expand_size:].reshape(out_half.shape)
    out_block = ordered(chip, out_total, far(out_total), 0)
    query_chain.step()
    query_chain.up, out_block = tie(query_chain.up, out_block)
    out_block_near = near(out_block)
    output_weight_grad = ordered(core, out_block, out_block_near, 0).astype(F32)
    query_block, query_block_near = all_blocks(query_chain.result())
    query_weight_grad, key_value_weight_grad = call(
        side_by_side_kernel,
        (width // min(512, width),),
        [
            (core.reshape(1), None, None),
            (query_block, (min(512, width), cols + dim), lambda i, *_: (i, 0)),
            (query_block_near, (min(512, width), cols + dim), lambda i, *_: (i, 0)),
        ],
        [
            ((width, 2 * cols), F32, (min(512, width), 2 * cols), lambda i, *_: (i, 0)),
            ((width, 2 * dim), F32, (min(512, width), 2 * dim), lambda i, *_: (i, 0)),
        ],
        prefetch=1,
        moved=12 * width * (cols + dim),
    )

    short_totals, at = [], 0
    for v in shorts:
        short_totals.append(short_sums[at : at + v.size].reshape(v.shape))
        at += v.size
    mid_total, first_total, query_bias_grad, value_bias_grad, units = short_totals
    expand_bias_grad = lax.dynamic_index_in_dim(units, row_index, 0, keepdims=False)
    return (
        layer_output,
        input_grad,
        first_total[0],
        first_total[1],
        query_weight_grad,
        query_bias_grad,
        key_value_weight_grad,
        value_bias_grad,
        output_weight_grad,
        mid_total[2],
        mid_total[0],
        mid_total[1],
        expand_weight_grad,
        expand_bias_grad,
        contract_weight_grad,
        mid_total[3],
    )


def solution(mesh):
    both = P(("heads", "rows"))
    in_specs = (
        P(("dp", "rows"), None),
        P("dp", None),
        P(),
        P(),
        P(None, "heads"),
        P("heads"),
        P(),
        P(),
        P("heads", None),
        P(),
        P(),
        P(),
        P(None, ("heads", "rows")),
        both,
        P(("heads", "rows"), None),
        P(),
        P(("dp", "rows"), None),
    )
    out_specs = (
        P(("dp", "rows"), None),
        P(("dp", "rows"), None),
        P(),
        P(),
        P(None, "heads"),
        P("heads"),
        P(),
        P(),
        P("heads", None),
        P(),
        P(),
        P(),
        P(None, ("heads", "rows")),
        both,
        P(("heads", "rows"), None),
        P(),
    )
    return jax.shard_map(body, mesh=mesh, in_specs=in_specs, out_specs=out_specs, check_vma=False)
```
